128 devices in a mesh: seq: 16 (over y_lo, z, core), head: 8 (over y_hi, x).
Axes of the slice: x: 4, y: 4 (y_hi: 2, y_lo: 2; y = y_hi * 2 + y_lo), z: 4, core: 2. Of those that a mesh axis runs over, the one named last changes fastest.
Arguments:
- queries: bfloat16 [3072, 128, 192], P('seq', 'head'), may hold values from -256 to 256
- latents: bfloat16 [3072, 576], P('seq'), may hold values from -10 to 10
- positions: int32 [3072], P('seq'), may hold values from 0 to 131072, as said below
- up_keys: bfloat16 [512, 128, 128], P(None, 'head'), may hold values from -0.25 to 0.25
- up_values: bfloat16 [512, 128, 128], P(None, 'head'), may hold values from -0.25 to 0.25
- out_weight: bfloat16 [16384, 7168], P('head', 'seq'), may hold values from -0.1875 to 0.1875
- residual: bfloat16 [3072, 7168], P('seq', 'head'), may hold values from -3 to 3
- router_gate: float32 [3072], P('seq'), may hold values from 0.5 to 2
Outputs:
- layer_out: bfloat16 [3072, 7168], P('seq', 'head')
The draws below stay inside these ranges and needn't reach their ends.
Inputs may be any that keep to these rules, and one draw needn't show every extreme that they name: Device s of seq holds, in its 192 slots, the kept tokens of sequence blocks s and 31 - s (each block 4096 positions long) in increasing order of position, then 131072 in its empty slots. Positions are distinct. Every device holds 2 or more kept tokens; one device's slots are all full.
All inputs are finite; a program needn't handle non-finite values.
Results may differ from the reference program's by a relative error of at most 0.017.
Values may be sent and summed in bfloat16 or wider, within the bound.
No kernel may reach another device: no remote copies, remote signals or barrier semaphores. Data moves between devices by JAX's collectives and lax.ppermute only.
A program may use at most 192 MiB of HBM per device.

```python
import math
import jax
import jax.numpy as jnp
from jax import lax

D = 7168
LAT = 512
ROPE = 64
NOPE = 128
VDIM = 128
HEADS = 128
MEAN_DEV = 64
KEPT_CAP = 192
KEPT_SLOTS = 3072
SEQ_LEN = 131072
N_SEQ = 16
N_HEAD = 8


def kept_positions(key):
    key = jax.random.fold_in(key, 11)
    block_len = SEQ_LEN // (2 * N_SEQ)
    shard_keys = jax.random.split(jax.random.fold_in(key, 4), N_SEQ)
    full_shard = jax.random.randint(jax.random.fold_in(key, 5), (), 0, N_SEQ)
    counts = jax.random.randint(jax.random.fold_in(key, 6), (N_SEQ,), 2, 2 * MEAN_DEV - 1)
    counts = jnp.where(jnp.arange(N_SEQ) == full_shard, KEPT_CAP, counts)

    def one_shard(shard_key, shard_index, count):
        order = jax.random.permutation(shard_key, 2 * block_len)[:KEPT_CAP]
        slot_index = jnp.arange(KEPT_CAP)
        chosen = jnp.sort(jnp.where(slot_index < count, order, 2 * block_len))
        early = shard_index * block_len + chosen
        later = (2 * N_SEQ - 1 - shard_index) * block_len + chosen - block_len
        placed = jnp.where(chosen < block_len, early, later)
        return jnp.where(chosen >= 2 * block_len, SEQ_LEN, placed)
    spots = jax.vmap(one_shard)(shard_keys, jnp.arange(N_SEQ), counts)
    return spots.reshape(-1).astype(jnp.int32)


def draw_positions(key, part):
    return kept_positions(key)


def draw_latents(key, part):
    key = jax.random.fold_in(key, 31)
    base = jnp.clip(jax.random.normal(key, (KEPT_SLOTS, LAT + ROPE), jnp.float32), -4.0, 4.0)
    return base.astype(jnp.bfloat16)


def draw_queries(key, part):
    key = jax.random.fold_in(key, 41)
    base = 2.0 * jnp.clip(jax.random.normal(key, (KEPT_SLOTS, HEADS, NOPE + ROPE), jnp.float32), -4.0, 4.0)
    return base.astype(jnp.bfloat16)


def block_levels(key, extent, cuts, smallest, high):
    factor_of = 1.0
    for dim, shards_of in cuts:
        draws = jax.random.uniform(jax.random.fold_in(jax.random.fold_in(key, 6), dim), (shards_of,), jnp.float32, smallest / len(cuts), high / len(cuts))
        factor_of = factor_of * jnp.repeat(jnp.exp(draws), extent[dim] // shards_of).reshape((-1,) + (1,) * (len(extent) - 1 - dim))
    return factor_of


def gaussian(stream_key, shape, width, reach, cuts=(), dtype=jnp.bfloat16):
    loudness = block_levels(stream_key, shape, cuts, -0.22, 0.18) if cuts else 1.0
    values = jax.random.normal(stream_key, shape, jnp.float32) * width * loudness
    return jnp.minimum(jnp.maximum(values, -reach), reach).astype(dtype)


def setup_inputs(seed: int = 0) -> dict:
    key_list = jax.random.split(jax.random.key(seed), 9)
    queries = draw_queries(jax.random.fold_in(key_list[8], 71), 0)
    latents = draw_latents(jax.random.fold_in(key_list[8], 71), 0)
    positions = draw_positions(jax.random.fold_in(key_list[8], 71), 0)
    up_keys = gaussian(key_list[3], (LAT, HEADS, NOPE), LAT ** -0.5, 0.25, ((1, 8),))
    up_values = gaussian(key_list[4], (LAT, HEADS, VDIM), LAT ** -0.5, 0.25, ((1, 8),))
    out_weight = gaussian(key_list[5], (HEADS * VDIM, D), (HEADS * 8) ** -0.5, 0.1875, ((0, 8), (1, 16)))
    residual = gaussian(key_list[6], (KEPT_SLOTS, D), 0.5, 3.0, ((0, 16), (1, 8)))
    router_gate = jnp.clip(jnp.exp(math.log(2.0) - 1.3862944 * jax.random.uniform(key_list[7], (KEPT_SLOTS,), jnp.float32) ** block_levels(key_list[7], (KEPT_SLOTS,), ((0, 16),), -0.2, 0.2)), 0.5, 2.0)
    return {"queries": queries, "latents": latents, "positions": positions, "up_keys": up_keys, "up_values": up_values, "out_weight": out_weight, "residual": residual, "router_gate": router_gate}


def reference(queries, latents, positions, up_keys, up_values, out_weight, residual, router_gate):
    score_scale = (NOPE + ROPE) ** -0.5
    content = latents[:, :LAT]
    rotary = latents[:, LAT:]
    allowed = positions[None, :] <= positions[:, None]

    def one_head(inputs_head):
        head_query, key_weight, value_weight = inputs_head
        key_nope = jnp.dot(content, key_weight, preferred_element_type=jnp.float32).astype(jnp.bfloat16)
        head_values = jnp.dot(content, value_weight, preferred_element_type=jnp.float32).astype(jnp.bfloat16)
        key_rows = jnp.concatenate([key_nope, rotary], axis=1)
        scores = jnp.dot(head_query, key_rows.T, preferred_element_type=jnp.float32) * score_scale
        masked = jnp.where(allowed, scores, -jnp.inf)
        row_max = jnp.max(masked, axis=1, keepdims=True)
        weights = jnp.where(allowed, jnp.exp(scores - row_max), 0.0)
        row_total = jnp.sum(weights, axis=1, keepdims=True)
        summed = jnp.dot(weights.astype(jnp.bfloat16), head_values, preferred_element_type=jnp.float32)
        return (summed / row_total).astype(jnp.bfloat16)

    per_head = (jnp.moveaxis(queries, 1, 0), jnp.moveaxis(up_keys, 1, 0), jnp.moveaxis(up_values, 1, 0))
    heads_out = lax.map(one_head, per_head)
    attended = jnp.moveaxis(heads_out, 0, 1).reshape(KEPT_SLOTS, HEADS * VDIM)
    group_width = HEADS * VDIM // N_HEAD
    projected = jnp.zeros((KEPT_SLOTS, D), jnp.float32)
    for group_index in range(N_HEAD):
        first_row = group_index * group_width
        partial_sum = jnp.dot(attended[:, first_row:first_row + group_width], out_weight[first_row:first_row + group_width], preferred_element_type=jnp.float32).astype(jnp.bfloat16)
        projected = projected + lax.optimization_barrier(partial_sum).astype(jnp.float32)
    live_rows = (positions < SEQ_LEN).astype(jnp.float32)
    gated = (live_rows * router_gate)[:, None] * projected
    return (residual.astype(jnp.float32) + gated).astype(jnp.bfloat16)
```

```python
import functools
import jax
import jax.numpy as jnp
from jax import lax
from jax.experimental import pallas as pl
from jax.experimental.pallas import tpu as pltpu
from jax.sharding import PartitionSpec as P

SEQ_LEN = 131072
BF = jnp.bfloat16
F32 = jnp.float32
CAP = 192
SHARDS = 16
TOT = CAP * SHARDS
LAT = 512
WIDE = 640
MIB = 1024 * 1024
VARIANTS = (1024, 1280, 1536, TOT)


def prep_kernel(all_ref, own_ref, packed_ref, bias_ref, total_ref):
    packed_ref[...] = jnp.zeros_like(packed_ref)
    lane = lax.broadcasted_iota(jnp.int32, (CAP, 128), 1)
    counts = []
    for s in range(SHARDS):
        tail = all_ref[s * CAP:(s + 1) * CAP, LAT:WIDE].astype(F32)
        counts.append(jnp.sum(jnp.where(lane == 67, tail, 0.0)).astype(jnp.int32))
    diff = (lax.broadcasted_iota(jnp.int32, (CAP + 16, CAP), 0)
            - lax.broadcasted_iota(jnp.int32, (CAP + 16, CAP), 1))
    col = lax.broadcasted_iota(jnp.int32, (CAP + 16, CAP), 1)
    offset = jnp.int32(0)
    for s in range(SHARDS):
        first = pl.multiple_of((offset // 16) * 16, 16)
        shift = offset - first
        pick = jnp.where((diff == shift) & (col < counts[s]), 1.0, 0.0).astype(BF)
        moved = jnp.dot(pick, all_ref[s * CAP:(s + 1) * CAP, :],
                        preferred_element_type=F32).astype(BF)
        packed_ref[pl.ds(first, 16), :] = packed_ref[pl.ds(first, 16), :] + moved[:16]
        packed_ref[pl.ds(pl.multiple_of(first + 16, 16), CAP), :] = moved[16:]
        offset = offset + counts[s]
    total_ref[0] = offset
    lane8 = lax.broadcasted_iota(jnp.int32, (8, 128), 1)
    coef = jnp.where(lane8 == 64, 1.0, jnp.where(lane8 == 65, 64.0, jnp.where(lane8 == 66, 4096.0, 0.0)))
    key_inv = lax.dot_general(coef.astype(BF), packed_ref[0:TOT, LAT:WIDE],
                              (((1,), (1,)), ((), ())), preferred_element_type=F32)
    own = own_ref[:, LAT:WIDE].astype(F32)
    query_inv = jnp.sum(own * coef[0:1, :], axis=1, keepdims=True)
    bias_ref[...] = jnp.where(key_inv[0:1, :] >= query_inv, 0.0, -1e30)


def prep(gathered, own):
    return pl.pallas_call(
        prep_kernel,
        out_shape=(jax.ShapeDtypeStruct((TOT + 16, WIDE), BF),
                   jax.ShapeDtypeStruct((CAP, TOT), F32),
                   jax.ShapeDtypeStruct((1,), jnp.int32)),
        in_specs=[pl.BlockSpec(memory_space=pltpu.VMEM)] * 2,
        out_specs=(pl.BlockSpec(memory_space=pltpu.VMEM), pl.BlockSpec(memory_space=pltpu.VMEM),
                   pl.BlockSpec(memory_space=pltpu.SMEM)),
        compiler_params=pltpu.CompilerParams(vmem_limit_bytes=40 * MIB),
        name="pack_live_rows",
    )(gathered, own)


def attend_kernel(scale, total_ref, packed_ref, bias_ref, q_ref, upk_ref, upv_ref, out_ref, k_ref, v_ref):
    def variant(width):
        for r in range(0, width, 256):
            x = packed_ref[r:r + 256, :LAT]
            k_ref[r:r + 256, :] = jnp.dot(x, upk_ref[...], preferred_element_type=F32).astype(BF)
            v_ref[r:r + 256, :] = jnp.dot(x, upv_ref[...], preferred_element_type=F32).astype(BF)
        for j in range(2):
            keys = jnp.concatenate(
                [k_ref[:width, j * 128:(j + 1) * 128], packed_ref[:width, LAT:WIDE]], axis=1)
            scores = lax.dot_general(q_ref[j], keys, (((1,), (1,)), ((), ())),
                                     preferred_element_type=F32)
            scores = scores * scale + bias_ref[:, :width]
            row_max = jnp.max(scores, axis=1, keepdims=True)
            weights = jnp.exp2(scores - row_max)
            total = jnp.sum(weights, axis=1, keepdims=True)
            summed = jnp.dot(weights.astype(BF), v_ref[:width, j * 128:(j + 1) * 128],
                             preferred_element_type=F32)
            out_ref[:, j * 128:(j + 1) * 128] = (summed / total).astype(BF)

    n = total_ref[0]
    low = 0
    for width in VARIANTS:
        pl.when((n > low) & (n <= width))(functools.partial(variant, width))
        low = width


def attend(total, packed, bias, q, upk, upv, scale):
    pairs = q.shape[0] // 2
    return pl.pallas_call(
        functools.partial(attend_kernel, scale),
        grid=(pairs,),
        out_shape=jax.ShapeDtypeStruct((CAP, pairs * 256), BF),
        in_specs=[
            pl.BlockSpec(memory_space=pltpu.SMEM),
            pl.BlockSpec((TOT + 16, WIDE), lambda i: (0, 0)),
            pl.BlockSpec((CAP, TOT), lambda i: (0, 0)),
            pl.BlockSpec((2, CAP, 256), lambda i: (i, 0, 0)),
            pl.BlockSpec((LAT, 256), lambda i: (0, i)),
            pl.BlockSpec((LAT, 256), lambda i: (0, i)),
        ],
        out_specs=pl.BlockSpec((CAP, 256), lambda i: (0, i)),
        scratch_shapes=[pltpu.VMEM((TOT, 256), BF), pltpu.VMEM((TOT, 256), BF)],
        compiler_params=pltpu.CompilerParams(vmem_limit_bytes=48 * MIB),
        name="attend_heads",
    )(total, packed, bias, q, upk, upv)


def project_kernel(sel_ref, *refs):
    rows = refs[:8]
    w_own, w_a, w_b, out_ref, a_ref, w_ref, sem = refs[8:]
    k, b, c = sel_ref[0], sel_ref[1], sel_ref[2]
    for kk in range(4):
        @pl.when(k == kk)
        def _():
            for half in range(2):
                pltpu.make_async_copy(rows[2 * kk + half], a_ref.at[:, half * 1024:(half + 1) * 1024],
                                      sem.at[half]).start()

    @pl.when(b == 0)
    def _():
        for half in range(2):
            pltpu.make_async_copy(w_own.at[half * 1024:(half + 1) * 1024],
                                  w_ref.at[half * 1024:(half + 1) * 1024], sem.at[2 + half]).start()

    for cc in range(2):
        @pl.when((b == 1) & (c == cc))
        def _():
            for half in range(2):
                pltpu.make_async_copy(w_a if half == cc else w_b,
                                      w_ref.at[half * 1024:(half + 1) * 1024], sem.at[2 + half]).start()
    acc = None
    for half in range(2):
        part = slice(half * 1024, (half + 1) * 1024)
        pltpu.make_async_copy(rows[half], a_ref.at[:, part], sem.at[half]).wait()
        pltpu.make_async_copy(w_own.at[part], w_ref.at[part], sem.at[2 + half]).wait()
        term = jnp.dot(a_ref[:, part], w_ref[part, :], preferred_element_type=F32)
        acc = term if acc is None else acc + term
    out_ref[...] = acc.astype(BF)


def project(sel, rows, w_own, w_a, w_b):
    return pl.pallas_call(
        project_kernel,
        out_shape=jax.ShapeDtypeStruct((CAP, 896), BF),
        in_specs=[pl.BlockSpec(memory_space=pltpu.SMEM)] + [pl.BlockSpec(memory_space=pl.ANY)] * 11,
        out_specs=pl.BlockSpec(memory_space=pltpu.VMEM),
        scratch_shapes=[pltpu.VMEM((CAP, 2048), BF), pltpu.VMEM((2048, 896), BF),
                        pltpu.SemaphoreType.DMA((4,))],
        cost_estimate=pl.CostEstimate(flops=2 * CAP * 2048 * 896, bytes_accessed=5 * 1000 * 1000, transcendentals=0),
        compiler_params=pltpu.CompilerParams(vmem_limit_bytes=16 * MIB),
        name="project_chunk",
    )(sel, *rows, w_own, w_a, w_b)


CORE = [(s, s ^ 1) for s in range(16)]
ALONG_Y = [(s, s ^ 8) for s in range(16)]


def along_z(k):
    return [(s, (s // 8) * 8 + ((s // 2 + k) % 4) * 2 + s % 2) for s in range(16)]


def to_head(dy, dx):
    return [(h, ((h // 4) ^ dy) * 4 + (h + dx) % 4) for h in range(8)]


def turn():
    pairs = []
    for s in range(16):
        y_lo, z, core = s // 8, (s // 2) % 4, s % 2
        for h in range(8):
            y_hi, x = h // 4, h % 4
            pairs.append((s * 8 + h, (y_lo * 8 + x * 2 + core) * 8 + y_hi * 4 + z))
    return pairs


def per_device(queries, latents, positions, up_keys, up_values, out_weight, residual, router_gate):
    heads, qk = queries.shape[1], queries.shape[2]
    s, h = lax.axis_index("seq"), lax.axis_index("head")
    y_lo, z, core = s // 8, (s // 2) % 4, s % 2
    y_hi, x = h // 4, h % 4
    inv = SEQ_LEN - positions
    extra = jnp.stack([inv & 63, (inv >> 6) & 63, inv >> 12, (inv > 0).astype(jnp.int32)], axis=1)
    own = jnp.concatenate([latents, extra.astype(BF), jnp.zeros((CAP, 60), BF)], axis=1)
    gathered = lax.all_gather(own, "seq", axis=0, tiled=True)

    swapped = lax.ppermute(out_weight, "seq", CORE)
    w_own = jnp.where(core == 0, jnp.concatenate([out_weight, swapped], axis=1),
                      jnp.concatenate([swapped, out_weight], axis=1))
    w_a = lax.ppermute(lax.dynamic_slice(w_own, (core * 1024, 0), (1024, 896)), "seq", ALONG_Y)
    w_b = lax.ppermute(w_a, "seq", CORE)

    q = jnp.pad(jnp.transpose(queries, (1, 0, 2)), ((0, 0), (0, 0), (0, 256 - qk)))
    upk = up_keys.reshape(LAT, heads * 128)
    upv = up_values.reshape(LAT, heads * 128)
    q, upk, upv = lax.optimization_barrier((q, upk, upv))

    packed, bias, total = prep(gathered, own)
    scale = (qk ** -0.5) * 1.4426950408889634
    rows = [None] * 8
    for i in range(2):
        part = slice(i * 1024, (i + 1) * 1024)
        mine = attend(total, packed, bias, q[i * 8:(i + 1) * 8], upk[:, part], upv[:, part], scale)
        from1 = lax.ppermute(mine, "seq", along_z(1))
        from3 = lax.ppermute(mine, "seq", along_z(3))
        from2 = lax.ppermute(from1, "seq", along_z(1)) if i == 0 else lax.ppermute(from3, "seq", along_z(3))
        for k, a in enumerate((mine, from1, from2, from3)):
            rows[2 * k + i] = a

    received = []
    for dy, dx in ((1, 2), (1, 1), (1, 3), (0, 2), (0, 1), (0, 3), (1, 0), (0, 0)):
        k = (z - x - dx) % 4
        b = y_lo ^ y_hi ^ dy
        chunk = project(jnp.stack([k, b, core]).astype(jnp.int32), rows, w_own, w_a, w_b)
        received.append(lax.ppermute(chunk, "head", to_head(dy, dx)) if dy or dx else chunk)
    projected = sum(r.astype(F32) for r in received).astype(BF)
    projected = lax.ppermute(projected, ("seq", "head"), turn()).astype(F32)
    live_rows = (positions < SEQ_LEN).astype(F32)
    gated = (live_rows * router_gate)[:, None] * projected
    return (residual.astype(F32) + gated).astype(BF)


def solution(mesh):
    return jax.shard_map(
        per_device,
        mesh=mesh,
        in_specs=(
            P("seq", "head", None),
            P("seq", None),
            P("seq"),
            P(None, "head", None),
            P(None, "head", None),
            P("head", "seq"),
            P("seq", "head"),
            P("seq"),
        ),
        out_specs=P("seq", "head"),
        check_vma=False,
    )
```

```python
import functools
import jax
import jax.numpy as jnp
from jax import lax
from jax.experimental import pallas as pl
from jax.experimental.pallas import tpu as pltpu
from jax.sharding import PartitionSpec as P

SEQ_LEN = 131072
BF = jnp.bfloat16
F32 = jnp.float32
CAP = 192
SHARDS = 16
TOT = CAP * SHARDS
LAT = 512
WIDE = 640
MIB = 1024 * 1024
VARIANTS = (1024, 1280, 1536, TOT)
PARTS = (6, 4, 4, 2)


def payload_kernel(lat_ref, pos_ref, out_ref):
    row = lax.broadcasted_iota(jnp.int32, (CAP, CAP), 0)
    col = lax.broadcasted_iota(jnp.int32, (CAP, CAP), 1)
    inv = jnp.sum(jnp.where(row == col, (SEQ_LEN - pos_ref[...]).astype(F32), 0.0), axis=1, keepdims=True)
    inv = inv.astype(jnp.int32)
    lane = lax.broadcasted_iota(jnp.int32, (CAP, 64), 1)
    digits = jnp.where(lane == 0, inv & 63, jnp.where(lane == 1, (inv >> 6) & 63, jnp.where(
        lane == 2, inv >> 12, jnp.where((lane == 3) & (inv > 0), 1, 0))))
    out_ref[...] = jnp.concatenate([lat_ref[...], digits.astype(F32).astype(BF)], axis=1)


def payload(latents, positions):
    return pl.pallas_call(
        payload_kernel,
        out_shape=jax.ShapeDtypeStruct((CAP, WIDE), BF),
        in_specs=[pl.BlockSpec(memory_space=pltpu.VMEM)] * 2,
        out_specs=pl.BlockSpec(memory_space=pltpu.VMEM),
        name="latents_and_positions",
    )(latents, positions.reshape(1, CAP))


def prep_kernel(all_ref, own_ref, packed_ref, bias_ref, total_ref):
    packed_ref[...] = jnp.zeros_like(packed_ref)
    lane = lax.broadcasted_iota(jnp.int32, (CAP, 128), 1)
    counts = []
    for s in range(SHARDS):
        tail = all_ref[s * CAP:(s + 1) * CAP, LAT:WIDE].astype(F32)
        counts.append(jnp.sum(jnp.where(lane == 67, tail, 0.0)).astype(jnp.int32))
    diff = (lax.broadcasted_iota(jnp.int32, (CAP + 16, CAP), 0)
            - lax.broadcasted_iota(jnp.int32, (CAP + 16, CAP), 1))
    col = lax.broadcasted_iota(jnp.int32, (CAP + 16, CAP), 1)
    offset = jnp.int32(0)
    for s in range(SHARDS):
        first = pl.multiple_of((offset // 16) * 16, 16)
        shift = offset - first
        pick = jnp.where((diff == shift) & (col < counts[s]), 1.0, 0.0).astype(BF)
        moved = jnp.dot(pick, all_ref[s * CAP:(s + 1) * CAP, :],
                        preferred_element_type=F32).astype(BF)
        packed_ref[pl.ds(first, 16), :] = packed_ref[pl.ds(first, 16), :] + moved[:16]
        packed_ref[pl.ds(pl.multiple_of(first + 16, 16), CAP), :] = moved[16:]
        offset = offset + counts[s]
    total_ref[0] = offset
    lane8 = lax.broadcasted_iota(jnp.int32, (8, 128), 1)
    coef = jnp.where(lane8 == 64, 1.0, jnp.where(lane8 == 65, 64.0, jnp.where(lane8 == 66, 4096.0, 0.0)))
    key_inv = lax.dot_general(coef.astype(BF), packed_ref[0:TOT, LAT:WIDE],
                              (((1,), (1,)), ((), ())), preferred_element_type=F32)
    own = own_ref[:, LAT:WIDE].astype(F32)
    query_inv = jnp.sum(own * coef[0:1, :], axis=1, keepdims=True)
    bias_ref[...] = jnp.where(key_inv[0:1, :] >= query_inv, 0.0, -1e30)


def prep(gathered, own):
    return pl.pallas_call(
        prep_kernel,
        out_shape=(jax.ShapeDtypeStruct((TOT + 16, WIDE), BF),
                   jax.ShapeDtypeStruct((CAP, TOT), F32),
                   jax.ShapeDtypeStruct((1,), jnp.int32)),
        in_specs=[pl.BlockSpec(memory_space=pltpu.VMEM)] * 2,
        out_specs=(pl.BlockSpec(memory_space=pltpu.VMEM), pl.BlockSpec(memory_space=pltpu.VMEM),
                   pl.BlockSpec(memory_space=pltpu.SMEM)),
        compiler_params=pltpu.CompilerParams(vmem_limit_bytes=40 * MIB),
        name="pack_live_rows",
    )(gathered, own)


def attend_kernel(scale, total_ref, packed_ref, bias_ref, q_ref, upk_ref, upv_ref, *rest):
    out_ref, next_ref, k_ref, v_ref = rest[-4:]

    def variant(width):
        for r in range(0, width, 256):
            x = packed_ref[r:r + 256, :LAT]
            k_ref[r:r + 256, :] = jnp.dot(x, upk_ref[...], preferred_element_type=F32).astype(BF)
            v_ref[r:r + 256, :] = jnp.dot(x, upv_ref[...], preferred_element_type=F32).astype(BF)
        for j in range(2):
            keys = jnp.concatenate(
                [k_ref[:width, j * 128:(j + 1) * 128], packed_ref[:width, LAT:WIDE]], axis=1)
            scores = lax.dot_general(q_ref[j], keys, (((1,), (1,)), ((), ())),
                                     preferred_element_type=F32)
            scores = scores * scale + bias_ref[:, :width]
            row_max = jnp.max(scores, axis=1, keepdims=True)
            weights = jnp.exp2(scores - row_max)
            total = jnp.sum(weights, axis=1, keepdims=True)
            summed = jnp.dot(weights.astype(BF), v_ref[:width, j * 128:(j + 1) * 128],
                             preferred_element_type=F32)
            out_ref[:, j * 128:(j + 1) * 128] = (summed / total).astype(BF)

    n = total_ref[0]
    next_ref[0] = n
    low = 0
    for width in VARIANTS:
        pl.when((n > low) & (n <= width))(functools.partial(variant, width))
        low = width


def attend(total, packed, bias, q, upk, upv, scale, first, heads, after):
    pairs, start = heads // 2, first // 2
    return pl.pallas_call(
        functools.partial(attend_kernel, scale),
        grid=(pairs,),
        out_shape=(jax.ShapeDtypeStruct((CAP, pairs * 256), BF), jax.ShapeDtypeStruct((1,), jnp.int32)),
        in_specs=[
            pl.BlockSpec(memory_space=pltpu.SMEM),
            pl.BlockSpec(memory_space=pltpu.VMEM),
            pl.BlockSpec(memory_space=pltpu.VMEM),
            pl.BlockSpec((2, CAP, 256), lambda i: (start + i, 0, 0)),
            pl.BlockSpec((LAT, 256), lambda i: (0, start + i)),
            pl.BlockSpec((LAT, 256), lambda i: (0, start + i)),
        ] + [pl.BlockSpec(memory_space=pltpu.HBM)] * len(after),
        out_specs=(pl.BlockSpec((CAP, 256), lambda i: (0, i)), pl.BlockSpec(memory_space=pltpu.SMEM)),
        scratch_shapes=[pltpu.VMEM((TOT, 256), BF), pltpu.VMEM((TOT, 256), BF)],
        cost_estimate=pl.CostEstimate(flops=pairs * 3 * 10 ** 9, bytes_accessed=pairs * 10 ** 6, transcendentals=0),
        compiler_params=pltpu.CompilerParams(vmem_limit_bytes=32 * MIB),
        name="attend_heads",
    )(total, packed, bias, q, upk, upv, *after)


def project_kernel(sel_ref, *refs):
    rows, (own, core_own, far0, far1, core_far0, core_far1) = refs[:16], refs[16:22]
    outs = refs[22:26]
    a_ref, w_ref, sem_a, sem_w = refs[26:]
    b, core, turned = sel_ref[0], sel_ref[1], sel_ref[2]
    for cc in range(2):
        @pl.when((b == 0) & (core == cc))
        def _():
            for j, src in enumerate((own, core_own)):
                pltpu.make_async_copy(src, w_ref.at[pl.ds((j ^ cc) * 448, 448)], sem_w.at[j]).start()

        @pl.when((b == 1) & (core == cc))
        def _():
            for j, pair in enumerate(((far0, far1), (core_far0, core_far1))):
                for i, src in enumerate(pair):
                    pltpu.make_async_copy(src, w_ref.at[pl.ds((j ^ cc) * 448 + i * 224, 224)], sem_w.at[j]).start()
    waits = []
    for k in range(4):
        slot = (turned + 4 - k) % 4
        first = 0
        for i, width in enumerate(PARTS):
            copy = pltpu.make_async_copy(rows[4 * k + i], a_ref.at[slot, :, pl.ds(first * 128, width * 128)],
                                         sem_a.at[4 * k + i])
            copy.start()
            waits.append(copy)
            first += width
    for copy in waits:
        copy.wait()
    for j in range(2):
        pltpu.make_async_copy(own, w_ref.at[pl.ds(0, 448)], sem_w.at[j]).wait()
    whole = lax.dot_general(a_ref[...].reshape(4 * CAP, 2048), w_ref[...], (((1,), (1,)), ((), ())),
                            preferred_element_type=F32).astype(BF)
    for dx in range(4):
        outs[dx][...] = whole[dx * CAP:(dx + 1) * CAP]


def project(sel, rows, shards):
    return pl.pallas_call(
        project_kernel,
        out_shape=(jax.ShapeDtypeStruct((CAP, 896), BF),) * 4,
        in_specs=[pl.BlockSpec(memory_space=pltpu.SMEM)] + [pl.BlockSpec(memory_space=pltpu.HBM)] * 22,
        out_specs=(pl.BlockSpec(memory_space=pltpu.VMEM),) * 4,
        scratch_shapes=[pltpu.VMEM((4, CAP, 2048), BF), pltpu.VMEM((896, 2048), BF),
                        pltpu.SemaphoreType.DMA((16,)), pltpu.SemaphoreType.DMA((2,))],
        cost_estimate=pl.CostEstimate(flops=8 * CAP * 2048 * 896, bytes_accessed=8 * 10 ** 6, transcendentals=0),
        compiler_params=pltpu.CompilerParams(vmem_limit_bytes=24 * MIB),
        name="project_chunks",
    )(sel, *rows, *shards)


CORE = [(s, s ^ 1) for s in range(16)]
ALONG_Y = [(s, s ^ 8) for s in range(16)]


def along_z(k):
    return [(s, (s // 8) * 8 + ((s // 2 + k) % 4) * 2 + s % 2) for s in range(16)]


def to_head(dy, dx):
    return [(h, ((h // 4) ^ dy) * 4 + (h + dx) % 4) for h in range(8)]


def turn():
    pairs = []
    for s in range(16):
        y_lo, z, core = s // 8, (s // 2) % 4, s % 2
        for h in range(8):
            y_hi, x = h // 4, h % 4
            pairs.append((s * 8 + h, (y_lo * 8 + x * 2 + core) * 8 + y_hi * 4 + z))
    return pairs


def per_device(queries, latents, positions, up_keys, up_values, out_weight, residual, router_gate):
    heads, qk = queries.shape[1], queries.shape[2]
    s, h = lax.axis_index("seq"), lax.axis_index("head")
    y_lo, z, core = s // 8, (s // 2) % 4, s % 2
    y_hi, x = h // 4, h % 4
    own = payload(latents, positions)
    gathered = lax.all_gather(own, "seq", axis=0, tiled=True)
    weight = out_weight.T
    w_core = lax.ppermute(weight, "seq", CORE)
    half = weight.shape[0] // 2
    w_far0 = lax.ppermute(weight[:half], "seq", ALONG_Y)

    q = jnp.pad(jnp.transpose(queries, (1, 0, 2)), ((0, 0), (0, 0), (0, 256 - qk)))
    upk = up_keys.reshape(LAT, heads * 128)
    upv = up_values.reshape(LAT, heads * 128)

    packed, bias, total = prep(gathered, own)
    second = jnp.where(total[0] > 0, half, 0)
    w_far1 = lax.ppermute(lax.dynamic_slice(weight, (second, 0), (half, weight.shape[1])), "seq", ALONG_Y)
    scale = (qk ** -0.5) * 1.4426950408889634
    rows, first, arrived = [None] * 16, 0, [()] * len(PARTS)
    for i, width in enumerate(PARTS):
        after = ()
        if i >= 2:
            after = arrived[i - 2] + ((rows[4 * 2 + i - 3],) if i >= 3 else ())
        mine, total = attend(total, packed, bias, q, upk, upv, scale, first, width, after)
        first += width
        from1 = lax.ppermute(mine, "seq", along_z(1))
        from3 = lax.ppermute(mine, "seq", along_z(3))
        from2 = lax.ppermute(from1, "seq", along_z(1)) if i % 2 else lax.ppermute(from3, "seq", along_z(3))
        arrived[i] = (from1, from3)
        for k, a in enumerate((mine, from1, from2, from3)):
            rows[4 * k + i] = a
    late = jnp.where(total[0] > 0, w_far1, jnp.zeros_like(w_far1))
    shards = (weight, w_core, w_far0, w_far1, lax.ppermute(w_far0, "seq", CORE), lax.ppermute(late, "seq", CORE))

    received = []
    for dy in (1, 0):
        sel = jnp.stack([y_lo ^ y_hi ^ dy, core, (z - x) % 4]).astype(jnp.int32)
        chunks = project(sel, rows, shards)
        for dx in (2, 1, 3, 0):
            received.append(lax.ppermute(chunks[dx], "head", to_head(dy, dx)) if dy or dx else chunks[dx])
    projected = sum(r.astype(F32) for r in received).astype(BF)
    projected = lax.ppermute(projected, ("seq", "head"), turn()).astype(F32)
    live_rows = (positions < SEQ_LEN).astype(F32)
    gated = (live_rows * router_gate)[:, None] * projected
    return (residual.astype(F32) + gated).astype(BF)


def solution(mesh):
    return jax.shard_map(
        per_device,
        mesh=mesh,
        in_specs=(
            P("seq", "head", None),
            P("seq", None),
            P("seq"),
            P(None, "head", None),
            P(None, "head", None),
            P("head", "seq"),
            P("seq", "head"),
            P("seq"),
        ),
        out_specs=P("seq", "head"),
        check_vma=False,
    )
```

```python
import functools
import jax
import jax.numpy as jnp
from jax import lax
from jax.experimental import pallas as pl
from jax.experimental.pallas import tpu as pltpu
from jax.sharding import PartitionSpec as P

SEQ_LEN = 131072
BF = jnp.bfloat16
F32 = jnp.float32
CAP = 192
SHARDS = 16
TOT = CAP * SHARDS
LAT = 512
WIDE = 640
MIB = 1024 * 1024
VARIANTS = (1024, 1280, 1536, TOT)
SPLIT = ((0, 96), (96, 96))
PARTS = (4, 4, 4, 4)


def payload_kernel(lat_ref, pos_ref, out_ref):
    row = lax.broadcasted_iota(jnp.int32, (CAP, CAP), 0)
    col = lax.broadcasted_iota(jnp.int32, (CAP, CAP), 1)
    inv = jnp.sum(jnp.where(row == col, (SEQ_LEN - pos_ref[...]).astype(F32), 0.0), axis=1, keepdims=True)
    inv = inv.astype(jnp.int32)
    lane = lax.broadcasted_iota(jnp.int32, (CAP, 64), 1)
    digits = jnp.where(lane == 0, inv & 63, jnp.where(lane == 1, (inv >> 6) & 63, jnp.where(
        lane == 2, inv >> 12, jnp.where((lane == 3) & (inv > 0), 1, 0))))
    out_ref[...] = jnp.concatenate([lat_ref[...], digits.astype(F32).astype(BF)], axis=1)


def payload(latents, positions):
    return pl.pallas_call(
        payload_kernel,
        out_shape=jax.ShapeDtypeStruct((CAP, WIDE), BF),
        in_specs=[pl.BlockSpec(memory_space=pltpu.VMEM)] * 2,
        out_specs=pl.BlockSpec(memory_space=pltpu.VMEM),
        name="latents_and_positions",
    )(latents, positions.reshape(1, CAP))


def prep_kernel(all_ref, own_ref, packed_ref, bias_ref, total_ref):
    packed_ref[...] = jnp.zeros_like(packed_ref)
    lane = lax.broadcasted_iota(jnp.int32, (CAP, 128), 1)
    counts = []
    for s in range(SHARDS):
        tail = all_ref[s * CAP:(s + 1) * CAP, LAT:WIDE].astype(F32)
        counts.append(jnp.sum(jnp.where(lane == 67, tail, 0.0)).astype(jnp.int32))
    diff = (lax.broadcasted_iota(jnp.int32, (CAP + 16, CAP), 0)
            - lax.broadcasted_iota(jnp.int32, (CAP + 16, CAP), 1))
    col = lax.broadcasted_iota(jnp.int32, (CAP + 16, CAP), 1)
    offset = jnp.int32(0)
    for s in range(SHARDS):
        first = pl.multiple_of((offset // 16) * 16, 16)
        shift = offset - first
        pick = jnp.where((diff == shift) & (col < counts[s]), 1.0, 0.0).astype(BF)
        moved = jnp.dot(pick, all_ref[s * CAP:(s + 1) * CAP, :],
                        preferred_element_type=F32).astype(BF)
        packed_ref[pl.ds(first, 16), :] = packed_ref[pl.ds(first, 16), :] + moved[:16]
        packed_ref[pl.ds(pl.multiple_of(first + 16, 16), CAP), :] = moved[16:]
        offset = offset + counts[s]
    total_ref[0] = offset
    lane8 = lax.broadcasted_iota(jnp.int32, (8, 128), 1)
    coef = jnp.where(lane8 == 64, 1.0, jnp.where(lane8 == 65, 64.0, jnp.where(lane8 == 66, 4096.0, 0.0)))
    key_inv = lax.dot_general(coef.astype(BF), packed_ref[0:TOT, LAT:WIDE],
                              (((1,), (1,)), ((), ())), preferred_element_type=F32)
    own = own_ref[:, LAT:WIDE].astype(F32)
    query_inv = jnp.sum(own * coef[0:1, :], axis=1, keepdims=True)
    bias_ref[...] = jnp.where(key_inv[0:1, :] >= query_inv, 0.0, -1e30)


def prep(gathered, own):
    return pl.pallas_call(
        prep_kernel,
        out_shape=(jax.ShapeDtypeStruct((TOT + 16, WIDE), BF),
                   jax.ShapeDtypeStruct((CAP, TOT), F32),
                   jax.ShapeDtypeStruct((1,), jnp.int32)),
        in_specs=[pl.BlockSpec(memory_space=pltpu.VMEM)] * 2,
        out_specs=(pl.BlockSpec(memory_space=pltpu.VMEM), pl.BlockSpec(memory_space=pltpu.VMEM),
                   pl.BlockSpec(memory_space=pltpu.SMEM)),
        compiler_params=pltpu.CompilerParams(vmem_limit_bytes=40 * MIB),
        name="pack_live_rows",
    )(gathered, own)


def attend_kernel(scale, total_ref, packed_ref, bias_ref, q_ref, upk_ref, upv_ref, *rest):
    out_ref, next_ref, k_ref, v_ref = rest[-4:]

    def variant(width):
        for r in range(0, width, 256):
            x = packed_ref[r:r + 256, :LAT]
            k_ref[r:r + 256, :] = jnp.dot(x, upk_ref[...], preferred_element_type=F32).astype(BF)
            v_ref[r:r + 256, :] = jnp.dot(x, upv_ref[...], preferred_element_type=F32).astype(BF)
        for j in range(2):
            keys = jnp.concatenate(
                [k_ref[:width, j * 128:(j + 1) * 128], packed_ref[:width, LAT:WIDE]], axis=1)
            scores = lax.dot_general(q_ref[j], keys, (((1,), (1,)), ((), ())),
                                     preferred_element_type=F32)
            scores = scores * scale + bias_ref[:, :width]
            row_max = jnp.max(scores, axis=1, keepdims=True)
            weights = jnp.exp2(scores - row_max)
            total = jnp.sum(weights, axis=1, keepdims=True)
            summed = jnp.dot(weights.astype(BF), v_ref[:width, j * 128:(j + 1) * 128],
                             preferred_element_type=F32)
            out_ref[:, j * 128:(j + 1) * 128] = (summed / total).astype(BF)

    n = total_ref[0]
    next_ref[0] = n
    low = 0
    for width in VARIANTS:
        pl.when((n > low) & (n <= width))(functools.partial(variant, width))
        low = width


def attend(total, packed, bias, q, upk, upv, scale, first, heads, after):
    pairs, start = heads // 2, first // 2
    return pl.pallas_call(
        functools.partial(attend_kernel, scale),
        grid=(pairs,),
        out_shape=(jax.ShapeDtypeStruct((CAP, pairs * 256), BF), jax.ShapeDtypeStruct((1,), jnp.int32)),
        in_specs=[
            pl.BlockSpec(memory_space=pltpu.SMEM),
            pl.BlockSpec(memory_space=pltpu.VMEM),
            pl.BlockSpec(memory_space=pltpu.VMEM),
            pl.BlockSpec((2, CAP, 256), lambda i: (start + i, 0, 0)),
            pl.BlockSpec((LAT, 256), lambda i: (0, start + i)),
            pl.BlockSpec((LAT, 256), lambda i: (0, start + i)),
        ] + [pl.BlockSpec(memory_space=pltpu.HBM)] * len(after),
        out_specs=(pl.BlockSpec((CAP, 256), lambda i: (0, i)), pl.BlockSpec(memory_space=pltpu.SMEM)),
        scratch_shapes=[pltpu.VMEM((TOT, 256), BF), pltpu.VMEM((TOT, 256), BF)],
        cost_estimate=pl.CostEstimate(flops=pairs * 3 * 10 ** 9, bytes_accessed=pairs * 10 ** 6, transcendentals=0),
        compiler_params=pltpu.CompilerParams(vmem_limit_bytes=32 * MIB),
        name="attend_heads",
    )(total, packed, bias, q, upk, upv, *after)


def project_kernel(first_row, count, sel_ref, *refs):
    n_rows = 4 * len(PARTS)
    rows, (own, core_own, far, core_far) = refs[:n_rows], refs[n_rows:n_rows + 4]
    outs = refs[n_rows + 4:n_rows + 12]
    a_ref, w_ref, sem_a, sem_w = refs[n_rows + 12:]
    same, core, turned = sel_ref[0], sel_ref[1], sel_ref[2]
    waits = []
    for k in range(4):
        slot = (turned + 4 - k) % 4
        first = 0
        for i, width in enumerate(PARTS):
            copy = pltpu.make_async_copy(rows[len(PARTS) * k + i].at[pl.ds(first_row, count)],
                                         a_ref.at[slot, :, pl.ds(first * 128, width * 128)],
                                         sem_a.at[len(PARTS) * k + i])
            copy.start()
            waits.append(copy)
            first += width
    for dy in (1, 0):
        for bb in range(2):
            for cc in range(2):
                @pl.when(((same ^ dy) == bb) & (core == cc))
                def _():
                    for j, src in enumerate((far, core_far) if bb else (own, core_own)):
                        pltpu.make_async_copy(src, w_ref.at[dy, pl.ds((j ^ cc) * 448, 448)], sem_w.at[dy, j]).start()
    for copy in waits:
        copy.wait()
    for dy in (1, 0):
        for j in range(2):
            pltpu.make_async_copy(own, w_ref.at[dy, pl.ds(j * 448, 448)], sem_w.at[dy, j]).wait()
        whole = lax.dot_general(a_ref[...].reshape(4 * count, 2048), w_ref[dy], (((1,), (1,)), ((), ())),
                                preferred_element_type=F32).astype(BF)
        for dx in range(4):
            outs[4 * dy + dx][...] = whole[dx * count:(dx + 1) * count]


def project(sel, rows, shards, first_row, count):
    return pl.pallas_call(
        functools.partial(project_kernel, first_row, count),
        out_shape=(jax.ShapeDtypeStruct((count, 896), BF),) * 8,
        in_specs=[pl.BlockSpec(memory_space=pltpu.SMEM)]
        + [pl.BlockSpec(memory_space=pltpu.HBM)] * (len(rows) + len(shards)),
        out_specs=(pl.BlockSpec(memory_space=pltpu.VMEM),) * 8,
        scratch_shapes=[pltpu.VMEM((4, count, 2048), BF), pltpu.VMEM((2, 896, 2048), BF),
                        pltpu.SemaphoreType.DMA((len(rows),)), pltpu.SemaphoreType.DMA((2, 2))],
        cost_estimate=pl.CostEstimate(flops=16 * count * 2048 * 896, bytes_accessed=10 ** 7, transcendentals=0),
        compiler_params=pltpu.CompilerParams(vmem_limit_bytes=58 * MIB),
        name="project_chunks",
    )(sel, *rows, *shards)


CORE = [(s, s ^ 1) for s in range(16)]
ALONG_Y = [(s, s ^ 8) for s in range(16)]


def along_z(k):
    return [(s, (s // 8) * 8 + ((s // 2 + k) % 4) * 2 + s % 2) for s in range(16)]


def to_head(dy, dx):
    return [(h, ((h // 4) ^ dy) * 4 + (h + dx) % 4) for h in range(8)]


def turn():
    pairs = []
    for s in range(16):
        y_lo, z, core = s // 8, (s // 2) % 4, s % 2
        for h in range(8):
            y_hi, x = h // 4, h % 4
            pairs.append((s * 8 + h, (y_lo * 8 + x * 2 + core) * 8 + y_hi * 4 + z))
    return pairs


def per_device(queries, latents, positions, up_keys, up_values, out_weight, residual, router_gate):
    heads, qk = queries.shape[1], queries.shape[2]
    s, h = lax.axis_index("seq"), lax.axis_index("head")
    y_lo, z, core = s // 8, (s // 2) % 4, s % 2
    y_hi, x = h // 4, h % 4
    own = payload(latents, positions)
    gathered = lax.all_gather(own, "seq", axis=0, tiled=True)
    weight = out_weight.T
    w_core = lax.ppermute(weight, "seq", CORE)

    q = jnp.pad(jnp.transpose(queries, (1, 0, 2)), ((0, 0), (0, 0), (0, 256 - qk)))
    upk = up_keys.reshape(LAT, heads * 128)
    upv = up_values.reshape(LAT, heads * 128)

    packed, bias, total = prep(gathered, own)
    start = jnp.where(total[0] > 0, 0, 448)
    w_far = lax.ppermute(lax.dynamic_slice(jnp.pad(weight, ((0, 448), (0, 0))), (start, 0), weight.shape), "seq", ALONG_Y)
    scale = (qk ** -0.5) * 1.4426950408889634
    n_parts = len(PARTS)
    rows, first, arrived = [None] * (4 * n_parts), 0, [()] * n_parts
    for i, width in enumerate(PARTS):
        after = (w_core,) if i == 0 else arrived[i - 2] if i >= 2 else ()
        mine, total = attend(total, packed, bias, q, upk, upv, scale, first, width, after)
        first += width
        from1 = lax.ppermute(mine, "seq", along_z(1))
        from3 = lax.ppermute(mine, "seq", along_z(3))
        from2 = lax.ppermute(from1, "seq", along_z(1)) if i % 2 else lax.ppermute(from3, "seq", along_z(3))
        arrived[i] = (from1, from3)
        for k, a in enumerate((mine, from1, from2, from3)):
            rows[n_parts * k + i] = a
    late = jnp.where(total[0] > 0, w_far, jnp.zeros_like(w_far))
    shards = (weight, w_core, w_far, lax.ppermute(late, "seq", CORE))

    sel = jnp.stack([y_lo ^ y_hi, core, (z - x) % 4]).astype(jnp.int32)
    pieces = []
    for first_row, count in SPLIT:
        chunks = project(sel, rows, shards, first_row, count)
        received = [chunks[0]]
        for dy, dx in ((1, 2), (1, 1), (1, 3), (1, 0), (0, 2), (0, 1), (0, 3)):
            received.append(lax.ppermute(chunks[4 * dy + dx], "head", to_head(dy, dx)))
        summed = sum(r.astype(F32) for r in received).astype(BF)
        pieces.append(lax.ppermute(summed, ("seq", "head"), turn()))
    projected = jnp.concatenate(pieces, axis=0).astype(F32)
    live_rows = (positions < SEQ_LEN).astype(F32)
    gated = (live_rows * router_gate)[:, None] * projected
    return (residual.astype(F32) + gated).astype(BF)


def solution(mesh):
    return jax.shard_map(
        per_device,
        mesh=mesh,
        in_specs=(
            P("seq", "head", None),
            P("seq", None),
            P("seq"),
            P(None, "head", None),
            P(None, "head", None),
            P("head", "seq"),
            P("seq", "head"),
            P("seq"),
        ),
        out_specs=P("seq", "head"),
        check_vma=False,
    )
```

```python
import functools
import jax
import jax.numpy as jnp
from jax import lax
from jax.experimental import pallas as pl
from jax.experimental.pallas import tpu as pltpu
from jax.sharding import PartitionSpec as P

SEQ_LEN = 131072
BF = jnp.bfloat16
F32 = jnp.float32
CAP = 192
SHARDS = 16
TOT = CAP * SHARDS
LAT = 512
WIDE = 640
MIB = 1024 * 1024
BASE = 128
SLAB = 16
PARTNERS = (1, 2, 8, 3)
VARIANTS = (1024, 1280, 1536, TOT)
PARTS = (4, 4, 4, 4)


def payload_kernel(lat_ref, pos_ref, out_ref):
    row = lax.broadcasted_iota(jnp.int32, (CAP, CAP), 0)
    col = lax.broadcasted_iota(jnp.int32, (CAP, CAP), 1)
    inv = jnp.sum(jnp.where(row == col, (SEQ_LEN - pos_ref[...]).astype(F32), 0.0), axis=1, keepdims=True)
    inv = inv.astype(jnp.int32)
    lane = lax.broadcasted_iota(jnp.int32, (CAP, 64), 1)
    digits = jnp.where(lane == 0, inv & 63, jnp.where(lane == 1, (inv >> 6) & 63, jnp.where(
        lane == 2, inv >> 12, jnp.where((lane == 3) & (inv > 0), 1, 0))))
    out_ref[...] = jnp.concatenate([lat_ref[...], digits.astype(F32).astype(BF)], axis=1)


def payload(latents, positions):
    return pl.pallas_call(
        payload_kernel,
        out_shape=jax.ShapeDtypeStruct((CAP, WIDE), BF),
        in_specs=[pl.BlockSpec(memory_space=pltpu.VMEM)] * 2,
        out_specs=pl.BlockSpec(memory_space=pltpu.VMEM),
        name="latents_and_positions",
    )(latents, positions.reshape(1, CAP))


def prep_kernel(me_ref, all_ref, packed_ref, bias_ref, meta_ref, counts_ref):
    me = me_ref[0]
    packed_ref[...] = jnp.zeros_like(packed_ref)
    lane = lax.broadcasted_iota(jnp.int32, (CAP, 128), 1)
    counts = []
    large = jnp.int32(0)
    for s in range(SHARDS):
        tail = all_ref[s * CAP:(s + 1) * CAP, LAT:WIDE].astype(F32)
        counts.append(jnp.sum(jnp.where(lane == 67, tail, 0.0)).astype(jnp.int32))
        counts_ref[s] = counts[s]
        large = large + jnp.where(counts[s] > BASE, 1, 0)
    diff = (lax.broadcasted_iota(jnp.int32, (CAP + 16, CAP), 0)
            - lax.broadcasted_iota(jnp.int32, (CAP + 16, CAP), 1))
    col = lax.broadcasted_iota(jnp.int32, (CAP + 16, CAP), 1)
    offset = jnp.int32(0)
    for s in range(SHARDS):
        first = pl.multiple_of((offset // 16) * 16, 16)
        shift = offset - first
        pick = jnp.where((diff == shift) & (col < counts[s]), 1.0, 0.0).astype(BF)
        moved = jnp.dot(pick, all_ref[s * CAP:(s + 1) * CAP, :],
                        preferred_element_type=F32).astype(BF)
        packed_ref[pl.ds(first, 16), :] = packed_ref[pl.ds(first, 16), :] + moved[:16]
        packed_ref[pl.ds(pl.multiple_of(first + 16, 16), CAP), :] = moved[16:]
        offset = offset + counts[s]
    few = large <= 1
    chosen, source = jnp.int32(0), me ^ PARTNERS[0]
    for j in range(1, 4):
        partner = me ^ PARTNERS[j]
        take = counts_ref[partner] > BASE
        chosen = jnp.where(take, j, chosen)
        source = jnp.where(take, partner, source)
    meta_ref[0] = offset
    meta_ref[1] = jnp.where(few, 1, 0)
    meta_ref[2] = chosen
    lane8 = lax.broadcasted_iota(jnp.int32, (8, 128), 1)
    coef = jnp.where(lane8 == 64, 1.0, jnp.where(lane8 == 65, 64.0, jnp.where(lane8 == 66, 4096.0, 0.0)))
    key_inv = lax.dot_general(coef.astype(BF), packed_ref[0:TOT, LAT:WIDE],
                              (((1,), (1,)), ((), ())), preferred_element_type=F32)
    mine = pl.multiple_of(me * CAP, 16)
    other = pl.multiple_of(jnp.where(few, source * CAP + BASE + chosen * SLAB, me * CAP + BASE), 16)
    for row, count, start in ((0, BASE, mine), (BASE, SLAB, other),
                              (BASE + SLAB, CAP - BASE - SLAB, pl.multiple_of(mine + (BASE + SLAB), 16))):
        digits = all_ref[pl.ds(start, count), LAT:WIDE].astype(F32)
        query_inv = jnp.sum(digits * coef[0:1, :], axis=1, keepdims=True)
        bias_ref[row:row + count, :] = jnp.where(key_inv[0:1, :] >= query_inv, 0.0, -1e30)


def prep(me, gathered):
    return pl.pallas_call(
        prep_kernel,
        out_shape=(jax.ShapeDtypeStruct((TOT + 16, WIDE), BF),
                   jax.ShapeDtypeStruct((CAP, TOT), F32),
                   jax.ShapeDtypeStruct((3,), jnp.int32)),
        in_specs=[pl.BlockSpec(memory_space=pltpu.SMEM), pl.BlockSpec(memory_space=pltpu.VMEM)],
        out_specs=(pl.BlockSpec(memory_space=pltpu.VMEM), pl.BlockSpec(memory_space=pltpu.VMEM),
                   pl.BlockSpec(memory_space=pltpu.SMEM)),
        scratch_shapes=[pltpu.SMEM((SHARDS,), jnp.int32)],
        compiler_params=pltpu.CompilerParams(vmem_limit_bytes=40 * MIB),
        name="pack_live_rows",
    )(me.reshape(1), gathered)


def attend_kernel(scale, n_rows, meta_ref, packed_ref, bias_ref, q_ref, upk_ref, upv_ref, *rest):
    out_ref, next_ref, k_ref, v_ref = rest[-4:]

    def variant(width):
        for r in range(0, width, 256):
            x = packed_ref[r:r + 256, :LAT]
            k_ref[r:r + 256, :] = jnp.dot(x, upk_ref[...], preferred_element_type=F32).astype(BF)
            v_ref[r:r + 256, :] = jnp.dot(x, upv_ref[...], preferred_element_type=F32).astype(BF)
        for j in range(2):
            keys = jnp.concatenate(
                [k_ref[:width, j * 128:(j + 1) * 128], packed_ref[:width, LAT:WIDE]], axis=1)
            query = q_ref[j] if n_rows == CAP else jnp.concatenate(
                [q_ref[j, :BASE], q_ref[j, pl.ds(pl.multiple_of(BASE + meta_ref[2] * SLAB, SLAB), SLAB)]], axis=0)
            scores = lax.dot_general(query, keys, (((1,), (1,)), ((), ())),
                                     preferred_element_type=F32)
            scores = scores * scale + bias_ref[:n_rows, :width]
            row_max = jnp.max(scores, axis=1, keepdims=True)
            weights = jnp.exp2(scores - row_max)
            total = jnp.sum(weights, axis=1, keepdims=True)
            summed = jnp.dot(weights.astype(BF), v_ref[:width, j * 128:(j + 1) * 128],
                             preferred_element_type=F32)
            out_ref[:, j * 128:(j + 1) * 128] = (summed / total).astype(BF)

    n = meta_ref[0]
    for i in range(3):
        next_ref[i] = meta_ref[i]
    low = 0
    for width in VARIANTS:
        pl.when((n > low) & (n <= width))(functools.partial(variant, width))
        low = width


def attend(meta, packed, bias, q, upk, upv, scale, n_rows, first, heads, after):
    pairs, start = heads // 2, first // 2
    return pl.pallas_call(
        functools.partial(attend_kernel, scale, n_rows),
        grid=(pairs,),
        out_shape=(jax.ShapeDtypeStruct((n_rows, pairs * 256), BF), jax.ShapeDtypeStruct((3,), jnp.int32)),
        in_specs=[
            pl.BlockSpec(memory_space=pltpu.SMEM),
            pl.BlockSpec(memory_space=pltpu.VMEM),
            pl.BlockSpec(memory_space=pltpu.VMEM),
            pl.BlockSpec((2, CAP, 256), lambda i: (start + i, 0, 0)),
            pl.BlockSpec((LAT, 256), lambda i: (0, start + i)),
            pl.BlockSpec((LAT, 256), lambda i: (0, start + i)),
        ] + [pl.BlockSpec(memory_space=pltpu.HBM)] * len(after),
        out_specs=(pl.BlockSpec((n_rows, 256), lambda i: (0, i)), pl.BlockSpec(memory_space=pltpu.SMEM)),
        scratch_shapes=[pltpu.VMEM((TOT, 256), BF), pltpu.VMEM((TOT, 256), BF)],
        cost_estimate=pl.CostEstimate(flops=pairs * 3 * 10 ** 9, bytes_accessed=pairs * 10 ** 6, transcendentals=0),
        compiler_params=pltpu.CompilerParams(vmem_limit_bytes=32 * MIB),
        name="attend_heads",
    )(meta, packed, bias, q, upk, upv, *after)


def project_kernel(count, sel_ref, *refs):
    n_parts = len(PARTS)
    rows, (w_own, w_a, w_b) = refs[:4 * n_parts], refs[4 * n_parts:4 * n_parts + 3]
    outs = refs[4 * n_parts + 3:4 * n_parts + 7]
    a_ref, w_ref, sem_a, sem_w = refs[4 * n_parts + 7:]
    b, core, turned = sel_ref[0], sel_ref[1], sel_ref[2]

    def w_part(half):
        return w_ref.at[pl.ds(half * 1024, 1024)]

    waits = []
    for k in range(4):
        slot = (turned + 4 - k) % 4
        first = 0
        for i, width in enumerate(PARTS):
            copy = pltpu.make_async_copy(rows[n_parts * k + i], a_ref.at[slot, :, pl.ds(first * 128, width * 128)],
                                         sem_a.at[n_parts * k + i])
            copy.start()
            waits.append(copy)
            first += width

    @pl.when(b == 0)
    def _():
        for half in range(2):
            pltpu.make_async_copy(w_own.at[pl.ds(half * 1024, 1024)], w_part(half), sem_w.at[half]).start()

    for cc in range(2):
        @pl.when((b == 1) & (core == cc))
        def _():
            for half in range(2):
                pltpu.make_async_copy(w_a if half == cc else w_b, w_part(half), sem_w.at[half]).start()
    for copy in waits:
        copy.wait()
    lhs = a_ref[...].reshape(4 * count, 2048)
    for half in range(2):
        pltpu.make_async_copy(w_a, w_part(half), sem_w.at[half]).wait()
    whole = jnp.dot(lhs, w_ref[...], preferred_element_type=F32).astype(BF)
    for dx in range(4):
        outs[dx][...] = whole[dx * count:(dx + 1) * count]


def project(sel, rows, weights):
    count = rows[0].shape[0]
    return pl.pallas_call(
        functools.partial(project_kernel, count),
        out_shape=(jax.ShapeDtypeStruct((count, 896), BF),) * 4,
        in_specs=[pl.BlockSpec(memory_space=pltpu.SMEM)]
        + [pl.BlockSpec(memory_space=pltpu.HBM)] * (len(rows) + len(weights)),
        out_specs=(pl.BlockSpec(memory_space=pltpu.VMEM),) * 4,
        scratch_shapes=[pltpu.VMEM((4, count, 2048), BF), pltpu.VMEM((2048, 896), BF),
                        pltpu.SemaphoreType.DMA((len(rows),)), pltpu.SemaphoreType.DMA((2,))],
        cost_estimate=pl.CostEstimate(flops=8 * count * 2048 * 896, bytes_accessed=8 * 10 ** 6, transcendentals=0),
        compiler_params=pltpu.CompilerParams(vmem_limit_bytes=58 * MIB),
        name="project_chunks",
    )(sel, *rows, *weights)


def behind(x, other):
    return pl.pallas_call(
        lambda *refs: None,
        out_shape=jax.ShapeDtypeStruct(x.shape, x.dtype),
        in_specs=[pl.BlockSpec(memory_space=pltpu.HBM)] * 2,
        out_specs=pl.BlockSpec(memory_space=pltpu.HBM),
        input_output_aliases={0: 0},
        name="behind",
    )(x, other)


CORE = [(s, s ^ 1) for s in range(16)]
ALONG_Y = [(s, s ^ 8) for s in range(16)]


def along_z(k):
    return [(s, (s // 8) * 8 + ((s // 2 + k) % 4) * 2 + s % 2) for s in range(16)]


def to_head(dy, dx):
    return [(h, ((h // 4) ^ dy) * 4 + (h + dx) % 4) for h in range(8)]


def partner(j):
    return [(s, s ^ PARTNERS[j]) for s in range(16)]


def turn(flip=0):
    pairs = []
    for s in range(16):
        y_lo, z, core = s // 8, (s // 2) % 4, s % 2
        for h in range(8):
            y_hi, x = h // 4, h % 4
            pairs.append((s * 8 + h, ((y_lo * 8 + x * 2 + core) ^ flip) * 8 + y_hi * 4 + z))
    return pairs


def heads_first(queries):
    return jnp.pad(jnp.transpose(queries, (1, 0, 2)), ((0, 0), (0, 0), (0, 256 - queries.shape[2])))


def finish(n_rows, scale, sel, meta, packed, bias, q, upk, upv, w_own):
    w_a = lax.ppermute(lax.dynamic_slice(w_own, (sel[1] * 1024, 0), (1024, 896)), "seq", ALONG_Y)
    n_parts = len(PARTS)
    rows, first, arrived = [None] * (4 * n_parts), 0, [()] * n_parts
    for i, width in enumerate(PARTS):
        after = arrived[i - 2] if i >= 2 else ()
        mine, meta = attend(meta, packed, bias, q, upk, upv, scale, n_rows, first, width, after)
        first += width
        from1 = lax.ppermute(mine, "seq", along_z(1))
        from3 = lax.ppermute(mine, "seq", along_z(3))
        from2 = lax.ppermute(from1, "seq", along_z(1)) if i % 2 else lax.ppermute(from3, "seq", along_z(3))
        arrived[i] = (from1, from3)
        for k, a in enumerate((mine, from1, from2, from3)):
            rows[n_parts * k + i] = a
    w_a = behind(w_a, rows[n_parts * 2 - 1])
    w_b = lax.ppermute(w_a, "seq", CORE)

    received = []
    for dy in (1, 0):
        chunks = project(jnp.stack([sel[0] ^ dy, sel[1], sel[2]]), rows, (w_own, w_a, w_b))
        for dx in (2, 1, 3, 0):
            received.append(lax.ppermute(chunks[dx], "head", to_head(dy, dx)) if dy or dx else chunks[dx])
    summed = sum(r.astype(F32) for r in received).astype(BF)
    if n_rows == CAP:
        return lax.ppermute(summed, ("seq", "head"), turn())
    pieces = [lax.ppermute(summed[:BASE], ("seq", "head"), turn())]
    for flip in PARTNERS:
        pieces.append(lax.ppermute(summed[BASE:], ("seq", "head"), turn(flip)))
    return jnp.concatenate(pieces, axis=0)


def per_device(queries, latents, positions, up_keys, up_values, out_weight, residual, router_gate):
    heads, qk = queries.shape[1], queries.shape[2]
    s, h = lax.axis_index("seq"), lax.axis_index("head")
    y_lo, z, core = s // 8, (s // 2) % 4, s % 2
    y_hi, x = h // 4, h % 4
    own = payload(latents, positions)
    gathered = lax.all_gather(own, "seq", axis=0, tiled=True)
    w_core = lax.ppermute(out_weight, "seq", CORE)
    slabs = [lax.ppermute(queries[BASE + j * SLAB:BASE + (j + 1) * SLAB], "seq", partner(j)) for j in range(4)]
    w_own = jnp.where(core == 0, jnp.concatenate([out_weight, w_core], axis=1),
                      jnp.concatenate([w_core, out_weight], axis=1))
    q = heads_first(jnp.concatenate([queries[:BASE]] + slabs, axis=0))
    upk = up_keys.reshape(LAT, heads * 128)
    upv = up_values.reshape(LAT, heads * 128)

    packed, bias, meta = prep(s, gathered)
    scale = (qk ** -0.5) * 1.4426950408889634
    sel = jnp.stack([y_lo ^ y_hi, core, (z - x) % 4]).astype(jnp.int32)
    projected = lax.cond(
        meta[1] == 1,
        lambda q, queries, *rest: finish(BASE + SLAB, scale, sel, meta, packed, bias, q, *rest),
        lambda q, queries, *rest: finish(CAP, scale, sel, meta, packed, bias, heads_first(queries), *rest),
        q, queries, upk, upv, w_own).astype(F32)
    live_rows = (positions < SEQ_LEN).astype(F32)
    gated = (live_rows * router_gate)[:, None] * projected
    return (residual.astype(F32) + gated).astype(BF)


def solution(mesh):
    return jax.shard_map(
        per_device,
        mesh=mesh,
        in_specs=(
            P("seq", "head", None),
            P("seq", None),
            P("seq"),
            P(None, "head", None),
            P(None, "head", None),
            P("head", "seq"),
            P("seq", "head"),
            P("seq"),
        ),
        out_specs=P("seq", "head"),
        check_vma=False,
    )
```

```python
import functools
import jax
import jax.numpy as jnp
from jax import lax
from jax.experimental import pallas as pl
from jax.experimental.pallas import tpu as pltpu
from jax.sharding import PartitionSpec as P

SEQ_LEN = 131072
BF = jnp.bfloat16
F32 = jnp.float32
CAP = 192
SHARDS = 16
TOT = CAP * SHARDS
LAT = 512
WIDE = 640
MIB = 1024 * 1024
VARIANTS = (1024, 1280, 1536, TOT)
PARTS = (4, 4, 4, 4)


def payload_kernel(lat_ref, pos_ref, out_ref):
    row = lax.broadcasted_iota(jnp.int32, (CAP, CAP), 0)
    col = lax.broadcasted_iota(jnp.int32, (CAP, CAP), 1)
    inv = jnp.sum(jnp.where(row == col, (SEQ_LEN - pos_ref[...]).astype(F32), 0.0), axis=1, keepdims=True)
    inv = inv.astype(jnp.int32)
    lane = lax.broadcasted_iota(jnp.int32, (CAP, 64), 1)
    digits = jnp.where(lane == 0, inv & 63, jnp.where(lane == 1, (inv >> 6) & 63, jnp.where(
        lane == 2, inv >> 12, jnp.where((lane == 3) & (inv > 0), 1, 0))))
    out_ref[...] = jnp.concatenate([lat_ref[...], digits.astype(F32).astype(BF)], axis=1)


def payload(latents, positions):
    return pl.pallas_call(
        payload_kernel,
        out_shape=jax.ShapeDtypeStruct((CAP, WIDE), BF),
        in_specs=[pl.BlockSpec(memory_space=pltpu.VMEM)] * 2,
        out_specs=pl.BlockSpec(memory_space=pltpu.VMEM),
        name="latents_and_positions",
    )(latents, positions.reshape(1, CAP))


def prep_kernel(all_ref, own_ref, packed_ref, bias_ref, total_ref):
    packed_ref[...] = jnp.zeros_like(packed_ref)
    lane = lax.broadcasted_iota(jnp.int32, (CAP, 128), 1)
    counts = []
    for s in range(SHARDS):
        tail = all_ref[s * CAP:(s + 1) * CAP, LAT:WIDE].astype(F32)
        counts.append(jnp.sum(jnp.where(lane == 67, tail, 0.0)).astype(jnp.int32))
    diff = (lax.broadcasted_iota(jnp.int32, (CAP + 16, CAP), 0)
            - lax.broadcasted_iota(jnp.int32, (CAP + 16, CAP), 1))
    col = lax.broadcasted_iota(jnp.int32, (CAP + 16, CAP), 1)
    offset = jnp.int32(0)
    for s in range(SHARDS):
        first = pl.multiple_of((offset // 16) * 16, 16)
        shift = offset - first
        pick = jnp.where((diff == shift) & (col < counts[s]), 1.0, 0.0).astype(BF)
        moved = jnp.dot(pick, all_ref[s * CAP:(s + 1) * CAP, :],
                        preferred_element_type=F32).astype(BF)
        packed_ref[pl.ds(first, 16), :] = packed_ref[pl.ds(first, 16), :] + moved[:16]
        packed_ref[pl.ds(pl.multiple_of(first + 16, 16), CAP), :] = moved[16:]
        offset = offset + counts[s]
    total_ref[0] = offset
    lane8 = lax.broadcasted_iota(jnp.int32, (8, 128), 1)
    coef = jnp.where(lane8 == 64, 1.0, jnp.where(lane8 == 65, 64.0, jnp.where(lane8 == 66, 4096.0, 0.0)))
    key_inv = lax.dot_general(coef.astype(BF), packed_ref[0:TOT, LAT:WIDE],
                              (((1,), (1,)), ((), ())), preferred_element_type=F32)
    own = own_ref[:, LAT:WIDE].astype(F32)
    query_inv = jnp.sum(own * coef[0:1, :], axis=1, keepdims=True)
    bias_ref[...] = jnp.where(key_inv[0:1, :] >= query_inv, 0.0, -1e30)


def prep(gathered, own):
    return pl.pallas_call(
        prep_kernel,
        out_shape=(jax.ShapeDtypeStruct((TOT + 16, WIDE), BF),
                   jax.ShapeDtypeStruct((CAP, TOT), F32),
                   jax.ShapeDtypeStruct((1,), jnp.int32)),
        in_specs=[pl.BlockSpec(memory_space=pltpu.VMEM)] * 2,
        out_specs=(pl.BlockSpec(memory_space=pltpu.VMEM), pl.BlockSpec(memory_space=pltpu.VMEM),
                   pl.BlockSpec(memory_space=pltpu.SMEM)),
        compiler_params=pltpu.CompilerParams(vmem_limit_bytes=40 * MIB),
        name="pack_live_rows",
    )(gathered, own)


def attend_kernel(scale, total_ref, packed_ref, bias_ref, q_ref, upk_ref, upv_ref, *rest):
    out_ref, next_ref, k_ref, v_ref = rest[-4:]

    def variant(width):
        for r in range(0, width, 256):
            x = packed_ref[r:r + 256, :LAT]
            k_ref[r:r + 256, :] = jnp.dot(x, upk_ref[...], preferred_element_type=F32).astype(BF)
            v_ref[r:r + 256, :] = jnp.dot(x, upv_ref[...], preferred_element_type=F32).astype(BF)
        for j in range(2):
            keys = jnp.concatenate(
                [k_ref[:width, j * 128:(j + 1) * 128], packed_ref[:width, LAT:WIDE]], axis=1)
            scores = lax.dot_general(q_ref[j], keys, (((1,), (1,)), ((), ())),
                                     preferred_element_type=F32)
            scores = scores * scale + bias_ref[:, :width]
            row_max = jnp.max(scores, axis=1, keepdims=True)
            weights = jnp.exp2(scores - row_max)
            total = jnp.sum(weights, axis=1, keepdims=True)
            summed = jnp.dot(weights.astype(BF), v_ref[:width, j * 128:(j + 1) * 128],
                             preferred_element_type=F32)
            out_ref[:, j * 128:(j + 1) * 128] = (summed / total).astype(BF)

    n = total_ref[0]
    next_ref[0] = n
    low = 0
    for width in VARIANTS:
        pl.when((n > low) & (n <= width))(functools.partial(variant, width))
        low = width


def attend(total, packed, bias, q, upk, upv, scale, first, heads, after):
    pairs, start = heads // 2, first // 2
    return pl.pallas_call(
        functools.partial(attend_kernel, scale),
        grid=(pairs,),
        out_shape=(jax.ShapeDtypeStruct((CAP, pairs * 256), BF), jax.ShapeDtypeStruct((1,), jnp.int32)),
        in_specs=[
            pl.BlockSpec(memory_space=pltpu.SMEM),
            pl.BlockSpec(memory_space=pltpu.VMEM),
            pl.BlockSpec(memory_space=pltpu.VMEM),
            pl.BlockSpec((2, CAP, 256), lambda i: (start + i, 0, 0)),
            pl.BlockSpec((LAT, 256), lambda i: (0, start + i)),
            pl.BlockSpec((LAT, 256), lambda i: (0, start + i)),
        ] + [pl.BlockSpec(memory_space=pltpu.HBM)] * len(after),
        out_specs=(pl.BlockSpec((CAP, 256), lambda i: (0, i)), pl.BlockSpec(memory_space=pltpu.SMEM)),
        scratch_shapes=[pltpu.VMEM((TOT, 256), BF), pltpu.VMEM((TOT, 256), BF)],
        cost_estimate=pl.CostEstimate(flops=pairs * 3 * 10 ** 9, bytes_accessed=pairs * 10 ** 6, transcendentals=0),
        compiler_params=pltpu.CompilerParams(vmem_limit_bytes=32 * MIB),
        name="attend_heads",
    )(total, packed, bias, q, upk, upv, *after)


def project_kernel(sel_ref, *refs):
    n = len(PARTS)
    rows, weights = refs[:2 * n], refs[2 * n:2 * n + 5]
    swapped = refs[2 * n + 5:2 * n + 10]
    outs = refs[2 * n + 10:2 * n + 12]
    a_ref, w_ref, sem_a, sem_w = refs[2 * n + 12:]
    ahead, core, slot = sel_ref[0], sel_ref[1], sel_ref[2]
    halves = [pl.ds(i * 1024, 1024) for i in range(2)]
    waits = []
    for p in range(2):
        first = 0
        for i, width in enumerate(PARTS):
            copy = pltpu.make_async_copy(rows[n * p + i], a_ref.at[slot ^ p, :, pl.ds(first * 128, width * 128)],
                                         sem_a.at[n * p + i])
            copy.start()
            waits.append((first // 8, copy))
            first += width
    for k, pieces in enumerate((((0, 0),), ((1, 0),), ((2, 0), (3, 224)), ((4, 0),))):
        for cc in range(2):
            @pl.when((ahead == k) & (core == cc))
            def _():
                for i in range(2):
                    for j, source in enumerate((weights, swapped)):
                        for index, start in pieces:
                            src = source[index]
                            pltpu.make_async_copy(
                                src.at[:, halves[i]],
                                w_ref.at[pl.ds((j ^ cc) * 448 + start, src.shape[0]), halves[i]], sem_w.at[i]).start()
    whole = None
    for i in range(2):
        for part, copy in waits:
            if part == i:
                copy.wait()
        pltpu.make_async_copy(w_ref.at[:, halves[1 - i]], w_ref.at[:, halves[i]], sem_w.at[i]).wait()
        term = lax.dot_general(a_ref[:, :, i * 1024:(i + 1) * 1024].reshape(2 * CAP, 1024),
                               w_ref[:, i * 1024:(i + 1) * 1024], (((1,), (1,)), ((), ())),
                               preferred_element_type=F32)
        whole = term if whole is None else whole + term
    for r in range(2):
        outs[r][...] = whole[r * CAP:(r + 1) * CAP].astype(BF)


def project(sel, rows, weights, swapped):
    operands = (*rows, *weights, *swapped)
    return pl.pallas_call(
        project_kernel,
        out_shape=(jax.ShapeDtypeStruct((CAP, 896), BF),) * 2,
        in_specs=[pl.BlockSpec(memory_space=pltpu.SMEM)] + [pl.BlockSpec(memory_space=pltpu.HBM)] * len(operands),
        out_specs=(pl.BlockSpec(memory_space=pltpu.VMEM),) * 2,
        scratch_shapes=[pltpu.VMEM((2, CAP, 2048), BF), pltpu.VMEM((896, 2048), BF),
                        pltpu.SemaphoreType.DMA((len(rows),)), pltpu.SemaphoreType.DMA((2,))],
        cost_estimate=pl.CostEstimate(flops=4 * CAP * 2048 * 896, bytes_accessed=8 * 10 ** 6, transcendentals=0),
        compiler_params=pltpu.CompilerParams(vmem_limit_bytes=58 * MIB),
        name="project_chunks",
    )(sel, *operands)


CORE = [(s, s ^ 1) for s in range(16)]
ALONG_Y = [(s, s ^ 8) for s in range(16)]


def along_z(k):
    return [(s, (s // 8) * 8 + ((s // 2 + k) % 4) * 2 + s % 2) for s in range(16)]


def to_owner(r, dx):
    pairs = []
    for s in range(16):
        for h in range(8):
            y_lo, y_hi, x = s // 8, h // 4, h % 4
            pairs.append((s * 8 + h, ((y_hi ^ r) * 8 + s % 8) * 8 + y_lo * 4 + (x + dx) % 4))
    return pairs


def per_device(queries, latents, positions, up_keys, up_values, out_weight, residual, router_gate):
    heads, qk = queries.shape[1], queries.shape[2]
    s, h = lax.axis_index("seq"), lax.axis_index("head")
    y_lo, z, core = s // 8, (s // 2) % 4, s % 2
    y_hi, x = h // 4, h % 4
    own = payload(latents, positions)
    gathered = lax.all_gather(own, "seq", axis=0, tiled=True)
    weight = out_weight.T
    behind1 = lax.ppermute(weight, "seq", along_z(1))
    ahead1 = lax.ppermute(weight, "seq", along_z(3))
    far0 = lax.ppermute(behind1[:224], "seq", along_z(1))
    far1 = lax.ppermute(ahead1[224:], "seq", along_z(3))
    weights = (weight, ahead1, far0, far1, behind1)
    swapped = tuple(lax.ppermute(w, "seq", CORE) for w in weights)

    q = jnp.pad(jnp.transpose(queries, (1, 0, 2)), ((0, 0), (0, 0), (0, 256 - qk)))
    upk = up_keys.reshape(LAT, heads * 128)
    upv = up_values.reshape(LAT, heads * 128)

    packed, bias, total = prep(gathered, own)
    scale = (qk ** -0.5) * 1.4426950408889634
    mine, theirs, first = [], [], 0
    for i, width in enumerate(PARTS):
        after = {0: (ahead1, behind1, swapped[0]), 1: (swapped[1], swapped[4]), 3: (far0, far1)}.get(i, ()) + ((theirs[i - 2],) if i >= 2 else ())
        part, total = attend(total, packed, bias, q, upk, upv, scale, first, width, after)
        first += width
        mine.append(part)
        theirs.append(lax.ppermute(part, "seq", ALONG_Y))

    received = []
    for dx in (2, 1, 3, 0):
        sel = jnp.stack([(x + dx - z) % 4, core, y_hi ^ y_lo]).astype(jnp.int32)
        chunks = project(sel, mine + theirs, weights, swapped)
        for r in (1, 0):
            received.append(lax.ppermute(chunks[r], ("seq", "head"), to_owner(r, dx)))
    projected = sum(r.astype(F32) for r in received)
    live_rows = (positions < SEQ_LEN).astype(F32)
    gated = (live_rows * router_gate)[:, None] * projected
    return (residual.astype(F32) + gated).astype(BF)


def solution(mesh):
    return jax.shard_map(
        per_device,
        mesh=mesh,
        in_specs=(
            P("seq", "head", None),
            P("seq", None),
            P("seq"),
            P(None, "head", None),
            P(None, "head", None),
            P("head", "seq"),
            P("seq", "head"),
            P("seq"),
        ),
        out_specs=P("seq", "head"),
        check_vma=False,
    )
```

```python
import functools
import jax
import jax.numpy as jnp
from jax import lax
from jax.experimental import pallas as pl
from jax.experimental.pallas import tpu as pltpu
from jax.sharding import PartitionSpec as P

SEQ_LEN = 131072
BF = jnp.bfloat16
F32 = jnp.float32
CAP = 192
SHARDS = 16
TOT = CAP * SHARDS
LAT = 512
WIDE = 640
MIB = 1024 * 1024
VARIANTS = (1024, 1280, 1536, TOT)
PARTS = (4, 4, 4, 4)


def payload_kernel(lat_ref, pos_ref, out_ref):
    row = lax.broadcasted_iota(jnp.int32, (CAP, CAP), 0)
    col = lax.broadcasted_iota(jnp.int32, (CAP, CAP), 1)
    inv = jnp.sum(jnp.where(row == col, (SEQ_LEN - pos_ref[...]).astype(F32), 0.0), axis=1, keepdims=True)
    inv = inv.astype(jnp.int32)
    lane = lax.broadcasted_iota(jnp.int32, (CAP, 64), 1)
    digits = jnp.where(lane == 0, inv & 63, jnp.where(lane == 1, (inv >> 6) & 63, jnp.where(
        lane == 2, inv >> 12, jnp.where((lane == 3) & (inv > 0), 1, 0))))
    out_ref[...] = jnp.concatenate([lat_ref[...], digits.astype(F32).astype(BF)], axis=1)


def payload(latents, positions):
    return pl.pallas_call(
        payload_kernel,
        out_shape=jax.ShapeDtypeStruct((CAP, WIDE), BF),
        in_specs=[pl.BlockSpec(memory_space=pltpu.VMEM)] * 2,
        out_specs=pl.BlockSpec(memory_space=pltpu.VMEM),
        name="latents_and_positions",
    )(latents, positions.reshape(1, CAP))


def prep_kernel(all_ref, own_ref, packed_ref, bias_ref, total_ref):
    packed_ref[...] = jnp.zeros_like(packed_ref)
    lane = lax.broadcasted_iota(jnp.int32, (CAP, 128), 1)
    counts = []
    for s in range(SHARDS):
        tail = all_ref[s * CAP:(s + 1) * CAP, LAT:WIDE].astype(F32)
        counts.append(jnp.sum(jnp.where(lane == 67, tail, 0.0)).astype(jnp.int32))
    diff = (lax.broadcasted_iota(jnp.int32, (CAP + 16, CAP), 0)
            - lax.broadcasted_iota(jnp.int32, (CAP + 16, CAP), 1))
    col = lax.broadcasted_iota(jnp.int32, (CAP + 16, CAP), 1)
    offset = jnp.int32(0)
    for s in range(SHARDS):
        first = pl.multiple_of((offset // 16) * 16, 16)
        shift = offset - first
        pick = jnp.where((diff == shift) & (col < counts[s]), 1.0, 0.0).astype(BF)
        moved = jnp.dot(pick, all_ref[s * CAP:(s + 1) * CAP, :],
                        preferred_element_type=F32).astype(BF)
        packed_ref[pl.ds(first, 16), :] = packed_ref[pl.ds(first, 16), :] + moved[:16]
        packed_ref[pl.ds(pl.multiple_of(first + 16, 16), CAP), :] = moved[16:]
        offset = offset + counts[s]
    total_ref[0] = offset
    lane8 = lax.broadcasted_iota(jnp.int32, (8, 128), 1)
    coef = jnp.where(lane8 == 64, 1.0, jnp.where(lane8 == 65, 64.0, jnp.where(lane8 == 66, 4096.0, 0.0)))
    key_inv = lax.dot_general(coef.astype(BF), packed_ref[0:TOT, LAT:WIDE],
                              (((1,), (1,)), ((), ())), preferred_element_type=F32)
    own = own_ref[:, LAT:WIDE].astype(F32)
    query_inv = jnp.sum(own * coef[0:1, :], axis=1, keepdims=True)
    bias_ref[...] = jnp.where(key_inv[0:1, :] >= query_inv, 0.0, -1e30)


def prep(gathered, own):
    return pl.pallas_call(
        prep_kernel,
        out_shape=(jax.ShapeDtypeStruct((TOT + 16, WIDE), BF),
                   jax.ShapeDtypeStruct((CAP, TOT), F32),
                   jax.ShapeDtypeStruct((1,), jnp.int32)),
        in_specs=[pl.BlockSpec(memory_space=pltpu.VMEM)] * 2,
        out_specs=(pl.BlockSpec(memory_space=pltpu.VMEM), pl.BlockSpec(memory_space=pltpu.VMEM),
                   pl.BlockSpec(memory_space=pltpu.SMEM)),
        compiler_params=pltpu.CompilerParams(vmem_limit_bytes=40 * MIB),
        name="pack_live_rows",
    )(gathered, own)


def attend_kernel(scale, total_ref, packed_ref, bias_ref, q_ref, upk_ref, upv_ref, *rest):
    out_ref, next_ref, k_ref, v_ref = rest[-4:]

    def variant(width):
        for r in range(0, width, 256):
            x = packed_ref[r:r + 256, :LAT]
            k_ref[r:r + 256, :] = jnp.dot(x, upk_ref[...], preferred_element_type=F32).astype(BF)
            v_ref[r:r + 256, :] = jnp.dot(x, upv_ref[...], preferred_element_type=F32).astype(BF)
        for j in range(2):
            keys = jnp.concatenate(
                [k_ref[:width, j * 128:(j + 1) * 128], packed_ref[:width, LAT:WIDE]], axis=1)
            scores = lax.dot_general(q_ref[j], keys, (((1,), (1,)), ((), ())),
                                     preferred_element_type=F32)
            scores = scores * scale + bias_ref[:, :width]
            row_max = jnp.max(scores, axis=1, keepdims=True)
            weights = jnp.exp2(scores - row_max)
            total = jnp.sum(weights, axis=1, keepdims=True)
            summed = jnp.dot(weights.astype(BF), v_ref[:width, j * 128:(j + 1) * 128],
                             preferred_element_type=F32)
            out_ref[:, j * 128:(j + 1) * 128] = (summed / total).astype(BF)

    n = total_ref[0]
    next_ref[0] = n
    low = 0
    for width in VARIANTS:
        pl.when((n > low) & (n <= width))(functools.partial(variant, width))
        low = width


def attend(total, packed, bias, q, upk, upv, scale, first, heads, after):
    pairs, start = heads // 2, first // 2
    return pl.pallas_call(
        functools.partial(attend_kernel, scale),
        grid=(pairs,),
        out_shape=(jax.ShapeDtypeStruct((CAP, pairs * 256), BF), jax.ShapeDtypeStruct((1,), jnp.int32)),
        in_specs=[
            pl.BlockSpec(memory_space=pltpu.SMEM),
            pl.BlockSpec(memory_space=pltpu.VMEM),
            pl.BlockSpec(memory_space=pltpu.VMEM),
            pl.BlockSpec((2, CAP, 256), lambda i: (start + i, 0, 0)),
            pl.BlockSpec((LAT, 256), lambda i: (0, start + i)),
            pl.BlockSpec((LAT, 256), lambda i: (0, start + i)),
        ] + [pl.BlockSpec(memory_space=pltpu.HBM)] * len(after),
        out_specs=(pl.BlockSpec((CAP, 256), lambda i: (0, i)), pl.BlockSpec(memory_space=pltpu.SMEM)),
        scratch_shapes=[pltpu.VMEM((TOT, 256), BF), pltpu.VMEM((TOT, 256), BF)],
        cost_estimate=pl.CostEstimate(flops=pairs * 3 * 10 ** 9, bytes_accessed=pairs * 10 ** 6, transcendentals=0),
        compiler_params=pltpu.CompilerParams(vmem_limit_bytes=32 * MIB),
        name="attend_heads",
    )(total, packed, bias, q, upk, upv, *after)


def project_kernel(sel_ref, *refs):
    n = len(PARTS)
    rows, weights = refs[:2 * n], refs[2 * n:2 * n + 5]
    swapped = refs[2 * n + 5:2 * n + 10]
    outs = refs[2 * n + 10:2 * n + 12]
    a_ref, w_ref, sem_a, sem_w = refs[2 * n + 12:]
    ahead, core, slot = sel_ref[0], sel_ref[1], sel_ref[2]
    halves = [pl.ds(i * 1024, 1024) for i in range(2)]
    waits = []
    for p in range(2):
        first = 0
        for i, width in enumerate(PARTS):
            copy = pltpu.make_async_copy(rows[n * p + i], a_ref.at[slot ^ p, :, pl.ds(first * 128, width * 128)],
                                         sem_a.at[n * p + i])
            copy.start()
            waits.append((first // 8, copy))
            first += width
    for k, pieces in enumerate((((0, 0),), ((1, 0),), ((2, 0), (3, 224)), ((4, 0),))):
        for cc in range(2):
            @pl.when((ahead == k) & (core == cc))
            def _():
                for i in range(2):
                    for j, source in enumerate((weights, swapped)):
                        for index, start in pieces:
                            src = source[index]
                            pltpu.make_async_copy(
                                src.at[:, halves[i]],
                                w_ref.at[pl.ds((j ^ cc) * 448 + start, src.shape[0]), halves[i]], sem_w.at[i]).start()
    whole = None
    for i in range(2):
        for part, copy in waits:
            if part == i:
                copy.wait()
        pltpu.make_async_copy(w_ref.at[:, halves[1 - i]], w_ref.at[:, halves[i]], sem_w.at[i]).wait()
        term = lax.dot_general(a_ref[:, :, i * 1024:(i + 1) * 1024].reshape(2 * CAP, 1024),
                               w_ref[:, i * 1024:(i + 1) * 1024], (((1,), (1,)), ((), ())),
                               preferred_element_type=F32)
        whole = term if whole is None else whole + term
    for r in range(2):
        outs[r][...] = whole[r * CAP:(r + 1) * CAP].astype(BF)


def project(sel, rows, weights, swapped):
    operands = (*rows, *weights, *swapped)
    return pl.pallas_call(
        project_kernel,
        out_shape=(jax.ShapeDtypeStruct((CAP, 896), BF),) * 2,
        in_specs=[pl.BlockSpec(memory_space=pltpu.SMEM)] + [pl.BlockSpec(memory_space=pltpu.HBM)] * len(operands),
        out_specs=(pl.BlockSpec(memory_space=pltpu.VMEM),) * 2,
        scratch_shapes=[pltpu.VMEM((2, CAP, 2048), BF), pltpu.VMEM((896, 2048), BF),
                        pltpu.SemaphoreType.DMA((len(rows),)), pltpu.SemaphoreType.DMA((2,))],
        cost_estimate=pl.CostEstimate(flops=4 * CAP * 2048 * 896, bytes_accessed=8 * 10 ** 6, transcendentals=0),
        compiler_params=pltpu.CompilerParams(vmem_limit_bytes=58 * MIB),
        name="project_chunks",
    )(sel, *operands)


def behind(x, other):
    return pl.pallas_call(
        lambda *refs: None,
        out_shape=jax.ShapeDtypeStruct(x.shape, x.dtype),
        in_specs=[pl.BlockSpec(memory_space=pltpu.HBM)] * 2,
        out_specs=pl.BlockSpec(memory_space=pltpu.HBM),
        input_output_aliases={0: 0},
        name="behind",
    )(x, other)


CORE = [(s, s ^ 1) for s in range(16)]
ALONG_Y = [(s, s ^ 8) for s in range(16)]


def along_z(k):
    return [(s, (s // 8) * 8 + ((s // 2 + k) % 4) * 2 + s % 2) for s in range(16)]


def to_owner(r, dx):
    pairs = []
    for s in range(16):
        for h in range(8):
            y_lo, y_hi, x = s // 8, h // 4, h % 4
            pairs.append((s * 8 + h, ((y_hi ^ r) * 8 + s % 8) * 8 + y_lo * 4 + (x + dx) % 4))
    return pairs


def per_device(queries, latents, positions, up_keys, up_values, out_weight, residual, router_gate):
    heads, qk = queries.shape[1], queries.shape[2]
    s, h = lax.axis_index("seq"), lax.axis_index("head")
    y_lo, z, core = s // 8, (s // 2) % 4, s % 2
    y_hi, x = h // 4, h % 4
    own = payload(latents, positions)
    gathered = lax.all_gather(own, "seq", axis=0, tiled=True)
    weight = out_weight.T
    behind1 = lax.ppermute(weight, "seq", along_z(1))
    ahead1 = lax.ppermute(weight, "seq", along_z(3))
    core_own = lax.ppermute(weight, "seq", CORE)

    q = jnp.pad(jnp.transpose(queries, (1, 0, 2)), ((0, 0), (0, 0), (0, 256 - qk)))
    upk = up_keys.reshape(LAT, heads * 128)
    upv = up_values.reshape(LAT, heads * 128)

    packed, bias, total = prep(gathered, own)
    scale = (qk ** -0.5) * 1.4426950408889634
    mine, theirs, first = [], [], 0
    for i, width in enumerate(PARTS):
        after = (theirs[i - 2],) if i >= 2 else ()
        if i == 1:
            ahead1, behind1 = behind(ahead1, mine[0]), behind(behind1, mine[0])
            far0 = lax.ppermute(behind1[:224], "seq", along_z(1))
            far1 = lax.ppermute(ahead1[224:], "seq", along_z(3))
            core_ahead1, core_behind1 = lax.ppermute(ahead1, "seq", CORE), lax.ppermute(behind1, "seq", CORE)
            after += (ahead1, behind1, core_own)
        if i == 2:
            after += (core_ahead1, core_behind1)
        if i == 3:
            far0, far1 = behind(far0, mine[2]), behind(far1, mine[2])
            weights = (weight, ahead1, far0, far1, behind1)
            swapped = (core_own, core_ahead1, lax.ppermute(far0, "seq", CORE), lax.ppermute(far1, "seq", CORE), core_behind1)
            after += (far0, far1)
        part, total = attend(total, packed, bias, q, upk, upv, scale, first, width, after)
        first += width
        mine.append(part)
        theirs.append(lax.ppermute(part, "seq", ALONG_Y))

    received = []
    for dx in (2, 1, 3, 0):
        sel = jnp.stack([(x + dx - z) % 4, core, y_hi ^ y_lo]).astype(jnp.int32)
        chunks = project(sel, mine + theirs, weights, swapped)
        for r in (1, 0):
            received.append(lax.ppermute(chunks[r], ("seq", "head"), to_owner(r, dx)))
    projected = sum(r.astype(F32) for r in received)
    live_rows = (positions < SEQ_LEN).astype(F32)
    gated = (live_rows * router_gate)[:, None] * projected
    return (residual.astype(F32) + gated).astype(BF)


def solution(mesh):
    return jax.shard_map(
        per_device,
        mesh=mesh,
        in_specs=(
            P("seq", "head", None),
            P("seq", None),
            P("seq"),
            P(None, "head", None),
            P(None, "head", None),
            P("head", "seq"),
            P("seq", "head"),
            P("seq"),
        ),
        out_specs=P("seq", "head"),
        check_vma=False,
    )
```

```python
import functools
import jax
import jax.numpy as jnp
from jax import lax
from jax.experimental import pallas as pl
from jax.experimental.pallas import tpu as pltpu
from jax.sharding import PartitionSpec as P

SEQ_LEN = 131072
BF = jnp.bfloat16
F32 = jnp.float32
CAP = 192
SHARDS = 16
TOT = CAP * SHARDS
LAT = 512
WIDE = 640
MIB = 1024 * 1024
VARIANTS = (1024, 1280, 1536, TOT)
PARTS = (8, 6, 2)


def payload_kernel(lat_ref, pos_ref, out_ref):
    row = lax.broadcasted_iota(jnp.int32, (CAP, CAP), 0)
    col = lax.broadcasted_iota(jnp.int32, (CAP, CAP), 1)
    inv = jnp.sum(jnp.where(row == col, (SEQ_LEN - pos_ref[...]).astype(F32), 0.0), axis=1, keepdims=True)
    inv = inv.astype(jnp.int32)
    lane = lax.broadcasted_iota(jnp.int32, (CAP, 64), 1)
    digits = jnp.where(lane == 0, inv & 63, jnp.where(lane == 1, (inv >> 6) & 63, jnp.where(
        lane == 2, inv >> 12, jnp.where((lane == 3) & (inv > 0), 1, 0))))
    out_ref[...] = jnp.concatenate([lat_ref[...], digits.astype(F32).astype(BF)], axis=1)


def payload(latents, positions):
    return pl.pallas_call(
        payload_kernel,
        out_shape=jax.ShapeDtypeStruct((CAP, WIDE), BF),
        in_specs=[pl.BlockSpec(memory_space=pltpu.VMEM)] * 2,
        out_specs=pl.BlockSpec(memory_space=pltpu.VMEM),
        compiler_params=pltpu.CompilerParams(vmem_limit_bytes=4 * MIB),
        name="latents_and_positions",
    )(latents, positions.reshape(1, CAP))


def prep_kernel(all_ref, own_ref, *refs):
    packed_ref, bias_ref, total_ref = refs[-3:]
    packed_ref[...] = jnp.zeros_like(packed_ref)
    lane = lax.broadcasted_iota(jnp.int32, (CAP, 128), 1)
    counts = []
    for s in range(SHARDS):
        tail = all_ref[s * CAP:(s + 1) * CAP, LAT:WIDE].astype(F32)
        counts.append(jnp.sum(jnp.where(lane == 67, tail, 0.0)).astype(jnp.int32))
    diff = (lax.broadcasted_iota(jnp.int32, (CAP + 16, CAP), 0)
            - lax.broadcasted_iota(jnp.int32, (CAP + 16, CAP), 1))
    col = lax.broadcasted_iota(jnp.int32, (CAP + 16, CAP), 1)
    offset = jnp.int32(0)
    for s in range(SHARDS):
        first = pl.multiple_of((offset // 16) * 16, 16)
        shift = offset - first
        pick = jnp.where((diff == shift) & (col < counts[s]), 1.0, 0.0).astype(BF)
        moved = jnp.dot(pick, all_ref[s * CAP:(s + 1) * CAP, :],
                        preferred_element_type=F32).astype(BF)
        packed_ref[pl.ds(first, 16), :] = packed_ref[pl.ds(first, 16), :] + moved[:16]
        packed_ref[pl.ds(pl.multiple_of(first + 16, 16), CAP), :] = moved[16:]
        offset = offset + counts[s]
    total_ref[0] = offset
    lane8 = lax.broadcasted_iota(jnp.int32, (8, 128), 1)
    coef = jnp.where(lane8 == 64, 1.0, jnp.where(lane8 == 65, 64.0, jnp.where(lane8 == 66, 4096.0, 0.0)))
    key_inv = lax.dot_general(coef.astype(BF), packed_ref[0:TOT, LAT:WIDE],
                              (((1,), (1,)), ((), ())), preferred_element_type=F32)
    own = own_ref[:, LAT:WIDE].astype(F32)
    query_inv = jnp.sum(own * coef[0:1, :], axis=1, keepdims=True)
    bias_ref[...] = jnp.where(key_inv[0:1, :] >= query_inv, 0.0, -1e30)


def prep(gathered, own, after):
    return pl.pallas_call(
        prep_kernel,
        out_shape=(jax.ShapeDtypeStruct((TOT + 16, WIDE), BF),
                   jax.ShapeDtypeStruct((CAP, TOT), F32),
                   jax.ShapeDtypeStruct((1,), jnp.int32)),
        in_specs=[pl.BlockSpec(memory_space=pltpu.VMEM)] * 2 + [pl.BlockSpec(memory_space=pltpu.HBM)] * len(after),
        out_specs=(pl.BlockSpec(memory_space=pltpu.VMEM), pl.BlockSpec(memory_space=pltpu.VMEM),
                   pl.BlockSpec(memory_space=pltpu.SMEM)),
        compiler_params=pltpu.CompilerParams(vmem_limit_bytes=20 * MIB),
        name="pack_live_rows",
    )(gathered, own, *after)


def attend_kernel(scale, total_ref, packed_ref, bias_ref, q_ref, upk_ref, upv_ref, *rest):
    out_ref, next_ref, k_ref, v_ref = rest[-4:]

    def variant(width):
        for r in range(0, width, 256):
            x = packed_ref[r:r + 256, :LAT]
            k_ref[r:r + 256, :] = jnp.dot(x, upk_ref[...], preferred_element_type=F32).astype(BF)
            v_ref[r:r + 256, :] = jnp.dot(x, upv_ref[...], preferred_element_type=F32).astype(BF)
        for j in range(2):
            keys = jnp.concatenate(
                [k_ref[:width, j * 128:(j + 1) * 128], packed_ref[:width, LAT:WIDE]], axis=1)
            scores = lax.dot_general(q_ref[j], keys, (((1,), (1,)), ((), ())),
                                     preferred_element_type=F32)
            scores = scores * scale + bias_ref[:, :width]
            row_max = jnp.max(scores, axis=1, keepdims=True)
            weights = jnp.exp2(scores - row_max)
            total = jnp.sum(weights, axis=1, keepdims=True)
            summed = jnp.dot(weights.astype(BF), v_ref[:width, j * 128:(j + 1) * 128],
                             preferred_element_type=F32)
            out_ref[:, j * 128:(j + 1) * 128] = (summed / total).astype(BF)

    n = total_ref[0]
    next_ref[0] = n
    low = 0
    for width in VARIANTS:
        pl.when((n > low) & (n <= width))(functools.partial(variant, width))
        low = width


def attend(total, packed, bias, q, upk, upv, scale, first, heads, after):
    pairs, start = heads // 2, first // 2
    return pl.pallas_call(
        functools.partial(attend_kernel, scale),
        grid=(pairs,),
        out_shape=(jax.ShapeDtypeStruct((CAP, pairs * 256), BF), jax.ShapeDtypeStruct((1,), jnp.int32)),
        in_specs=[
            pl.BlockSpec(memory_space=pltpu.SMEM),
            pl.BlockSpec(memory_space=pltpu.VMEM),
            pl.BlockSpec(memory_space=pltpu.VMEM),
            pl.BlockSpec((2, CAP, 256), lambda i: (start + i, 0, 0)),
            pl.BlockSpec((LAT, 256), lambda i: (0, start + i)),
            pl.BlockSpec((LAT, 256), lambda i: (0, start + i)),
        ] + [pl.BlockSpec(memory_space=pltpu.HBM)] * len(after),
        out_specs=(pl.BlockSpec((CAP, 256), lambda i: (0, i)), pl.BlockSpec(memory_space=pltpu.SMEM)),
        scratch_shapes=[pltpu.VMEM((TOT, 256), BF), pltpu.VMEM((TOT, 256), BF)],
        cost_estimate=pl.CostEstimate(flops=pairs * 3 * 10 ** 9, bytes_accessed=pairs * 10 ** 6, transcendentals=0),
        compiler_params=pltpu.CompilerParams(vmem_limit_bytes=24 * MIB),
        name="attend_heads",
    )(total, packed, bias, q, upk, upv, *after)


def project_kernel(sel_ref, *refs):
    n = len(PARTS)
    rows, weights = refs[:2 * n], refs[2 * n:2 * n + 5]
    swapped = refs[2 * n + 5:2 * n + 10]
    outs = refs[2 * n + 10:2 * n + 12]
    a_ref, w_ref, sem_a, sem_w = refs[2 * n + 12:]
    ahead, core, slot = sel_ref[0], sel_ref[1], sel_ref[2]
    halves = [pl.ds(i * 1024, 1024) for i in range(2)]
    waits = []
    for p in range(2):
        first = 0
        for i, width in enumerate(PARTS):
            copy = pltpu.make_async_copy(rows[n * p + i], a_ref.at[slot ^ p, :, pl.ds(first * 128, width * 128)],
                                         sem_a.at[n * p + i])
            copy.start()
            waits.append((first // 8, copy))
            first += width
    for k, pieces in enumerate((((0, 0),), ((1, 0),), ((2, 0), (3, 224)), ((4, 0),))):
        for cc in range(2):
            @pl.when((ahead == k) & (core == cc))
            def _():
                for i in range(2):
                    for j, source in enumerate((weights, swapped)):
                        for index, start in pieces:
                            src = source[index]
                            pltpu.make_async_copy(
                                src.at[:, halves[i]],
                                w_ref.at[pl.ds((j ^ cc) * 448 + start, src.shape[0]), halves[i]], sem_w.at[i]).start()
    whole = None
    for i in range(2):
        for part, copy in waits:
            if part == i:
                copy.wait()
        pltpu.make_async_copy(w_ref.at[:, halves[1 - i]], w_ref.at[:, halves[i]], sem_w.at[i]).wait()
        term = lax.dot_general(a_ref[:, :, i * 1024:(i + 1) * 1024].reshape(2 * CAP, 1024),
                               w_ref[:, i * 1024:(i + 1) * 1024], (((1,), (1,)), ((), ())),
                               preferred_element_type=F32)
        whole = term if whole is None else whole + term
    for r in range(2):
        outs[r][...] = whole[r * CAP:(r + 1) * CAP].astype(BF)


def project(sel, rows, weights, swapped):
    operands = (*rows, *weights, *swapped)
    return pl.pallas_call(
        project_kernel,
        out_shape=(jax.ShapeDtypeStruct((CAP, 896), BF),) * 2,
        in_specs=[pl.BlockSpec(memory_space=pltpu.SMEM)] + [pl.BlockSpec(memory_space=pltpu.HBM)] * len(operands),
        out_specs=(pl.BlockSpec(memory_space=pltpu.VMEM),) * 2,
        scratch_shapes=[pltpu.VMEM((2, CAP, 2048), BF), pltpu.VMEM((896, 2048), BF),
                        pltpu.SemaphoreType.DMA((len(rows),)), pltpu.SemaphoreType.DMA((2,))],
        cost_estimate=pl.CostEstimate(flops=4 * CAP * 2048 * 896, bytes_accessed=8 * 10 ** 6, transcendentals=0),
        compiler_params=pltpu.CompilerParams(vmem_limit_bytes=58 * MIB),
        name="project_chunks",
    )(sel, *operands)


def behind(x, other):
    return pl.pallas_call(
        lambda *refs: None,
        out_shape=jax.ShapeDtypeStruct(x.shape, x.dtype),
        in_specs=[pl.BlockSpec(memory_space=pltpu.HBM), pl.BlockSpec(memory_space=pltpu.SMEM)],
        out_specs=pl.BlockSpec(memory_space=pltpu.HBM),
        input_output_aliases={0: 0},
        compiler_params=pltpu.CompilerParams(vmem_limit_bytes=MIB),
        name="behind",
    )(x, other)


CORE = [(s, s ^ 1) for s in range(16)]
ALONG_Y = [(s, s ^ 8) for s in range(16)]


def along_z(k):
    return [(s, (s // 8) * 8 + ((s // 2 + k) % 4) * 2 + s % 2) for s in range(16)]


def along_x(k):
    return [(h, (h // 4) * 4 + (h + k) % 4) for h in range(8)]


def to_owner(r, dx):
    pairs = []
    for s in range(16):
        for h in range(8):
            y_lo, y_hi, x = s // 8, h // 4, h % 4
            pairs.append((s * 8 + h, ((y_hi ^ r) * 8 + s % 8) * 8 + y_lo * 4 + (x + dx) % 4))
    return pairs


def per_device(queries, latents, positions, up_keys, up_values, out_weight, residual, router_gate):
    heads, qk = queries.shape[1], queries.shape[2]
    s, h = lax.axis_index("seq"), lax.axis_index("head")
    y_lo, z, core = s // 8, (s // 2) % 4, s % 2
    y_hi, x = h // 4, h % 4
    own = payload(latents, positions)
    gathered = lax.all_gather(own, "seq", axis=0, tiled=True)
    weight = out_weight.T
    behind1 = lax.ppermute(weight, "seq", along_z(1))
    ahead1 = lax.ppermute(weight, "seq", along_z(3))
    core_own = lax.ppermute(weight, "seq", CORE)

    q = jnp.pad(jnp.transpose(queries, (1, 0, 2)), ((0, 0), (0, 0), (0, 256 - qk)))
    upk = up_keys.reshape(LAT, heads * 128)
    upv = up_values.reshape(LAT, heads * 128)

    packed, bias, total = prep(gathered, own, (q, upk, upv))
    scale = (qk ** -0.5) * 1.4426950408889634
    ahead1, behind1 = behind(ahead1, total), behind(behind1, total)
    far0 = lax.ppermute(behind1[:224], "seq", along_z(1))
    far1 = lax.ppermute(ahead1[224:], "seq", along_z(3))
    core_ahead1, core_behind1 = lax.ppermute(ahead1, "seq", CORE), lax.ppermute(behind1, "seq", CORE)
    mine, theirs, first = [], [], 0
    for i, width in enumerate(PARTS):
        after = ((core_own,), (core_ahead1, core_behind1), tuple(theirs[:1]))[i]
        part, total = attend(total, packed, bias, q, upk, upv, scale, first, width, after)
        first += width
        mine.append(part)
        theirs.append(lax.ppermute(part, "seq", ALONG_Y))
    far0, far1 = behind(far0, total), behind(far1, total)
    weights = (weight, ahead1, far0, far1, behind1)
    swapped = (core_own, core_ahead1, lax.ppermute(far0, "seq", CORE), lax.ppermute(far1, "seq", CORE), core_behind1)

    direct, crossing = [], []
    for dx in (2, 1, 3, 0):
        sel = jnp.stack([(x + dx - z) % 4, core, y_hi ^ y_lo]).astype(jnp.int32)
        chunks = project(sel, mine + theirs, weights, swapped)
        crossing.append(lax.ppermute(chunks[1], "head", along_x(dx)) if dx else chunks[1])
        direct.append(lax.ppermute(chunks[0], ("seq", "head"), to_owner(0, dx)))
    crossed = lax.ppermute(sum(c.astype(F32) for c in crossing).astype(BF), ("seq", "head"), to_owner(1, 0))
    projected = sum(r.astype(F32) for r in direct) + crossed.astype(F32)
    live_rows = (positions < SEQ_LEN).astype(F32)
    gated = (live_rows * router_gate)[:, None] * projected
    return (residual.astype(F32) + gated).astype(BF)


def solution(mesh):
    return jax.shard_map(
        per_device,
        mesh=mesh,
        in_specs=(
            P("seq", "head", None),
            P("seq", None),
            P("seq"),
            P(None, "head", None),
            P(None, "head", None),
            P("head", "seq"),
            P("seq", "head"),
            P("seq"),
        ),
        out_specs=P("seq", "head"),
        check_vma=False,
    )
```

```python
import functools
import jax
import jax.numpy as jnp
from jax import lax
from jax.experimental import pallas as pl
from jax.experimental.pallas import tpu as pltpu
from jax.sharding import PartitionSpec as P

SEQ_LEN = 131072
BF = jnp.bfloat16
F32 = jnp.float32
CAP = 192
SHARDS = 16
TOT = CAP * SHARDS
LAT = 512
WIDE = 640
MIB = 1024 * 1024
VARIANTS = (1024, 1280, 1536, TOT)
PARTS = (8, 6, 2)


def payload_kernel(lat_ref, pos_ref, out_ref):
    row = lax.broadcasted_iota(jnp.int32, (CAP, CAP), 0)
    col = lax.broadcasted_iota(jnp.int32, (CAP, CAP), 1)
    inv = jnp.sum(jnp.where(row == col, (SEQ_LEN - pos_ref[...]).astype(F32), 0.0), axis=1, keepdims=True)
    inv = inv.astype(jnp.int32)
    lane = lax.broadcasted_iota(jnp.int32, (CAP, 64), 1)
    digits = jnp.where(lane == 0, inv & 63, jnp.where(lane == 1, (inv >> 6) & 63, jnp.where(
        lane == 2, inv >> 12, jnp.where((lane == 3) & (inv > 0), 1, 0))))
    out_ref[...] = jnp.concatenate([lat_ref[...], digits.astype(F32).astype(BF)], axis=1)


def payload(latents, positions):
    return pl.pallas_call(
        payload_kernel,
        out_shape=jax.ShapeDtypeStruct((CAP, WIDE), BF),
        in_specs=[pl.BlockSpec(memory_space=pltpu.VMEM)] * 2,
        out_specs=pl.BlockSpec(memory_space=pltpu.VMEM),
        compiler_params=pltpu.CompilerParams(vmem_limit_bytes=4 * MIB),
        name="latents_and_positions",
    )(latents, positions.reshape(1, CAP))


def prep_kernel(all_ref, own_ref, *refs):
    out_ref, key_ref, query_ref, total_ref, packed_ref, sem = refs[-6:]
    packed_ref[...] = jnp.zeros_like(packed_ref)
    lane = lax.broadcasted_iota(jnp.int32, (CAP, 128), 1)
    counts = []
    for s in range(SHARDS):
        tail = all_ref[s * CAP:(s + 1) * CAP, LAT:WIDE].astype(F32)
        counts.append(jnp.sum(jnp.where(lane == 67, tail, 0.0)).astype(jnp.int32))
    diff = (lax.broadcasted_iota(jnp.int32, (CAP + 16, CAP), 0)
            - lax.broadcasted_iota(jnp.int32, (CAP + 16, CAP), 1))
    col = lax.broadcasted_iota(jnp.int32, (CAP + 16, CAP), 1)
    offset = jnp.int32(0)
    for s in range(SHARDS):
        first = pl.multiple_of((offset // 16) * 16, 16)
        shift = offset - first
        pick = jnp.where((diff == shift) & (col < counts[s]), 1.0, 0.0).astype(BF)
        moved = jnp.dot(pick, all_ref[s * CAP:(s + 1) * CAP, :],
                        preferred_element_type=F32).astype(BF)
        packed_ref[pl.ds(first, 16), :] = packed_ref[pl.ds(first, 16), :] + moved[:16]
        packed_ref[pl.ds(pl.multiple_of(first + 16, 16), CAP), :] = moved[16:]
        offset = offset + counts[s]
    total_ref[0] = offset
    lane8 = lax.broadcasted_iota(jnp.int32, (8, 128), 1)
    coef = jnp.where(lane8 == 64, 1.0, jnp.where(lane8 == 65, 64.0, jnp.where(lane8 == 66, 4096.0, 0.0)))
    key_ref[...] = lax.dot_general(coef.astype(BF), packed_ref[0:TOT, LAT:WIDE],
                                   (((1,), (1,)), ((), ())), preferred_element_type=F32)
    own = own_ref[:, LAT:WIDE].astype(F32)
    query_ref[...] = jnp.broadcast_to(jnp.sum(own * coef[0:1, :], axis=1, keepdims=True), query_ref.shape)
    low = 0
    for width in VARIANTS:
        @pl.when((offset > low) & (offset <= width))
        def _():
            copy = pltpu.make_async_copy(packed_ref.at[pl.ds(0, width)], out_ref.at[pl.ds(0, width)], sem)
            copy.start()
            copy.wait()
        low = width


def prep(gathered, own, after):
    return pl.pallas_call(
        prep_kernel,
        out_shape=(jax.ShapeDtypeStruct((TOT, WIDE), BF),
                   jax.ShapeDtypeStruct((8, TOT), F32),
                   jax.ShapeDtypeStruct((CAP, 128), F32),
                   jax.ShapeDtypeStruct((1,), jnp.int32)),
        in_specs=[pl.BlockSpec(memory_space=pltpu.VMEM)] * 2 + [pl.BlockSpec(memory_space=pltpu.HBM)] * len(after),
        out_specs=(pl.BlockSpec(memory_space=pltpu.HBM), pl.BlockSpec(memory_space=pltpu.VMEM),
                   pl.BlockSpec(memory_space=pltpu.VMEM), pl.BlockSpec(memory_space=pltpu.SMEM)),
        scratch_shapes=[pltpu.VMEM((TOT + 16, WIDE), BF), pltpu.SemaphoreType.DMA],
        compiler_params=pltpu.CompilerParams(vmem_limit_bytes=50 * MIB),
        name="pack_live_rows",
    )(gathered, own, *after)


def attend_kernel(scale, total_ref, source_ref, key_ref, query_ref, q_ref, upk_ref, upv_ref, *rest):
    out_ref, next_ref, k_ref, v_ref, packed_ref, bias_ref, sem = rest[-7:]

    def variant(width):
        @pl.when(pl.program_id(0) == 0)
        def _():
            copy = pltpu.make_async_copy(source_ref.at[pl.ds(0, width)], packed_ref.at[pl.ds(0, width)], sem)
            copy.start()
            bias_ref[:, :width] = jnp.where(key_ref[0:1, :width] >= query_ref[:, 0:1], 0.0, -1e30)
            copy.wait()

        for r in range(0, width, 256):
            x = packed_ref[r:r + 256, :LAT]
            k_ref[r:r + 256, :] = jnp.dot(x, upk_ref[...], preferred_element_type=F32).astype(BF)
            v_ref[r:r + 256, :] = jnp.dot(x, upv_ref[...], preferred_element_type=F32).astype(BF)
        for j in range(2):
            keys = jnp.concatenate(
                [k_ref[:width, j * 128:(j + 1) * 128], packed_ref[:width, LAT:WIDE]], axis=1)
            scores = lax.dot_general(q_ref[j], keys, (((1,), (1,)), ((), ())),
                                     preferred_element_type=F32)
            scores = scores * scale + bias_ref[:, :width]
            row_max = jnp.max(scores, axis=1, keepdims=True)
            weights = jnp.exp2(scores - row_max)
            total = jnp.sum(weights, axis=1, keepdims=True)
            summed = jnp.dot(weights.astype(BF), v_ref[:width, j * 128:(j + 1) * 128],
                             preferred_element_type=F32)
            out_ref[:, j * 128:(j + 1) * 128] = (summed / total).astype(BF)

    n = total_ref[0]
    next_ref[0] = n
    low = 0
    for width in VARIANTS:
        pl.when((n > low) & (n <= width))(functools.partial(variant, width))
        low = width


def attend(total, packed, keys, queries, q, upk, upv, scale, first, heads, after):
    pairs, start = heads // 2, first // 2
    return pl.pallas_call(
        functools.partial(attend_kernel, scale),
        grid=(pairs,),
        out_shape=(jax.ShapeDtypeStruct((CAP, pairs * 256), BF), jax.ShapeDtypeStruct((1,), jnp.int32)),
        in_specs=[
            pl.BlockSpec(memory_space=pltpu.SMEM),
            pl.BlockSpec(memory_space=pltpu.HBM),
            pl.BlockSpec(memory_space=pltpu.VMEM),
            pl.BlockSpec(memory_space=pltpu.VMEM),
            pl.BlockSpec((2, CAP, 256), lambda i: (start + i, 0, 0)),
            pl.BlockSpec((LAT, 256), lambda i: (0, start + i)),
            pl.BlockSpec((LAT, 256), lambda i: (0, start + i)),
        ] + [pl.BlockSpec(memory_space=pltpu.HBM)] * len(after),
        out_specs=(pl.BlockSpec((CAP, 256), lambda i: (0, i)), pl.BlockSpec(memory_space=pltpu.SMEM)),
        scratch_shapes=[pltpu.VMEM((TOT, 256), BF), pltpu.VMEM((TOT, 256), BF), pltpu.VMEM((TOT, WIDE), BF),
                        pltpu.VMEM((CAP, TOT), F32), pltpu.SemaphoreType.DMA],
        cost_estimate=pl.CostEstimate(flops=pairs * 3 * 10 ** 9, bytes_accessed=pairs * 10 ** 6, transcendentals=0),
        compiler_params=pltpu.CompilerParams(vmem_limit_bytes=50 * MIB),
        name="attend_heads",
    )(total, packed, keys, queries, q, upk, upv, *after)


def project_kernel(sel_ref, *refs):
    n = len(PARTS)
    rows, weights = refs[:2 * n], refs[2 * n:2 * n + 5]
    swapped = refs[2 * n + 5:2 * n + 10]
    outs = refs[2 * n + 10:2 * n + 14]
    a_ref, w_ref, sem_a, sem_w = refs[2 * n + 14:]
    core, slot = sel_ref[2], sel_ref[3]
    waits = []
    for p in range(2):
        first = 0
        for i, width in enumerate(PARTS):
            copy = pltpu.make_async_copy(rows[n * p + i], a_ref.at[slot ^ p, :, pl.ds(first * 128, width * 128)],
                                         sem_a.at[n * p + i])
            copy.start()
            waits.append(copy)
            first += width
    for t in range(2):
        for k, pieces in enumerate((((0, 0),), ((1, 0),), ((2, 0), (3, 224)), ((4, 0),))):
            for cc in range(2):
                @pl.when((sel_ref[t] == k) & (core == cc))
                def _():
                    for j, source in enumerate((weights, swapped)):
                        for index, start in pieces:
                            src = source[index]
                            pltpu.make_async_copy(
                                src, w_ref.at[t, pl.ds((j ^ cc) * 448 + start, src.shape[0])], sem_w.at[t]).start()
    for copy in waits:
        copy.wait()
    for t in range(2):
        pltpu.make_async_copy(w_ref.at[1 - t], w_ref.at[t], sem_w.at[t]).wait()
        whole = lax.dot_general(a_ref[...].reshape(2 * CAP, 2048), w_ref[t], (((1,), (1,)), ((), ())),
                                preferred_element_type=F32)
        for r in range(2):
            outs[2 * t + r][...] = whole[r * CAP:(r + 1) * CAP].astype(BF)


def project(sel, rows, weights, swapped):
    operands = (*rows, *weights, *swapped)
    return pl.pallas_call(
        project_kernel,
        out_shape=(jax.ShapeDtypeStruct((CAP, 896), BF),) * 4,
        in_specs=[pl.BlockSpec(memory_space=pltpu.SMEM)] + [pl.BlockSpec(memory_space=pltpu.HBM)] * len(operands),
        out_specs=(pl.BlockSpec(memory_space=pltpu.VMEM),) * 4,
        scratch_shapes=[pltpu.VMEM((2, CAP, 2048), BF), pltpu.VMEM((2, 896, 2048), BF),
                        pltpu.SemaphoreType.DMA((len(rows),)), pltpu.SemaphoreType.DMA((2,))],
        cost_estimate=pl.CostEstimate(flops=8 * CAP * 2048 * 896, bytes_accessed=12 * 10 ** 6, transcendentals=0),
        compiler_params=pltpu.CompilerParams(vmem_limit_bytes=58 * MIB),
        name="project_chunks",
    )(sel, *operands)


def behind(x, other):
    return pl.pallas_call(
        lambda *refs: None,
        out_shape=jax.ShapeDtypeStruct(x.shape, x.dtype),
        in_specs=[pl.BlockSpec(memory_space=pltpu.HBM), pl.BlockSpec(memory_space=pltpu.SMEM)],
        out_specs=pl.BlockSpec(memory_space=pltpu.HBM),
        input_output_aliases={0: 0},
        compiler_params=pltpu.CompilerParams(vmem_limit_bytes=MIB),
        name="behind",
    )(x, other)


CORE = [(s, s ^ 1) for s in range(16)]
ALONG_Y = [(s, s ^ 8) for s in range(16)]


def along_z(k):
    return [(s, (s // 8) * 8 + ((s // 2 + k) % 4) * 2 + s % 2) for s in range(16)]


def along_x(k):
    return [(h, (h // 4) * 4 + (h + k) % 4) for h in range(8)]


def to_owner(r, dx):
    pairs = []
    for s in range(16):
        for h in range(8):
            y_lo, y_hi, x = s // 8, h // 4, h % 4
            pairs.append((s * 8 + h, ((y_hi ^ r) * 8 + s % 8) * 8 + y_lo * 4 + (x + dx) % 4))
    return pairs


def per_device(queries, latents, positions, up_keys, up_values, out_weight, residual, router_gate):
    heads, qk = queries.shape[1], queries.shape[2]
    s, h = lax.axis_index("seq"), lax.axis_index("head")
    y_lo, z, core = s // 8, (s // 2) % 4, s % 2
    y_hi, x = h // 4, h % 4
    own = payload(latents, positions)
    gathered = lax.all_gather(own, "seq", axis=0, tiled=True)
    weight = out_weight.T
    behind1 = lax.ppermute(weight, "seq", along_z(1))
    ahead1 = lax.ppermute(weight, "seq", along_z(3))
    core_own = lax.ppermute(weight, "seq", CORE)

    q = jnp.pad(jnp.transpose(queries, (1, 0, 2)), ((0, 0), (0, 0), (0, 256 - qk)))
    upk = up_keys.reshape(LAT, heads * 128)
    upv = up_values.reshape(LAT, heads * 128)

    packed, key_inv, query_inv, total = prep(gathered, own, (q, upk, upv))
    scale = (qk ** -0.5) * 1.4426950408889634
    ahead1, behind1 = behind(ahead1, total), behind(behind1, total)
    far0 = lax.ppermute(behind1[:224], "seq", along_z(1))
    far1 = lax.ppermute(ahead1[224:], "seq", along_z(3))
    core_ahead1, core_behind1 = lax.ppermute(ahead1, "seq", CORE), lax.ppermute(behind1, "seq", CORE)
    mine, theirs, first, after = [], [], 0, (core_own,)
    for i, width in enumerate(PARTS):
        part, total = attend(total, packed, key_inv, query_inv, q, upk, upv, scale, first, width, after)
        first += width
        mine.append(part)
        theirs.append(lax.ppermute(part, "seq", ALONG_Y))
        if i == 0:
            far0, far1 = behind(far0, total), behind(far1, total)
            core_far0, core_far1 = lax.ppermute(far0, "seq", CORE), lax.ppermute(far1, "seq", CORE)
            after = (far0, far1, core_ahead1, core_behind1)
        else:
            after = (theirs[0], core_far0, core_far1)
    weights = (weight, ahead1, far0, far1, behind1)
    swapped = (core_own, core_ahead1, core_far0, core_far1, core_behind1)

    direct, crossing = [], []
    for pair in ((2, 1), (3, 0)):
        sel = jnp.stack([(x + dx - z) % 4 for dx in pair] + [core, y_hi ^ y_lo]).astype(jnp.int32)
        chunks = project(sel, mine + theirs, weights, swapped)
        for t, dx in enumerate(pair):
            direct.append(lax.ppermute(chunks[2 * t], ("seq", "head"), to_owner(0, dx)))
            crossing.append(lax.ppermute(chunks[2 * t + 1], "head", along_x(dx)) if dx else chunks[2 * t + 1])
    crossed = lax.ppermute(sum(c.astype(F32) for c in crossing).astype(BF), ("seq", "head"), to_owner(1, 0))
    projected = sum(r.astype(F32) for r in direct) + crossed.astype(F32)
    live_rows = (positions < SEQ_LEN).astype(F32)
    gated = (live_rows * router_gate)[:, None] * projected
    return (residual.astype(F32) + gated).astype(BF)


def solution(mesh):
    return jax.shard_map(
        per_device,
        mesh=mesh,
        in_specs=(
            P("seq", "head", None),
            P("seq", None),
            P("seq"),
            P(None, "head", None),
            P(None, "head", None),
            P("head", "seq"),
            P("seq", "head"),
            P("seq"),
        ),
        out_specs=P("seq", "head"),
        check_vma=False,
    )
```

```python
import functools
import jax
import jax.numpy as jnp
from jax import lax
from jax.experimental import pallas as pl
from jax.experimental.pallas import tpu as pltpu
from jax.sharding import PartitionSpec as P

SEQ_LEN = 131072
BF = jnp.bfloat16
F32 = jnp.float32
CAP = 192
SHARDS = 16
TOT = CAP * SHARDS
LAT = 512
WIDE = 640
MIB = 1024 * 1024
VARIANTS = (1024, 1280, 1536, TOT)
PARTS = (8, 6, 2)


def payload_kernel(lat_ref, pos_ref, out_ref):
    row = lax.broadcasted_iota(jnp.int32, (CAP, CAP), 0)
    col = lax.broadcasted_iota(jnp.int32, (CAP, CAP), 1)
    inv = jnp.sum(jnp.where(row == col, (SEQ_LEN - pos_ref[...]).astype(F32), 0.0), axis=1, keepdims=True)
    inv = inv.astype(jnp.int32)
    lane = lax.broadcasted_iota(jnp.int32, (CAP, 64), 1)
    digits = jnp.where(lane == 0, inv & 63, jnp.where(lane == 1, (inv >> 6) & 63, jnp.where(
        lane == 2, inv >> 12, jnp.where((lane == 3) & (inv > 0), 1, 0))))
    out_ref[...] = jnp.concatenate([lat_ref[...], digits.astype(F32).astype(BF)], axis=1)


def payload(latents, positions):
    return pl.pallas_call(
        payload_kernel,
        out_shape=jax.ShapeDtypeStruct((CAP, WIDE), BF),
        in_specs=[pl.BlockSpec(memory_space=pltpu.VMEM)] * 2,
        out_specs=pl.BlockSpec(memory_space=pltpu.VMEM),
        compiler_params=pltpu.CompilerParams(vmem_limit_bytes=4 * MIB),
        name="latents_and_positions",
    )(latents, positions.reshape(1, CAP))


def prep_kernel(all_ref, own_ref, *refs):
    out_ref, key_ref, query_ref, total_ref, packed_ref, sem = refs[-6:]
    packed_ref[...] = jnp.zeros_like(packed_ref)
    lane = lax.broadcasted_iota(jnp.int32, (CAP, 128), 1)
    counts = []
    for s in range(SHARDS):
        tail = all_ref[s * CAP:(s + 1) * CAP, LAT:WIDE].astype(F32)
        counts.append(jnp.sum(jnp.where(lane == 67, tail, 0.0)).astype(jnp.int32))
    diff = (lax.broadcasted_iota(jnp.int32, (CAP + 16, CAP), 0)
            - lax.broadcasted_iota(jnp.int32, (CAP + 16, CAP), 1))
    col = lax.broadcasted_iota(jnp.int32, (CAP + 16, CAP), 1)
    offset = jnp.int32(0)
    for s in range(SHARDS):
        first = pl.multiple_of((offset // 16) * 16, 16)
        shift = offset - first
        pick = jnp.where((diff == shift) & (col < counts[s]), 1.0, 0.0).astype(BF)
        moved = jnp.dot(pick, all_ref[s * CAP:(s + 1) * CAP, :],
                        preferred_element_type=F32).astype(BF)
        packed_ref[pl.ds(first, 16), :] = packed_ref[pl.ds(first, 16), :] + moved[:16]
        packed_ref[pl.ds(pl.multiple_of(first + 16, 16), CAP), :] = moved[16:]
        offset = offset + counts[s]
    total_ref[0] = offset
    lane8 = lax.broadcasted_iota(jnp.int32, (8, 128), 1)
    coef = jnp.where(lane8 == 64, 1.0, jnp.where(lane8 == 65, 64.0, jnp.where(lane8 == 66, 4096.0, 0.0)))
    key_ref[...] = lax.dot_general(coef.astype(BF), packed_ref[0:TOT, LAT:WIDE],
                                   (((1,), (1,)), ((), ())), preferred_element_type=F32)
    own = own_ref[:, LAT:WIDE].astype(F32)
    query_ref[...] = jnp.broadcast_to(jnp.sum(own * coef[0:1, :], axis=1, keepdims=True), query_ref.shape)
    low = 0
    for width in VARIANTS:
        @pl.when((offset > low) & (offset <= width))
        def _():
            copy = pltpu.make_async_copy(packed_ref.at[pl.ds(0, width)], out_ref.at[pl.ds(0, width)], sem)
            copy.start()
            copy.wait()
        low = width


def prep(gathered, own, after):
    return pl.pallas_call(
        prep_kernel,
        out_shape=(jax.ShapeDtypeStruct((TOT, WIDE), BF),
                   jax.ShapeDtypeStruct((8, TOT), F32),
                   jax.ShapeDtypeStruct((CAP, 128), F32),
                   jax.ShapeDtypeStruct((1,), jnp.int32)),
        in_specs=[pl.BlockSpec(memory_space=pltpu.VMEM)] * 2 + [pl.BlockSpec(memory_space=pltpu.HBM)] * len(after),
        out_specs=(pl.BlockSpec(memory_space=pltpu.HBM), pl.BlockSpec(memory_space=pltpu.VMEM),
                   pl.BlockSpec(memory_space=pltpu.VMEM), pl.BlockSpec(memory_space=pltpu.SMEM)),
        scratch_shapes=[pltpu.VMEM((TOT + 16, WIDE), BF), pltpu.SemaphoreType.DMA],
        compiler_params=pltpu.CompilerParams(vmem_limit_bytes=50 * MIB),
        name="pack_live_rows",
    )(gathered, own, *after)


def attend_kernel(scale, total_ref, source_ref, key_ref, query_ref, q_ref, upk_ref, upv_ref, *rest):
    out_ref, next_ref, k_ref, v_ref, packed_ref, bias_ref, sem = rest[-7:]

    def variant(width):
        @pl.when(pl.program_id(0) == 0)
        def _():
            copy = pltpu.make_async_copy(source_ref.at[pl.ds(0, width)], packed_ref.at[pl.ds(0, width)], sem)
            copy.start()
            bias_ref[:, :width] = jnp.where(key_ref[0:1, :width] >= query_ref[:, 0:1], 0.0, -1e30)
            copy.wait()

        for r in range(0, width, 256):
            x = packed_ref[r:r + 256, :LAT]
            k_ref[r:r + 256, :] = jnp.dot(x, upk_ref[...], preferred_element_type=F32).astype(BF)
            v_ref[r:r + 256, :] = jnp.dot(x, upv_ref[...], preferred_element_type=F32).astype(BF)
        for j in range(2):
            keys = jnp.concatenate(
                [k_ref[:width, j * 128:(j + 1) * 128], packed_ref[:width, LAT:WIDE]], axis=1)
            scores = lax.dot_general(q_ref[j], keys, (((1,), (1,)), ((), ())),
                                     preferred_element_type=F32)
            scores = scores * scale + bias_ref[:, :width]
            row_max = jnp.max(scores, axis=1, keepdims=True)
            weights = jnp.exp2(scores - row_max)
            total = jnp.sum(weights, axis=1, keepdims=True)
            summed = jnp.dot(weights.astype(BF), v_ref[:width, j * 128:(j + 1) * 128],
                             preferred_element_type=F32)
            out_ref[:, j * 128:(j + 1) * 128] = (summed / total).astype(BF)

    n = total_ref[0]
    next_ref[0] = n
    low = 0
    for width in VARIANTS:
        pl.when((n > low) & (n <= width))(functools.partial(variant, width))
        low = width


def attend(total, packed, keys, queries, q, upk, upv, scale, first, heads, after):
    pairs, start = heads // 2, first // 2
    return pl.pallas_call(
        functools.partial(attend_kernel, scale),
        grid=(pairs,),
        out_shape=(jax.ShapeDtypeStruct((CAP, pairs * 256), BF), jax.ShapeDtypeStruct((1,), jnp.int32)),
        in_specs=[
            pl.BlockSpec(memory_space=pltpu.SMEM),
            pl.BlockSpec(memory_space=pltpu.HBM),
            pl.BlockSpec(memory_space=pltpu.VMEM),
            pl.BlockSpec(memory_space=pltpu.VMEM),
            pl.BlockSpec((2, CAP, 256), lambda i: (start + i, 0, 0)),
            pl.BlockSpec((LAT, 256), lambda i: (0, start + i)),
            pl.BlockSpec((LAT, 256), lambda i: (0, start + i)),
        ] + [pl.BlockSpec(memory_space=pltpu.HBM)] * len(after),
        out_specs=(pl.BlockSpec((CAP, 256), lambda i: (0, i)), pl.BlockSpec(memory_space=pltpu.SMEM)),
        scratch_shapes=[pltpu.VMEM((TOT, 256), BF), pltpu.VMEM((TOT, 256), BF), pltpu.VMEM((TOT, WIDE), BF),
                        pltpu.VMEM((CAP, TOT), F32), pltpu.SemaphoreType.DMA],
        cost_estimate=pl.CostEstimate(flops=pairs * 10 ** 8, bytes_accessed=0, transcendentals=0),
        compiler_params=pltpu.CompilerParams(vmem_limit_bytes=50 * MIB),
        name="attend_heads",
    )(total, packed, keys, queries, q, upk, upv, *after)


def project_kernel(sel_ref, *refs):
    n = len(PARTS)
    rows, weights = refs[:2 * n], refs[2 * n:2 * n + 5]
    swapped = refs[2 * n + 5:2 * n + 10]
    outs = refs[2 * n + 10:2 * n + 14]
    a_ref, w_ref, sem_a, sem_w = refs[2 * n + 14:]
    core, slot = sel_ref[2], sel_ref[3]
    waits = []
    for p in range(2):
        first = 0
        for i, width in enumerate(PARTS):
            copy = pltpu.make_async_copy(rows[n * p + i], a_ref.at[slot ^ p, :, pl.ds(first * 128, width * 128)],
                                         sem_a.at[n * p + i])
            copy.start()
            waits.append(copy)
            first += width
    for t in range(2):
        for k, pieces in enumerate((((0, 0),), ((1, 0),), ((2, 0), (3, 224)), ((4, 0),))):
            for cc in range(2):
                @pl.when((sel_ref[t] == k) & (core == cc))
                def _():
                    for j, source in enumerate((weights, swapped)):
                        for index, start in pieces:
                            src = source[index]
                            pltpu.make_async_copy(
                                src, w_ref.at[t, pl.ds((j ^ cc) * 448 + start, src.shape[0])], sem_w.at[t]).start()
    for copy in waits:
        copy.wait()
    for t in range(2):
        pltpu.make_async_copy(w_ref.at[1 - t], w_ref.at[t], sem_w.at[t]).wait()
        whole = lax.dot_general(a_ref[...].reshape(2 * CAP, 2048), w_ref[t], (((1,), (1,)), ((), ())),
                                preferred_element_type=F32)
        for r in range(2):
            outs[2 * t + r][...] = whole[r * CAP:(r + 1) * CAP].astype(BF)


def project(sel, rows, weights, swapped):
    operands = (*rows, *weights, *swapped)
    return pl.pallas_call(
        project_kernel,
        out_shape=(jax.ShapeDtypeStruct((CAP, 896), BF),) * 4,
        in_specs=[pl.BlockSpec(memory_space=pltpu.SMEM)] + [pl.BlockSpec(memory_space=pltpu.HBM)] * len(operands),
        out_specs=(pl.BlockSpec(memory_space=pltpu.VMEM),) * 4,
        scratch_shapes=[pltpu.VMEM((2, CAP, 2048), BF), pltpu.VMEM((2, 896, 2048), BF),
                        pltpu.SemaphoreType.DMA((len(rows),)), pltpu.SemaphoreType.DMA((2,))],
        cost_estimate=pl.CostEstimate(flops=10 ** 8, bytes_accessed=0, transcendentals=0),
        compiler_params=pltpu.CompilerParams(vmem_limit_bytes=58 * MIB),
        name="project_chunks",
    )(sel, *operands)


def behind(x, other, more):
    return pl.pallas_call(
        lambda *refs: None,
        out_shape=jax.ShapeDtypeStruct(x.shape, x.dtype),
        in_specs=[pl.BlockSpec(memory_space=pltpu.HBM), pl.BlockSpec(memory_space=pltpu.SMEM)]
        + [pl.BlockSpec(memory_space=pltpu.HBM)] * len(more),
        out_specs=pl.BlockSpec(memory_space=pltpu.HBM),
        input_output_aliases={0: 0},
        cost_estimate=pl.CostEstimate(flops=0, bytes_accessed=0, transcendentals=0),
        compiler_params=pltpu.CompilerParams(vmem_limit_bytes=MIB),
        name="behind",
    )(x, other, *more)


def total_kernel(*refs):
    total = refs[0][...].astype(F32)
    for ref in refs[1:4]:
        total = total + ref[...].astype(F32)
    refs[-1][...] = total.astype(BF)


def total_of(chunks, after):
    return pl.pallas_call(
        total_kernel,
        out_shape=jax.ShapeDtypeStruct(chunks[0].shape, BF),
        in_specs=[pl.BlockSpec(memory_space=pltpu.VMEM)] * 4 + [pl.BlockSpec(memory_space=pltpu.HBM)] * len(after),
        out_specs=pl.BlockSpec(memory_space=pltpu.VMEM),
        compiler_params=pltpu.CompilerParams(vmem_limit_bytes=8 * MIB),
        name="sum_over_x",
    )(*chunks, *after)


CORE = [(s, s ^ 1) for s in range(16)]
ALONG_Y = [(s, s ^ 8) for s in range(16)]


def along_z(k):
    return [(s, (s // 8) * 8 + ((s // 2 + k) % 4) * 2 + s % 2) for s in range(16)]


def along_x(k):
    return [(h, (h // 4) * 4 + (h + k) % 4) for h in range(8)]


def to_owner(r, dx):
    pairs = []
    for s in range(16):
        for h in range(8):
            y_lo, y_hi, x = s // 8, h // 4, h % 4
            pairs.append((s * 8 + h, ((y_hi ^ r) * 8 + s % 8) * 8 + y_lo * 4 + (x + dx) % 4))
    return pairs


def per_device(queries, latents, positions, up_keys, up_values, out_weight, residual, router_gate):
    heads, qk = queries.shape[1], queries.shape[2]
    s, h = lax.axis_index("seq"), lax.axis_index("head")
    y_lo, z, core = s // 8, (s // 2) % 4, s % 2
    y_hi, x = h // 4, h % 4
    own = payload(latents, positions)
    gathered = lax.all_gather(own, "seq", axis=0, tiled=True)
    weight = out_weight.T
    behind1 = lax.ppermute(weight, "seq", along_z(1))
    ahead1 = lax.ppermute(weight, "seq", along_z(3))
    core_own = lax.ppermute(weight, "seq", CORE)

    q = jnp.pad(jnp.transpose(queries, (1, 0, 2)), ((0, 0), (0, 0), (0, 256 - qk)))
    upk = up_keys.reshape(LAT, heads * 128)
    upv = up_values.reshape(LAT, heads * 128)

    packed, key_inv, query_inv, total = prep(gathered, own, (q, upk, upv))
    scale = (qk ** -0.5) * 1.4426950408889634
    ahead1, behind1 = behind(ahead1, total, ()), behind(behind1, total, ())
    far0 = lax.ppermute(behind1[:224], "seq", along_z(1))
    far1 = lax.ppermute(ahead1[224:], "seq", along_z(3))
    core_ahead1, core_behind1 = lax.ppermute(ahead1, "seq", CORE), lax.ppermute(behind1, "seq", CORE)
    mine, theirs, first, after = [], [], 0, (core_own,)
    for i, width in enumerate(PARTS):
        part, total = attend(total, packed, key_inv, query_inv, q, upk, upv, scale, first, width, after)
        first += width
        mine.append(part)
        theirs.append(lax.ppermute(part, "seq", ALONG_Y))
        after = (core_ahead1, core_behind1)
        if i == 1:
            far0, far1 = behind(far0, total, theirs[:1]), behind(far1, total, theirs[:1])
            core_far0, core_far1 = lax.ppermute(far0, "seq", CORE), lax.ppermute(far1, "seq", CORE)
            after = (theirs[0],)
    weights = (weight, ahead1, far0, far1, behind1)
    swapped = (core_own, core_ahead1, core_far0, core_far1, core_behind1)

    direct, crossing = [], []
    for pair in ((2, 1), (3, 0)):
        sel = jnp.stack([(x + dx - z) % 4 for dx in pair] + [core, y_hi ^ y_lo]).astype(jnp.int32)
        chunks = project(sel, mine + theirs, weights, swapped)
        for t, dx in enumerate(pair):
            direct.append(lax.ppermute(chunks[2 * t], ("seq", "head"), to_owner(0, dx)))
            crossing.append(lax.ppermute(chunks[2 * t + 1], "head", along_x(dx)) if dx else chunks[2 * t + 1])
    crossed = lax.ppermute(total_of(crossing, direct[:2]), ("seq", "head"), to_owner(1, 0))
    projected = sum(r.astype(F32) for r in direct) + crossed.astype(F32)
    live_rows = (positions < SEQ_LEN).astype(F32)
    gated = (live_rows * router_gate)[:, None] * projected
    return (residual.astype(F32) + gated).astype(BF)


def solution(mesh):
    return jax.shard_map(
        per_device,
        mesh=mesh,
        in_specs=(
            P("seq", "head", None),
            P("seq", None),
            P("seq"),
            P(None, "head", None),
            P(None, "head", None),
            P("head", "seq"),
            P("seq", "head"),
            P("seq"),
        ),
        out_specs=P("seq", "head"),
        check_vma=False,
    )
```

```python
import functools
import jax
import jax.numpy as jnp
from jax import lax
from jax.experimental import pallas as pl
from jax.experimental.pallas import tpu as pltpu
from jax.sharding import PartitionSpec as P

SEQ_LEN = 131072
BF = jnp.bfloat16
F32 = jnp.float32
CAP = 192
SHARDS = 16
TOT = CAP * SHARDS
LAT = 512
WIDE = 640
MIB = 1024 * 1024
VARIANTS = (1024, 1280, 1536, TOT)
PARTS = (8, 6, 2)


def payload_kernel(lat_ref, pos_ref, out_ref):
    row = lax.broadcasted_iota(jnp.int32, (CAP, CAP), 0)
    col = lax.broadcasted_iota(jnp.int32, (CAP, CAP), 1)
    inv = jnp.sum(jnp.where(row == col, (SEQ_LEN - pos_ref[...]).astype(F32), 0.0), axis=1, keepdims=True)
    inv = inv.astype(jnp.int32)
    lane = lax.broadcasted_iota(jnp.int32, (CAP, 64), 1)
    digits = jnp.where(lane == 0, inv & 63, jnp.where(lane == 1, (inv >> 6) & 63, jnp.where(
        lane == 2, inv >> 12, jnp.where((lane == 3) & (inv > 0), 1, 0))))
    out_ref[...] = jnp.concatenate([lat_ref[...], digits.astype(F32).astype(BF)], axis=1)


def payload(latents, positions):
    return pl.pallas_call(
        payload_kernel,
        out_shape=jax.ShapeDtypeStruct((CAP, WIDE), BF),
        in_specs=[pl.BlockSpec(memory_space=pltpu.VMEM)] * 2,
        out_specs=pl.BlockSpec(memory_space=pltpu.VMEM),
        compiler_params=pltpu.CompilerParams(vmem_limit_bytes=4 * MIB),
        name="latents_and_positions",
    )(latents, positions.reshape(1, CAP))


def prep_kernel(all_ref, own_ref, *refs):
    out_ref, key_ref, query_ref, total_ref, packed_ref, sem = refs[-6:]
    packed_ref[...] = jnp.zeros_like(packed_ref)
    lane = lax.broadcasted_iota(jnp.int32, (CAP, 128), 1)
    counts = []
    for s in range(SHARDS):
        tail = all_ref[s * CAP:(s + 1) * CAP, LAT:WIDE].astype(F32)
        counts.append(jnp.sum(jnp.where(lane == 67, tail, 0.0)).astype(jnp.int32))
    diff = (lax.broadcasted_iota(jnp.int32, (CAP + 16, CAP), 0)
            - lax.broadcasted_iota(jnp.int32, (CAP + 16, CAP), 1))
    col = lax.broadcasted_iota(jnp.int32, (CAP + 16, CAP), 1)
    offset = jnp.int32(0)
    for s in range(SHARDS):
        first = pl.multiple_of((offset // 16) * 16, 16)
        shift = offset - first
        pick = jnp.where((diff == shift) & (col < counts[s]), 1.0, 0.0).astype(BF)
        moved = jnp.dot(pick, all_ref[s * CAP:(s + 1) * CAP, :],
                        preferred_element_type=F32).astype(BF)
        packed_ref[pl.ds(first, 16), :] = packed_ref[pl.ds(first, 16), :] + moved[:16]
        packed_ref[pl.ds(pl.multiple_of(first + 16, 16), CAP), :] = moved[16:]
        offset = offset + counts[s]
    total_ref[0] = offset
    lane8 = lax.broadcasted_iota(jnp.int32, (8, 128), 1)
    coef = jnp.where(lane8 == 64, 1.0, jnp.where(lane8 == 65, 64.0, jnp.where(lane8 == 66, 4096.0, 0.0)))
    key_ref[...] = lax.dot_general(coef.astype(BF), packed_ref[0:TOT, LAT:WIDE],
                                   (((1,), (1,)), ((), ())), preferred_element_type=F32)
    own = own_ref[:, LAT:WIDE].astype(F32)
    query_ref[...] = jnp.broadcast_to(jnp.sum(own * coef[0:1, :], axis=1, keepdims=True), query_ref.shape)
    low = 0
    for width in VARIANTS:
        @pl.when((offset > low) & (offset <= width))
        def _():
            copy = pltpu.make_async_copy(packed_ref.at[pl.ds(0, width)], out_ref.at[pl.ds(0, width)], sem)
            copy.start()
            copy.wait()
        low = width


def prep(gathered, own, after):
    return pl.pallas_call(
        prep_kernel,
        out_shape=(jax.ShapeDtypeStruct((TOT, WIDE), BF),
                   jax.ShapeDtypeStruct((8, TOT), F32),
                   jax.ShapeDtypeStruct((CAP, 128), F32),
                   jax.ShapeDtypeStruct((1,), jnp.int32)),
        in_specs=[pl.BlockSpec(memory_space=pltpu.VMEM)] * 2 + [pl.BlockSpec(memory_space=pltpu.HBM)] * len(after),
        out_specs=(pl.BlockSpec(memory_space=pltpu.HBM), pl.BlockSpec(memory_space=pltpu.VMEM),
                   pl.BlockSpec(memory_space=pltpu.VMEM), pl.BlockSpec(memory_space=pltpu.SMEM)),
        scratch_shapes=[pltpu.VMEM((TOT + 16, WIDE), BF), pltpu.SemaphoreType.DMA],
        compiler_params=pltpu.CompilerParams(vmem_limit_bytes=50 * MIB),
        name="pack_live_rows",
    )(gathered, own, *after)


def attend_kernel(scale, total_ref, source_ref, key_ref, query_ref, q_ref, upk_ref, upv_ref, *rest):
    out_ref, next_ref, k_ref, v_ref, packed_ref, bias_ref, sem = rest[-7:]

    def variant(width):
        @pl.when(pl.program_id(0) == 0)
        def _():
            copy = pltpu.make_async_copy(source_ref.at[pl.ds(0, width)], packed_ref.at[pl.ds(0, width)], sem)
            copy.start()
            bias_ref[:, :width] = jnp.where(key_ref[0:1, :width] >= query_ref[:, 0:1], 0.0, -1e30)
            copy.wait()

        for r in range(0, width, 256):
            x = packed_ref[r:r + 256, :LAT]
            k_ref[r:r + 256, :] = jnp.dot(x, upk_ref[...], preferred_element_type=F32).astype(BF)
            v_ref[r:r + 256, :] = jnp.dot(x, upv_ref[...], preferred_element_type=F32).astype(BF)
        for j in range(2):
            keys = jnp.concatenate(
                [k_ref[:width, j * 128:(j + 1) * 128], packed_ref[:width, LAT:WIDE]], axis=1)
            scores = lax.dot_general(q_ref[j], keys, (((1,), (1,)), ((), ())),
                                     preferred_element_type=F32)
            scores = scores * scale + bias_ref[:, :width]
            row_max = jnp.max(scores, axis=1, keepdims=True)
            weights = jnp.exp2(scores - row_max)
            total = jnp.sum(weights, axis=1, keepdims=True)
            summed = jnp.dot(weights.astype(BF), v_ref[:width, j * 128:(j + 1) * 128],
                             preferred_element_type=F32)
            out_ref[:, j * 128:(j + 1) * 128] = (summed / total).astype(BF)

    n = total_ref[0]
    next_ref[0] = n
    low = 0
    for width in VARIANTS:
        pl.when((n > low) & (n <= width))(functools.partial(variant, width))
        low = width


def attend(total, packed, keys, queries, q, upk, upv, scale, first, heads, after):
    pairs, start = heads // 2, first // 2
    return pl.pallas_call(
        functools.partial(attend_kernel, scale),
        grid=(pairs,),
        out_shape=(jax.ShapeDtypeStruct((CAP, pairs * 256), BF), jax.ShapeDtypeStruct((1,), jnp.int32)),
        in_specs=[
            pl.BlockSpec(memory_space=pltpu.SMEM),
            pl.BlockSpec(memory_space=pltpu.HBM),
            pl.BlockSpec(memory_space=pltpu.VMEM),
            pl.BlockSpec(memory_space=pltpu.VMEM),
            pl.BlockSpec((2, CAP, 256), lambda i: (start + i, 0, 0)),
            pl.BlockSpec((LAT, 256), lambda i: (0, start + i)),
            pl.BlockSpec((LAT, 256), lambda i: (0, start + i)),
        ] + [pl.BlockSpec(memory_space=pltpu.HBM)] * len(after),
        out_specs=(pl.BlockSpec((CAP, 256), lambda i: (0, i)), pl.BlockSpec(memory_space=pltpu.SMEM)),
        scratch_shapes=[pltpu.VMEM((TOT, 256), BF), pltpu.VMEM((TOT, 256), BF), pltpu.VMEM((TOT, WIDE), BF),
                        pltpu.VMEM((CAP, TOT), F32), pltpu.SemaphoreType.DMA],
        cost_estimate=pl.CostEstimate(flops=pairs * 10 ** 8, bytes_accessed=0, transcendentals=0),
        compiler_params=pltpu.CompilerParams(vmem_limit_bytes=50 * MIB),
        name="attend_heads",
    )(total, packed, keys, queries, q, upk, upv, *after)


def project_kernel(blocks, sel_ref, *refs):
    n = len(PARTS)
    rows, weights = refs[:2 * n], refs[2 * n:2 * n + 5]
    swapped = refs[2 * n + 5:2 * n + 10]
    outs = refs[-4 - 2 * blocks:-4]
    a_ref, w_ref, sem_a, sem_w = refs[-4:]
    core, slot = sel_ref[blocks], sel_ref[blocks + 1]
    waits = []
    for p in range(2):
        first = 0
        for i, width in enumerate(PARTS):
            copy = pltpu.make_async_copy(rows[n * p + i], a_ref.at[slot ^ p, :, pl.ds(first * 128, width * 128)],
                                         sem_a.at[n * p + i])
            copy.start()
            waits.append(copy)
            first += width
    for t in range(blocks):
        for k, pieces in enumerate((((0, 0),), ((1, 0),), ((2, 0), (3, 224)), ((4, 0),))):
            for cc in range(2):
                @pl.when((sel_ref[t] == k) & (core == cc))
                def _():
                    for j, source in enumerate((weights, swapped)):
                        for index, start in pieces:
                            src = source[index]
                            pltpu.make_async_copy(
                                src, w_ref.at[t, pl.ds((j ^ cc) * 448 + start, src.shape[0])], sem_w.at[t]).start()
    for copy in waits:
        copy.wait()
    for t in range(blocks):
        pltpu.make_async_copy(w_ref.at[t], w_ref.at[t], sem_w.at[t]).wait()
        whole = lax.dot_general(a_ref[...].reshape(2 * CAP, 2048), w_ref[t], (((1,), (1,)), ((), ())),
                                preferred_element_type=F32)
        for r in range(2):
            outs[2 * t + r][...] = whole[r * CAP:(r + 1) * CAP].astype(BF)


def project(sel, rows, weights, swapped, blocks, after):
    operands = (*rows, *weights, *swapped, *after)
    return pl.pallas_call(
        functools.partial(project_kernel, blocks),
        out_shape=(jax.ShapeDtypeStruct((CAP, 896), BF),) * (2 * blocks),
        in_specs=[pl.BlockSpec(memory_space=pltpu.SMEM)] + [pl.BlockSpec(memory_space=pltpu.HBM)] * len(operands),
        out_specs=(pl.BlockSpec(memory_space=pltpu.VMEM),) * (2 * blocks),
        scratch_shapes=[pltpu.VMEM((2, CAP, 2048), BF), pltpu.VMEM((blocks, 896, 2048), BF),
                        pltpu.SemaphoreType.DMA((len(rows),)), pltpu.SemaphoreType.DMA((2,))],
        cost_estimate=pl.CostEstimate(flops=10 ** 8, bytes_accessed=0, transcendentals=0),
        compiler_params=pltpu.CompilerParams(vmem_limit_bytes=58 * MIB),
        name="project_chunks",
    )(sel, *operands)


def behind(x, other, more):
    return pl.pallas_call(
        lambda *refs: None,
        out_shape=jax.ShapeDtypeStruct(x.shape, x.dtype),
        in_specs=[pl.BlockSpec(memory_space=pltpu.HBM), pl.BlockSpec(memory_space=pltpu.SMEM)]
        + [pl.BlockSpec(memory_space=pltpu.HBM)] * len(more),
        out_specs=pl.BlockSpec(memory_space=pltpu.HBM),
        input_output_aliases={0: 0},
        cost_estimate=pl.CostEstimate(flops=0, bytes_accessed=0, transcendentals=0),
        compiler_params=pltpu.CompilerParams(vmem_limit_bytes=MIB),
        name="behind",
    )(x, other, *more)


def forward_kernel(ahead_ref, behind_ref, after_ref, ahead_out, behind_out, first_ref, second_ref, sems):
    copies = [pltpu.make_async_copy(behind_ref.at[pl.ds(0, 224)], first_ref, sems.at[0]),
              pltpu.make_async_copy(ahead_ref.at[pl.ds(224, 224)], second_ref, sems.at[1])]
    for copy in copies:
        copy.start()
    for copy in copies:
        copy.wait()


def forward(ahead, back, after):
    return pl.pallas_call(
        forward_kernel,
        out_shape=(jax.ShapeDtypeStruct(ahead.shape, BF),) * 2 + (jax.ShapeDtypeStruct((224, 2048), BF),) * 2,
        in_specs=[pl.BlockSpec(memory_space=pltpu.HBM)] * 2 + [pl.BlockSpec(memory_space=pltpu.SMEM)],
        out_specs=(pl.BlockSpec(memory_space=pltpu.HBM),) * 4,
        input_output_aliases={0: 0, 1: 1},
        scratch_shapes=[pltpu.SemaphoreType.DMA((2,))],
        cost_estimate=pl.CostEstimate(flops=0, bytes_accessed=0, transcendentals=0),
        compiler_params=pltpu.CompilerParams(vmem_limit_bytes=MIB),
        name="forward_halves",
    )(ahead, back, after)


def total_kernel(*refs):
    total = refs[0][...].astype(F32)
    for ref in refs[1:4]:
        total = total + ref[...].astype(F32)
    refs[-1][...] = total.astype(BF)


def total_of(chunks, after):
    return pl.pallas_call(
        total_kernel,
        out_shape=jax.ShapeDtypeStruct(chunks[0].shape, BF),
        in_specs=[pl.BlockSpec(memory_space=pltpu.VMEM)] * 4 + [pl.BlockSpec(memory_space=pltpu.HBM)] * len(after),
        out_specs=pl.BlockSpec(memory_space=pltpu.VMEM),
        compiler_params=pltpu.CompilerParams(vmem_limit_bytes=8 * MIB),
        name="sum_over_x",
    )(*chunks, *after)


CORE = [(s, s ^ 1) for s in range(16)]
ALONG_Y = [(s, s ^ 8) for s in range(16)]


def along_z(k):
    return [(s, (s // 8) * 8 + ((s // 2 + k) % 4) * 2 + s % 2) for s in range(16)]


def along_x(k):
    return [(h, (h // 4) * 4 + (h + k) % 4) for h in range(8)]


def to_owner(r, dx):
    pairs = []
    for s in range(16):
        for h in range(8):
            y_lo, y_hi, x = s // 8, h // 4, h % 4
            pairs.append((s * 8 + h, ((y_hi ^ r) * 8 + s % 8) * 8 + y_lo * 4 + (x + dx) % 4))
    return pairs


def per_device(queries, latents, positions, up_keys, up_values, out_weight, residual, router_gate):
    heads, qk = queries.shape[1], queries.shape[2]
    s, h = lax.axis_index("seq"), lax.axis_index("head")
    y_lo, z, core = s // 8, (s // 2) % 4, s % 2
    y_hi, x = h // 4, h % 4
    own = payload(latents, positions)
    gathered = lax.all_gather(own, "seq", axis=0, tiled=True)
    weight = out_weight.T
    behind1 = lax.ppermute(weight, "seq", along_z(1))
    ahead1 = lax.ppermute(weight, "seq", along_z(3))
    core_own = lax.ppermute(weight, "seq", CORE)

    q = jnp.pad(jnp.transpose(queries, (1, 0, 2)), ((0, 0), (0, 0), (0, 256 - qk)))
    upk = up_keys.reshape(LAT, heads * 128)
    upv = up_values.reshape(LAT, heads * 128)

    packed, key_inv, query_inv, total = prep(gathered, own, (q, upk, upv))
    scale = (qk ** -0.5) * 1.4426950408889634
    ahead1, behind1, first_half, second_half = forward(ahead1, behind1, total)
    far0 = lax.ppermute(first_half, "seq", along_z(1))
    far1 = lax.ppermute(second_half, "seq", along_z(3))
    core_ahead1, core_behind1 = lax.ppermute(ahead1, "seq", CORE), lax.ppermute(behind1, "seq", CORE)
    mine, theirs, first, after = [], [], 0, (core_own,)
    for i, width in enumerate(PARTS):
        part, total = attend(total, packed, key_inv, query_inv, q, upk, upv, scale, first, width, after)
        first += width
        mine.append(part)
        theirs.append(lax.ppermute(part, "seq", ALONG_Y))
        after = (core_ahead1, core_behind1)
        if i == 1:
            far0, far1 = behind(far0, total, theirs[:1]), behind(far1, total, theirs[:1])
            core_far0, core_far1 = lax.ppermute(far0, "seq", CORE), lax.ppermute(far1, "seq", CORE)
            after = (theirs[0],)
    weights = (weight, ahead1, far0, far1, behind1)
    swapped = (core_own, core_ahead1, core_far0, core_far1, core_behind1)

    direct, crossing = [], []
    for pair in ((2, 1), (3,), (0,)):
        sel = jnp.stack([(x + dx - z) % 4 for dx in pair] + [core, y_hi ^ y_lo]).astype(jnp.int32)
        chunks = project(sel, mine + theirs, weights, swapped, len(pair), direct[:2] if pair == (0,) else ())
        for t, dx in enumerate(pair):
            direct.append(lax.ppermute(chunks[2 * t], ("seq", "head"), to_owner(0, dx)))
            crossing.append(lax.ppermute(chunks[2 * t + 1], "head", along_x(dx)) if dx else chunks[2 * t + 1])
    crossed = lax.ppermute(total_of(crossing, direct[:2]), ("seq", "head"), to_owner(1, 0))
    projected = sum(r.astype(F32) for r in direct) + crossed.astype(F32)
    live_rows = (positions < SEQ_LEN).astype(F32)
    gated = (live_rows * router_gate)[:, None] * projected
    return (residual.astype(F32) + gated).astype(BF)


def solution(mesh):
    return jax.shard_map(
        per_device,
        mesh=mesh,
        in_specs=(
            P("seq", "head", None),
            P("seq", None),
            P("seq"),
            P(None, "head", None),
            P(None, "head", None),
            P("head", "seq"),
            P("seq", "head"),
            P("seq"),
        ),
        out_specs=P("seq", "head"),
        check_vma=False,
    )
```

```python
import functools
import jax
import jax.numpy as jnp
from jax import lax
from jax.experimental import pallas as pl
from jax.experimental.pallas import tpu as pltpu
from jax.sharding import PartitionSpec as P

SEQ_LEN = 131072
BF = jnp.bfloat16
F32 = jnp.float32
CAP = 192
SHARDS = 16
TOT = CAP * SHARDS
LAT = 512
WIDE = 640
MIB = 1024 * 1024
VARIANTS = (1024, 1280, 1536, TOT)
PARTS = (8, 6, 2)


def payload_kernel(lat_ref, pos_ref, out_ref):
    row = lax.broadcasted_iota(jnp.int32, (CAP, CAP), 0)
    col = lax.broadcasted_iota(jnp.int32, (CAP, CAP), 1)
    inv = jnp.sum(jnp.where(row == col, (SEQ_LEN - pos_ref[...]).astype(F32), 0.0), axis=1, keepdims=True)
    inv = inv.astype(jnp.int32)
    lane = lax.broadcasted_iota(jnp.int32, (CAP, 64), 1)
    digits = jnp.where(lane == 0, inv & 63, jnp.where(lane == 1, (inv >> 6) & 63, jnp.where(
        lane == 2, inv >> 12, jnp.where((lane == 3) & (inv > 0), 1, 0))))
    out_ref[...] = jnp.concatenate([lat_ref[...], digits.astype(F32).astype(BF)], axis=1)


def payload(latents, positions):
    return pl.pallas_call(
        payload_kernel,
        out_shape=jax.ShapeDtypeStruct((CAP, WIDE), BF),
        in_specs=[pl.BlockSpec(memory_space=pltpu.VMEM)] * 2,
        out_specs=pl.BlockSpec(memory_space=pltpu.VMEM),
        compiler_params=pltpu.CompilerParams(vmem_limit_bytes=4 * MIB),
        name="latents_and_positions",
    )(latents, positions.reshape(1, CAP))


def prep_kernel(all_ref, own_ref, *refs):
    out_ref, key_ref, query_ref, total_ref, packed_ref, sem = refs[-6:]
    packed_ref[...] = jnp.zeros_like(packed_ref)
    lane = lax.broadcasted_iota(jnp.int32, (CAP, 128), 1)
    counts = []
    for s in range(SHARDS):
        tail = all_ref[s * CAP:(s + 1) * CAP, LAT:WIDE].astype(F32)
        counts.append(jnp.sum(jnp.where(lane == 67, tail, 0.0)).astype(jnp.int32))
    diff = (lax.broadcasted_iota(jnp.int32, (CAP + 16, CAP), 0)
            - lax.broadcasted_iota(jnp.int32, (CAP + 16, CAP), 1))
    col = lax.broadcasted_iota(jnp.int32, (CAP + 16, CAP), 1)
    offset = jnp.int32(0)
    for s in range(SHARDS):
        first = pl.multiple_of((offset // 16) * 16, 16)
        shift = offset - first
        pick = jnp.where((diff == shift) & (col < counts[s]), 1.0, 0.0).astype(BF)
        moved = jnp.dot(pick, all_ref[s * CAP:(s + 1) * CAP, :],
                        preferred_element_type=F32).astype(BF)
        packed_ref[pl.ds(first, 16), :] = packed_ref[pl.ds(first, 16), :] + moved[:16]
        packed_ref[pl.ds(pl.multiple_of(first + 16, 16), CAP), :] = moved[16:]
        offset = offset + counts[s]
    total_ref[0] = offset
    lane8 = lax.broadcasted_iota(jnp.int32, (8, 128), 1)
    coef = jnp.where(lane8 == 64, 1.0, jnp.where(lane8 == 65, 64.0, jnp.where(lane8 == 66, 4096.0, 0.0)))
    key_ref[...] = lax.dot_general(coef.astype(BF), packed_ref[0:TOT, LAT:WIDE],
                                   (((1,), (1,)), ((), ())), preferred_element_type=F32)
    own = own_ref[:, LAT:WIDE].astype(F32)
    query_ref[...] = jnp.broadcast_to(jnp.sum(own * coef[0:1, :], axis=1, keepdims=True), query_ref.shape)
    low = 0
    for width in VARIANTS:
        @pl.when((offset > low) & (offset <= width))
        def _():
            copy = pltpu.make_async_copy(packed_ref.at[pl.ds(0, width)], out_ref.at[pl.ds(0, width)], sem)
            copy.start()
            copy.wait()
        low = width


def prep(gathered, own, after):
    return pl.pallas_call(
        prep_kernel,
        out_shape=(jax.ShapeDtypeStruct((TOT, WIDE), BF),
                   jax.ShapeDtypeStruct((8, TOT), F32),
                   jax.ShapeDtypeStruct((CAP, 128), F32),
                   jax.ShapeDtypeStruct((1,), jnp.int32)),
        in_specs=[pl.BlockSpec(memory_space=pltpu.VMEM)] * 2 + [pl.BlockSpec(memory_space=pltpu.HBM)] * len(after),
        out_specs=(pl.BlockSpec(memory_space=pltpu.HBM), pl.BlockSpec(memory_space=pltpu.VMEM),
                   pl.BlockSpec(memory_space=pltpu.VMEM), pl.BlockSpec(memory_space=pltpu.SMEM)),
        scratch_shapes=[pltpu.VMEM((TOT + 16, WIDE), BF), pltpu.SemaphoreType.DMA],
        compiler_params=pltpu.CompilerParams(vmem_limit_bytes=50 * MIB),
        name="pack_live_rows",
    )(gathered, own, *after)


def attend_kernel(scale, total_ref, source_ref, key_ref, query_ref, q_ref, upk_ref, upv_ref, *rest):
    out_ref, next_ref, k_ref, v_ref, packed_ref, bias_ref, sem = rest[-7:]

    def variant(width):
        @pl.when(pl.program_id(0) == 0)
        def _():
            copy = pltpu.make_async_copy(source_ref.at[pl.ds(0, width)], packed_ref.at[pl.ds(0, width)], sem)
            copy.start()
            bias_ref[:, :width] = jnp.where(key_ref[0:1, :width] >= query_ref[:, 0:1], 0.0, -1e30)
            copy.wait()

        for r in range(0, width, 256):
            x = packed_ref[r:r + 256, :LAT]
            k_ref[r:r + 256, :] = jnp.dot(x, upk_ref[...], preferred_element_type=F32).astype(BF)
            v_ref[r:r + 256, :] = jnp.dot(x, upv_ref[...], preferred_element_type=F32).astype(BF)
        for j in range(2):
            keys = jnp.concatenate(
                [k_ref[:width, j * 128:(j + 1) * 128], packed_ref[:width, LAT:WIDE]], axis=1)
            scores = lax.dot_general(q_ref[j], keys, (((1,), (1,)), ((), ())),
                                     preferred_element_type=F32)
            scores = scores * scale + bias_ref[:, :width]
            row_max = jnp.max(scores, axis=1, keepdims=True)
            weights = jnp.exp2(scores - row_max)
            total = jnp.sum(weights, axis=1, keepdims=True)
            summed = jnp.dot(weights.astype(BF), v_ref[:width, j * 128:(j + 1) * 128],
                             preferred_element_type=F32)
            out_ref[:, j * 128:(j + 1) * 128] = (summed / total).astype(BF)

    n = total_ref[0]
    next_ref[0] = n
    low = 0
    for width in VARIANTS:
        pl.when((n > low) & (n <= width))(functools.partial(variant, width))
        low = width


def attend(total, packed, keys, queries, q, upk, upv, scale, first, heads, after):
    pairs, start = heads // 2, first // 2
    return pl.pallas_call(
        functools.partial(attend_kernel, scale),
        grid=(pairs,),
        out_shape=(jax.ShapeDtypeStruct((CAP, pairs * 256), BF), jax.ShapeDtypeStruct((1,), jnp.int32)),
        in_specs=[
            pl.BlockSpec(memory_space=pltpu.SMEM),
            pl.BlockSpec(memory_space=pltpu.HBM),
            pl.BlockSpec(memory_space=pltpu.VMEM),
            pl.BlockSpec(memory_space=pltpu.VMEM),
            pl.BlockSpec((2, CAP, 256), lambda i: (start + i, 0, 0)),
            pl.BlockSpec((LAT, 256), lambda i: (0, start + i)),
            pl.BlockSpec((LAT, 256), lambda i: (0, start + i)),
        ] + [pl.BlockSpec(memory_space=pltpu.HBM)] * len(after),
        out_specs=(pl.BlockSpec((CAP, 256), lambda i: (0, i)), pl.BlockSpec(memory_space=pltpu.SMEM)),
        scratch_shapes=[pltpu.VMEM((TOT, 256), BF), pltpu.VMEM((TOT, 256), BF), pltpu.VMEM((TOT, WIDE), BF),
                        pltpu.VMEM((CAP, TOT), F32), pltpu.SemaphoreType.DMA],
        cost_estimate=pl.CostEstimate(flops=pairs * 10 ** 8, bytes_accessed=0, transcendentals=0),
        compiler_params=pltpu.CompilerParams(vmem_limit_bytes=50 * MIB),
        name="attend_heads",
    )(total, packed, keys, queries, q, upk, upv, *after)


def project_kernel(blocks, sel_ref, *refs):
    n = len(PARTS)
    rows, weights = refs[:2 * n], refs[2 * n:2 * n + 5]
    swapped = refs[2 * n + 5:2 * n + 10]
    outs = refs[-4 - 2 * blocks:-4]
    a_ref, w_ref, sem_a, sem_w = refs[-4:]
    core, slot = sel_ref[blocks], sel_ref[blocks + 1]
    waits = []
    for p in range(2):
        first = 0
        for i, width in enumerate(PARTS):
            copy = pltpu.make_async_copy(rows[n * p + i], a_ref.at[slot ^ p, :, pl.ds(first * 128, width * 128)],
                                         sem_a.at[n * p + i])
            copy.start()
            waits.append(copy)
            first += width
    for t in range(blocks):
        for k, pieces in enumerate((((0, 0),), ((1, 0),), ((2, 0), (3, 224)), ((4, 0),))):
            for cc in range(2):
                @pl.when((sel_ref[t] == k) & (core == cc))
                def _():
                    for j, source in enumerate((weights, swapped)):
                        for index, start in pieces:
                            src = source[index]
                            pltpu.make_async_copy(
                                src, w_ref.at[t, pl.ds((j ^ cc) * 448 + start, src.shape[0])], sem_w.at[t]).start()
    for copy in waits:
        copy.wait()
    for t in range(blocks):
        pltpu.make_async_copy(w_ref.at[t], w_ref.at[t], sem_w.at[t]).wait()
        whole = lax.dot_general(a_ref[...].reshape(2 * CAP, 2048), w_ref[t], (((1,), (1,)), ((), ())),
                                preferred_element_type=F32)
        for r in range(2):
            outs[2 * t + r][...] = whole[r * CAP:(r + 1) * CAP].astype(BF)


def project(sel, rows, weights, swapped, blocks, after):
    operands = (*rows, *weights, *swapped, *after)
    return pl.pallas_call(
        functools.partial(project_kernel, blocks),
        out_shape=(jax.ShapeDtypeStruct((CAP, 896), BF),) * (2 * blocks),
        in_specs=[pl.BlockSpec(memory_space=pltpu.SMEM)] + [pl.BlockSpec(memory_space=pltpu.HBM)] * len(operands),
        out_specs=(pl.BlockSpec(memory_space=pltpu.VMEM),) * (2 * blocks),
        scratch_shapes=[pltpu.VMEM((2, CAP, 2048), BF), pltpu.VMEM((blocks, 896, 2048), BF),
                        pltpu.SemaphoreType.DMA((len(rows),)), pltpu.SemaphoreType.DMA((2,))],
        cost_estimate=pl.CostEstimate(flops=10 ** 8, bytes_accessed=0, transcendentals=0),
        compiler_params=pltpu.CompilerParams(vmem_limit_bytes=58 * MIB),
        name="project_chunks",
    )(sel, *operands)


def behind(x, other, more):
    return pl.pallas_call(
        lambda *refs: None,
        out_shape=jax.ShapeDtypeStruct(x.shape, x.dtype),
        in_specs=[pl.BlockSpec(memory_space=pltpu.HBM), pl.BlockSpec(memory_space=pltpu.SMEM)]
        + [pl.BlockSpec(memory_space=pltpu.HBM)] * len(more),
        out_specs=pl.BlockSpec(memory_space=pltpu.HBM),
        input_output_aliases={0: 0},
        cost_estimate=pl.CostEstimate(flops=0, bytes_accessed=0, transcendentals=0),
        compiler_params=pltpu.CompilerParams(vmem_limit_bytes=MIB),
        name="behind",
    )(x, other, *more)


def forward_kernel(ahead_ref, behind_ref, after_ref, ahead_out, behind_out, first_ref, second_ref, sems):
    copies = [pltpu.make_async_copy(behind_ref.at[pl.ds(0, 224)], first_ref, sems.at[0]),
              pltpu.make_async_copy(ahead_ref.at[pl.ds(224, 224)], second_ref, sems.at[1])]
    for copy in copies:
        copy.start()
    for copy in copies:
        copy.wait()


def forward(ahead, back, after):
    return pl.pallas_call(
        forward_kernel,
        out_shape=(jax.ShapeDtypeStruct(ahead.shape, BF),) * 2 + (jax.ShapeDtypeStruct((224, 2048), BF),) * 2,
        in_specs=[pl.BlockSpec(memory_space=pltpu.HBM)] * 2 + [pl.BlockSpec(memory_space=pltpu.SMEM)],
        out_specs=(pl.BlockSpec(memory_space=pltpu.HBM),) * 4,
        input_output_aliases={0: 0, 1: 1},
        scratch_shapes=[pltpu.SemaphoreType.DMA((2,))],
        cost_estimate=pl.CostEstimate(flops=0, bytes_accessed=0, transcendentals=0),
        compiler_params=pltpu.CompilerParams(vmem_limit_bytes=MIB),
        name="forward_halves",
    )(ahead, back, after)


CORE = [(s, s ^ 1) for s in range(16)]
ALONG_Y = [(s, s ^ 8) for s in range(16)]


def along_z(k):
    return [(s, (s // 8) * 8 + ((s // 2 + k) % 4) * 2 + s % 2) for s in range(16)]


def along_x(k):
    return [(h, (h // 4) * 4 + (h + k) % 4) for h in range(8)]


def to_owner(r, dx):
    pairs = []
    for s in range(16):
        for h in range(8):
            y_lo, y_hi, x = s // 8, h // 4, h % 4
            pairs.append((s * 8 + h, ((y_hi ^ r) * 8 + s % 8) * 8 + y_lo * 4 + (x + dx) % 4))
    return pairs


def per_device(queries, latents, positions, up_keys, up_values, out_weight, residual, router_gate):
    heads, qk = queries.shape[1], queries.shape[2]
    s, h = lax.axis_index("seq"), lax.axis_index("head")
    y_lo, z, core = s // 8, (s // 2) % 4, s % 2
    y_hi, x = h // 4, h % 4
    own = payload(latents, positions)
    gathered = lax.all_gather(own, "seq", axis=0, tiled=True)
    weight = out_weight.T
    behind1 = lax.ppermute(weight, "seq", along_z(1))
    ahead1 = lax.ppermute(weight, "seq", along_z(3))
    core_own = lax.ppermute(weight, "seq", CORE)

    q = jnp.pad(jnp.transpose(queries, (1, 0, 2)), ((0, 0), (0, 0), (0, 256 - qk)))
    upk = up_keys.reshape(LAT, heads * 128)
    upv = up_values.reshape(LAT, heads * 128)

    packed, key_inv, query_inv, total = prep(gathered, own, (q, upk, upv))
    scale = (qk ** -0.5) * 1.4426950408889634
    ahead1, behind1, first_half, second_half = forward(ahead1, behind1, total)
    far0 = lax.ppermute(first_half, "seq", along_z(1))
    far1 = lax.ppermute(second_half, "seq", along_z(3))
    core_ahead1, core_behind1 = lax.ppermute(ahead1, "seq", CORE), lax.ppermute(behind1, "seq", CORE)
    mine, theirs, first, after = [], [], 0, (core_own,)
    for i, width in enumerate(PARTS):
        part, total = attend(total, packed, key_inv, query_inv, q, upk, upv, scale, first, width, after)
        first += width
        mine.append(part)
        theirs.append(lax.ppermute(part, "seq", ALONG_Y))
        after = (core_ahead1, core_behind1)
        if i == 1:
            far0, far1 = behind(far0, total, theirs[:1]), behind(far1, total, theirs[:1])
            core_far0, core_far1 = lax.ppermute(far0, "seq", CORE), lax.ppermute(far1, "seq", CORE)
            after = (theirs[0],)
    weights = (weight, ahead1, far0, far1, behind1)
    swapped = (core_own, core_ahead1, core_far0, core_far1, core_behind1)

    direct, crossing = [], []
    for pair in ((2, 1), (3,), (0,)):
        sel = jnp.stack([(x + dx - z) % 4 for dx in pair] + [core, y_hi ^ y_lo]).astype(jnp.int32)
        chunks = project(sel, mine + theirs, weights, swapped, len(pair), direct[:1] + crossing[:2] if pair == (0,) else [])
        for t, dx in enumerate(pair):
            direct.append(lax.ppermute(chunks[2 * t], ("seq", "head"), to_owner(0, dx)))
            crossing.append(lax.ppermute(chunks[2 * t + 1], "head", along_x(dx)) if dx else chunks[2 * t + 1])
    crossed = lax.ppermute(sum(c.astype(F32) for c in crossing).astype(BF), ("seq", "head"), to_owner(1, 0))
    projected = sum(r.astype(F32) for r in direct) + crossed.astype(F32)
    live_rows = (positions < SEQ_LEN).astype(F32)
    gated = (live_rows * router_gate)[:, None] * projected
    return (residual.astype(F32) + gated).astype(BF)


def solution(mesh):
    return jax.shard_map(
        per_device,
        mesh=mesh,
        in_specs=(
            P("seq", "head", None),
            P("seq", None),
            P("seq"),
            P(None, "head", None),
            P(None, "head", None),
            P("head", "seq"),
            P("seq", "head"),
            P("seq"),
        ),
        out_specs=P("seq", "head"),
        check_vma=False,
    )
```

```python
import functools
import jax
import jax.numpy as jnp
from jax import lax
from jax.experimental import pallas as pl
from jax.experimental.pallas import tpu as pltpu
from jax.sharding import PartitionSpec as P

SEQ_LEN = 131072
BF = jnp.bfloat16
F32 = jnp.float32
CAP = 192
SHARDS = 16
TOT = CAP * SHARDS
LAT = 512
WIDE = 640
MIB = 1024 * 1024
VARIANTS = (1024, 1280, 1536, TOT)
PARTS = (8, 6, 2)


def payload_kernel(lat_ref, pos_ref, out_ref):
    row = lax.broadcasted_iota(jnp.int32, (CAP, CAP), 0)
    col = lax.broadcasted_iota(jnp.int32, (CAP, CAP), 1)
    inv = jnp.sum(jnp.where(row == col, (SEQ_LEN - pos_ref[...]).astype(F32), 0.0), axis=1, keepdims=True)
    inv = inv.astype(jnp.int32)
    lane = lax.broadcasted_iota(jnp.int32, (CAP, 64), 1)
    digits = jnp.where(lane == 0, inv & 63, jnp.where(lane == 1, (inv >> 6) & 63, jnp.where(
        lane == 2, inv >> 12, jnp.where((lane == 3) & (inv > 0), 1, 0))))
    out_ref[...] = jnp.concatenate([lat_ref[...], digits.astype(F32).astype(BF)], axis=1)


def payload(latents, positions):
    return pl.pallas_call(
        payload_kernel,
        out_shape=jax.ShapeDtypeStruct((CAP, WIDE), BF),
        in_specs=[pl.BlockSpec(memory_space=pltpu.VMEM)] * 2,
        out_specs=pl.BlockSpec(memory_space=pltpu.VMEM),
        compiler_params=pltpu.CompilerParams(vmem_limit_bytes=4 * MIB),
        name="latents_and_positions",
    )(latents, positions.reshape(1, CAP))


def prep_kernel(all_ref, own_ref, *refs):
    out_ref, key_ref, query_ref, total_ref, packed_ref, sem = refs[-6:]
    packed_ref[...] = jnp.zeros_like(packed_ref)
    lane = lax.broadcasted_iota(jnp.int32, (CAP, 128), 1)
    counts = []
    for s in range(SHARDS):
        tail = all_ref[s * CAP:(s + 1) * CAP, LAT:WIDE].astype(F32)
        counts.append(jnp.sum(jnp.where(lane == 67, tail, 0.0)).astype(jnp.int32))
    diff = (lax.broadcasted_iota(jnp.int32, (CAP + 16, CAP), 0)
            - lax.broadcasted_iota(jnp.int32, (CAP + 16, CAP), 1))
    col = lax.broadcasted_iota(jnp.int32, (CAP + 16, CAP), 1)
    offset = jnp.int32(0)
    for s in range(SHARDS):
        first = pl.multiple_of((offset // 16) * 16, 16)
        shift = offset - first
        pick = jnp.where((diff == shift) & (col < counts[s]), 1.0, 0.0).astype(BF)
        moved = jnp.dot(pick, all_ref[s * CAP:(s + 1) * CAP, :],
                        preferred_element_type=F32).astype(BF)
        packed_ref[pl.ds(first, 16), :] = packed_ref[pl.ds(first, 16), :] + moved[:16]
        packed_ref[pl.ds(pl.multiple_of(first + 16, 16), CAP), :] = moved[16:]
        offset = offset + counts[s]
    total_ref[0] = offset
    lane8 = lax.broadcasted_iota(jnp.int32, (8, 128), 1)
    coef = jnp.where(lane8 == 64, 1.0, jnp.where(lane8 == 65, 64.0, jnp.where(lane8 == 66, 4096.0, 0.0)))
    key_ref[...] = lax.dot_general(coef.astype(BF), packed_ref[0:TOT, LAT:WIDE],
                                   (((1,), (1,)), ((), ())), preferred_element_type=F32)
    own = own_ref[:, LAT:WIDE].astype(F32)
    query_ref[...] = jnp.broadcast_to(jnp.sum(own * coef[0:1, :], axis=1, keepdims=True), query_ref.shape)
    low = 0
    for width in VARIANTS:
        @pl.when((offset > low) & (offset <= width))
        def _():
            copy = pltpu.make_async_copy(packed_ref.at[pl.ds(0, width)], out_ref.at[pl.ds(0, width)], sem)
            copy.start()
            copy.wait()
        low = width


def prep(gathered, own, after):
    return pl.pallas_call(
        prep_kernel,
        out_shape=(jax.ShapeDtypeStruct((TOT, WIDE), BF),
                   jax.ShapeDtypeStruct((8, TOT), F32),
                   jax.ShapeDtypeStruct((CAP, 128), F32),
                   jax.ShapeDtypeStruct((1,), jnp.int32)),
        in_specs=[pl.BlockSpec(memory_space=pltpu.VMEM)] * 2 + [pl.BlockSpec(memory_space=pltpu.HBM)] * len(after),
        out_specs=(pl.BlockSpec(memory_space=pltpu.HBM), pl.BlockSpec(memory_space=pltpu.VMEM),
                   pl.BlockSpec(memory_space=pltpu.VMEM), pl.BlockSpec(memory_space=pltpu.SMEM)),
        scratch_shapes=[pltpu.VMEM((TOT + 16, WIDE), BF), pltpu.SemaphoreType.DMA],
        compiler_params=pltpu.CompilerParams(vmem_limit_bytes=50 * MIB),
        name="pack_live_rows",
    )(gathered, own, *after)


def attend_kernel(scale, total_ref, source_ref, key_ref, query_ref, q_ref, upk_ref, upv_ref, *rest):
    out_ref, next_ref, k_ref, v_ref, packed_ref, bias_ref, sem = rest[-7:]

    def variant(width):
        @pl.when(pl.program_id(0) == 0)
        def _():
            copy = pltpu.make_async_copy(source_ref.at[pl.ds(0, width)], packed_ref.at[pl.ds(0, width)], sem)
            copy.start()
            bias_ref[:, :width] = jnp.where(key_ref[0:1, :width] >= query_ref[:, 0:1], 0.0, -1e30)
            copy.wait()

        for r in range(0, width, 256):
            x = packed_ref[r:r + 256, :LAT]
            k_ref[r:r + 256, :] = jnp.dot(x, upk_ref[...], preferred_element_type=F32).astype(BF)
            v_ref[r:r + 256, :] = jnp.dot(x, upv_ref[...], preferred_element_type=F32).astype(BF)
        for j in range(2):
            keys = jnp.concatenate(
                [k_ref[:width, j * 128:(j + 1) * 128], packed_ref[:width, LAT:WIDE]], axis=1)
            scores = lax.dot_general(q_ref[j], keys, (((1,), (1,)), ((), ())),
                                     preferred_element_type=F32)
            scores = scores * scale + bias_ref[:, :width]
            row_max = jnp.max(scores, axis=1, keepdims=True)
            weights = jnp.exp2(scores - row_max)
            total = jnp.sum(weights, axis=1, keepdims=True)
            summed = jnp.dot(weights.astype(BF), v_ref[:width, j * 128:(j + 1) * 128],
                             preferred_element_type=F32)
            out_ref[:, j * 128:(j + 1) * 128] = (summed / total).astype(BF)

    n = total_ref[0]
    next_ref[0] = n
    low = 0
    for width in VARIANTS:
        pl.when((n > low) & (n <= width))(functools.partial(variant, width))
        low = width


def attend(total, packed, keys, queries, q, upk, upv, scale, first, heads, after):
    pairs, start = heads // 2, first // 2
    return pl.pallas_call(
        functools.partial(attend_kernel, scale),
        grid=(pairs,),
        out_shape=(jax.ShapeDtypeStruct((CAP, pairs * 256), BF), jax.ShapeDtypeStruct((1,), jnp.int32)),
        in_specs=[
            pl.BlockSpec(memory_space=pltpu.SMEM),
            pl.BlockSpec(memory_space=pltpu.HBM),
            pl.BlockSpec(memory_space=pltpu.VMEM),
            pl.BlockSpec(memory_space=pltpu.VMEM),
            pl.BlockSpec((2, CAP, 256), lambda i: (start + i, 0, 0)),
            pl.BlockSpec((LAT, 256), lambda i: (0, start + i)),
            pl.BlockSpec((LAT, 256), lambda i: (0, start + i)),
        ] + [pl.BlockSpec(memory_space=pltpu.HBM)] * len(after),
        out_specs=(pl.BlockSpec((CAP, 256), lambda i: (0, i)), pl.BlockSpec(memory_space=pltpu.SMEM)),
        scratch_shapes=[pltpu.VMEM((TOT, 256), BF), pltpu.VMEM((TOT, 256), BF), pltpu.VMEM((TOT, WIDE), BF),
                        pltpu.VMEM((CAP, TOT), F32), pltpu.SemaphoreType.DMA],
        cost_estimate=pl.CostEstimate(flops=pairs * 10 ** 8, bytes_accessed=0, transcendentals=0),
        compiler_params=pltpu.CompilerParams(vmem_limit_bytes=50 * MIB),
        name="attend_heads",
    )(total, packed, keys, queries, q, upk, upv, *after)


def project_kernel(blocks, sel_ref, *refs):
    n = len(PARTS)
    rows, weights = refs[:2 * n], refs[2 * n:2 * n + 5]
    swapped = refs[2 * n + 5:2 * n + 10]
    outs = refs[-4 - 2 * blocks:-4]
    a_ref, w_ref, sem_a, sem_w = refs[-4:]
    core, slot = sel_ref[blocks], sel_ref[blocks + 1]
    waits = []
    for p in range(2):
        first = 0
        for i, width in enumerate(PARTS):
            copy = pltpu.make_async_copy(rows[n * p + i], a_ref.at[slot ^ p, :, pl.ds(first * 128, width * 128)],
                                         sem_a.at[n * p + i])
            copy.start()
            waits.append(copy)
            first += width
    for t in range(blocks):
        for k, pieces in enumerate((((0, 0),), ((1, 0),), ((2, 0), (3, 224)), ((4, 0),))):
            for cc in range(2):
                @pl.when((sel_ref[t] == k) & (core == cc))
                def _():
                    for j, source in enumerate((weights, swapped)):
                        for index, start in pieces:
                            src = source[index]
                            pltpu.make_async_copy(
                                src, w_ref.at[t, pl.ds((j ^ cc) * 448 + start, src.shape[0])], sem_w.at[t]).start()
    for copy in waits:
        copy.wait()
    for t in range(blocks):
        pltpu.make_async_copy(w_ref.at[t], w_ref.at[t], sem_w.at[t]).wait()
        whole = lax.dot_general(a_ref[...].reshape(2 * CAP, 2048), w_ref[t], (((1,), (1,)), ((), ())),
                                preferred_element_type=F32)
        for r in range(2):
            outs[2 * t + r][...] = whole[r * CAP:(r + 1) * CAP].astype(BF)


def project(sel, rows, weights, swapped, blocks, after):
    operands = (*rows, *weights, *swapped, *after)
    return pl.pallas_call(
        functools.partial(project_kernel, blocks),
        out_shape=(jax.ShapeDtypeStruct((CAP, 896), BF),) * (2 * blocks),
        in_specs=[pl.BlockSpec(memory_space=pltpu.SMEM)] + [pl.BlockSpec(memory_space=pltpu.HBM)] * len(operands),
        out_specs=(pl.BlockSpec(memory_space=pltpu.VMEM),) * (2 * blocks),
        scratch_shapes=[pltpu.VMEM((2, CAP, 2048), BF), pltpu.VMEM((blocks, 896, 2048), BF),
                        pltpu.SemaphoreType.DMA((len(rows),)), pltpu.SemaphoreType.DMA((2,))],
        cost_estimate=pl.CostEstimate(flops=10 ** 8, bytes_accessed=0, transcendentals=0),
        compiler_params=pltpu.CompilerParams(vmem_limit_bytes=58 * MIB),
        name="project_chunks",
    )(sel, *operands)


def behind(x, other, more):
    return pl.pallas_call(
        lambda *refs: None,
        out_shape=jax.ShapeDtypeStruct(x.shape, x.dtype),
        in_specs=[pl.BlockSpec(memory_space=pltpu.HBM), pl.BlockSpec(memory_space=pltpu.SMEM)]
        + [pl.BlockSpec(memory_space=pltpu.HBM)] * len(more),
        out_specs=pl.BlockSpec(memory_space=pltpu.HBM),
        input_output_aliases={0: 0},
        cost_estimate=pl.CostEstimate(flops=0, bytes_accessed=0, transcendentals=0),
        compiler_params=pltpu.CompilerParams(vmem_limit_bytes=MIB),
        name="behind",
    )(x, other, *more)


def forward_kernel(ahead_ref, behind_ref, after_ref, ahead_out, behind_out, first_ref, second_ref, sems):
    copies = [pltpu.make_async_copy(behind_ref.at[pl.ds(0, 224)], first_ref, sems.at[0]),
              pltpu.make_async_copy(ahead_ref.at[pl.ds(224, 224)], second_ref, sems.at[1])]
    for copy in copies:
        copy.start()
    for copy in copies:
        copy.wait()


def forward(ahead, back, after):
    return pl.pallas_call(
        forward_kernel,
        out_shape=(jax.ShapeDtypeStruct(ahead.shape, BF),) * 2 + (jax.ShapeDtypeStruct((224, 2048), BF),) * 2,
        in_specs=[pl.BlockSpec(memory_space=pltpu.HBM)] * 2 + [pl.BlockSpec(memory_space=pltpu.SMEM)],
        out_specs=(pl.BlockSpec(memory_space=pltpu.HBM),) * 4,
        input_output_aliases={0: 0, 1: 1},
        scratch_shapes=[pltpu.SemaphoreType.DMA((2,))],
        cost_estimate=pl.CostEstimate(flops=0, bytes_accessed=0, transcendentals=0),
        compiler_params=pltpu.CompilerParams(vmem_limit_bytes=MIB),
        name="forward_halves",
    )(ahead, back, after)


CORE = [(s, s ^ 1) for s in range(16)]
ALONG_Y = [(s, s ^ 8) for s in range(16)]


def along_z(k):
    return [(s, (s // 8) * 8 + ((s // 2 + k) % 4) * 2 + s % 2) for s in range(16)]


def along_x(k):
    return [(h, (h // 4) * 4 + (h + k) % 4) for h in range(8)]


def to_owner(r, dx):
    pairs = []
    for s in range(16):
        for h in range(8):
            y_lo, y_hi, x = s // 8, h // 4, h % 4
            pairs.append((s * 8 + h, ((y_hi ^ r) * 8 + s % 8) * 8 + y_lo * 4 + (x + dx) % 4))
    return pairs


def per_device(queries, latents, positions, up_keys, up_values, out_weight, residual, router_gate):
    heads, qk = queries.shape[1], queries.shape[2]
    s, h = lax.axis_index("seq"), lax.axis_index("head")
    y_lo, z, core = s // 8, (s // 2) % 4, s % 2
    y_hi, x = h // 4, h % 4
    own = payload(latents, positions)
    gathered = lax.all_gather(own, "seq", axis=0, tiled=True)
    weight = out_weight.T
    behind1 = lax.ppermute(weight, "seq", along_z(1))
    ahead1 = lax.ppermute(weight, "seq", along_z(3))
    core_own = lax.ppermute(weight, "seq", CORE)

    q = jnp.pad(jnp.transpose(queries, (1, 0, 2)), ((0, 0), (0, 0), (0, 256 - qk)))
    upk = up_keys.reshape(LAT, heads * 128)
    upv = up_values.reshape(LAT, heads * 128)

    packed, key_inv, query_inv, total = prep(gathered, own, (q, upk, upv))
    scale = (qk ** -0.5) * 1.4426950408889634
    ahead1, behind1, first_half, second_half = forward(ahead1, behind1, total)
    far0 = lax.ppermute(first_half, "seq", along_z(1))
    far1 = lax.ppermute(second_half, "seq", along_z(3))
    core_ahead1, core_behind1 = lax.ppermute(ahead1, "seq", CORE), lax.ppermute(behind1, "seq", CORE)
    mine, theirs, first, after = [], [], 0, (core_own,)
    for i, width in enumerate(PARTS):
        part, total = attend(total, packed, key_inv, query_inv, q, upk, upv, scale, first, width, after)
        first += width
        mine.append(part)
        theirs.append(lax.ppermute(part, "seq", ALONG_Y))
        after = (core_ahead1, core_behind1)
        if i == 1:
            far0, far1 = behind(far0, total, theirs[:1]), behind(far1, total, theirs[:1])
            core_far0, core_far1 = lax.ppermute(far0, "seq", CORE), lax.ppermute(far1, "seq", CORE)
            after = (theirs[0],)
    weights = (weight, ahead1, far0, far1, behind1)
    swapped = (core_own, core_ahead1, core_far0, core_far1, core_behind1)

    direct, crossing = [], []
    for pair in ((2, 1), (3,), (0,)):
        sel = jnp.stack([(x + dx - z) % 4 for dx in pair] + [core, y_hi ^ y_lo]).astype(jnp.int32)
        chunks = project(sel, mine + theirs, weights, swapped, len(pair), direct[:1] + crossing[:1] if pair == (0,) else [])
        for t, dx in enumerate(pair):
            direct.append(lax.ppermute(chunks[2 * t], ("seq", "head"), to_owner(0, dx)))
            crossing.append(lax.ppermute(chunks[2 * t + 1], "head", along_x(dx)) if dx else chunks[2 * t + 1])
    crossed = lax.ppermute(sum(c.astype(F32) for c in crossing).astype(BF), ("seq", "head"), to_owner(1, 0))
    projected = sum(r.astype(F32) for r in direct) + crossed.astype(F32)
    live_rows = (positions < SEQ_LEN).astype(F32)
    gated = (live_rows * router_gate)[:, None] * projected
    return (residual.astype(F32) + gated).astype(BF)


def solution(mesh):
    return jax.shard_map(
        per_device,
        mesh=mesh,
        in_specs=(
            P("seq", "head", None),
            P("seq", None),
            P("seq"),
            P(None, "head", None),
            P(None, "head", None),
            P("head", "seq"),
            P("seq", "head"),
            P("seq"),
        ),
        out_specs=P("seq", "head"),
        check_vma=False,
    )
```

```python
import functools
import jax
import jax.numpy as jnp
from jax import lax
from jax.experimental import pallas as pl
from jax.experimental.pallas import tpu as pltpu
from jax.sharding import PartitionSpec as P

SEQ_LEN = 131072
BF = jnp.bfloat16
F32 = jnp.float32
CAP = 192
SHARDS = 16
TOT = CAP * SHARDS
LAT = 512
WIDE = 640
MIB = 1024 * 1024
VARIANTS = (1024, 1280, 1536, TOT)
PARTS = (8, 6, 2)


def payload_kernel(lat_ref, pos_ref, out_ref):
    row = lax.broadcasted_iota(jnp.int32, (CAP, CAP), 0)
    col = lax.broadcasted_iota(jnp.int32, (CAP, CAP), 1)
    inv = jnp.sum(jnp.where(row == col, (SEQ_LEN - pos_ref[...]).astype(F32), 0.0), axis=1, keepdims=True)
    inv = inv.astype(jnp.int32)
    lane = lax.broadcasted_iota(jnp.int32, (CAP, 64), 1)
    digits = jnp.where(lane == 0, inv & 63, jnp.where(lane == 1, (inv >> 6) & 63, jnp.where(
        lane == 2, inv >> 12, jnp.where((lane == 3) & (inv > 0), 1, 0))))
    out_ref[...] = jnp.concatenate([lat_ref[...], digits.astype(F32).astype(BF)], axis=1)


def payload(latents, positions):
    return pl.pallas_call(
        payload_kernel,
        out_shape=jax.ShapeDtypeStruct((CAP, WIDE), BF),
        in_specs=[pl.BlockSpec(memory_space=pltpu.VMEM)] * 2,
        out_specs=pl.BlockSpec(memory_space=pltpu.VMEM),
        compiler_params=pltpu.CompilerParams(vmem_limit_bytes=4 * MIB),
        name="latents_and_positions",
    )(latents, positions.reshape(1, CAP))


def prep_kernel(all_ref, own_ref, *refs):
    out_ref, key_ref, query_ref, total_ref, packed_ref, sem = refs[-6:]
    packed_ref[...] = jnp.zeros_like(packed_ref)
    lane = lax.broadcasted_iota(jnp.int32, (CAP, 128), 1)
    counts = []
    for s in range(SHARDS):
        tail = all_ref[s * CAP:(s + 1) * CAP, LAT:WIDE].astype(F32)
        counts.append(jnp.sum(jnp.where(lane == 67, tail, 0.0)).astype(jnp.int32))
    diff = (lax.broadcasted_iota(jnp.int32, (CAP + 16, CAP), 0)
            - lax.broadcasted_iota(jnp.int32, (CAP + 16, CAP), 1))
    col = lax.broadcasted_iota(jnp.int32, (CAP + 16, CAP), 1)
    offset = jnp.int32(0)
    for s in range(SHARDS):
        first = pl.multiple_of((offset // 16) * 16, 16)
        shift = offset - first
        pick = jnp.where((diff == shift) & (col < counts[s]), 1.0, 0.0).astype(BF)
        moved = jnp.dot(pick, all_ref[s * CAP:(s + 1) * CAP, :],
                        preferred_element_type=F32).astype(BF)
        packed_ref[pl.ds(first, 16), :] = packed_ref[pl.ds(first, 16), :] + moved[:16]
        packed_ref[pl.ds(pl.multiple_of(first + 16, 16), CAP), :] = moved[16:]
        offset = offset + counts[s]
    total_ref[0] = offset
    lane8 = lax.broadcasted_iota(jnp.int32, (8, 128), 1)
    coef = jnp.where(lane8 == 64, 1.0, jnp.where(lane8 == 65, 64.0, jnp.where(lane8 == 66, 4096.0, 0.0)))
    key_ref[...] = lax.dot_general(coef.astype(BF), packed_ref[0:TOT, LAT:WIDE],
                                   (((1,), (1,)), ((), ())), preferred_element_type=F32)
    own = own_ref[:, LAT:WIDE].astype(F32)
    query_ref[...] = jnp.broadcast_to(jnp.sum(own * coef[0:1, :], axis=1, keepdims=True), query_ref.shape)
    low = 0
    for width in VARIANTS:
        @pl.when((offset > low) & (offset <= width))
        def _():
            copy = pltpu.make_async_copy(packed_ref.at[pl.ds(0, width)], out_ref.at[pl.ds(0, width)], sem)
            copy.start()
            copy.wait()
        low = width


def prep(gathered, own, after):
    return pl.pallas_call(
        prep_kernel,
        out_shape=(jax.ShapeDtypeStruct((TOT, WIDE), BF),
                   jax.ShapeDtypeStruct((8, TOT), F32),
                   jax.ShapeDtypeStruct((CAP, 128), F32),
                   jax.ShapeDtypeStruct((1,), jnp.int32)),
        in_specs=[pl.BlockSpec(memory_space=pltpu.VMEM)] * 2 + [pl.BlockSpec(memory_space=pltpu.HBM)] * len(after),
        out_specs=(pl.BlockSpec(memory_space=pltpu.HBM), pl.BlockSpec(memory_space=pltpu.VMEM),
                   pl.BlockSpec(memory_space=pltpu.VMEM), pl.BlockSpec(memory_space=pltpu.SMEM)),
        scratch_shapes=[pltpu.VMEM((TOT + 16, WIDE), BF), pltpu.SemaphoreType.DMA],
        compiler_params=pltpu.CompilerParams(vmem_limit_bytes=50 * MIB),
        name="pack_live_rows",
    )(gathered, own, *after)


def attend_kernel(scale, total_ref, source_ref, key_ref, query_ref, q_ref, upk_ref, upv_ref, *rest):
    out_ref, next_ref, k_ref, v_ref, packed_ref, bias_ref, sem = rest[-7:]

    def variant(width):
        @pl.when(pl.program_id(0) == 0)
        def _():
            copy = pltpu.make_async_copy(source_ref.at[pl.ds(0, width)], packed_ref.at[pl.ds(0, width)], sem)
            copy.start()
            bias_ref[:, :width] = jnp.where(key_ref[0:1, :width] >= query_ref[:, 0:1], 0.0, -1e30)
            copy.wait()

        for r in range(0, width, 256):
            x = packed_ref[r:r + 256, :LAT]
            k_ref[r:r + 256, :] = jnp.dot(x, upk_ref[...], preferred_element_type=F32).astype(BF)
            v_ref[r:r + 256, :] = jnp.dot(x, upv_ref[...], preferred_element_type=F32).astype(BF)
        for j in range(2):
            keys = jnp.concatenate(
                [k_ref[:width, j * 128:(j + 1) * 128], packed_ref[:width, LAT:WIDE]], axis=1)
            scores = lax.dot_general(q_ref[j], keys, (((1,), (1,)), ((), ())),
                                     preferred_element_type=F32)
            scores = scores * scale + bias_ref[:, :width]
            row_max = jnp.max(scores, axis=1, keepdims=True)
            weights = jnp.exp2(scores - row_max)
            total = jnp.sum(weights, axis=1, keepdims=True)
            summed = jnp.dot(weights.astype(BF), v_ref[:width, j * 128:(j + 1) * 128],
                             preferred_element_type=F32)
            out_ref[:, j * 128:(j + 1) * 128] = (summed / total).astype(BF)

    n = total_ref[0]
    next_ref[0] = n
    low = 0
    for width in VARIANTS:
        pl.when((n > low) & (n <= width))(functools.partial(variant, width))
        low = width


def attend(total, packed, keys, queries, q, upk, upv, scale, first, heads, after):
    pairs, start = heads // 2, first // 2
    return pl.pallas_call(
        functools.partial(attend_kernel, scale),
        grid=(pairs,),
        out_shape=(jax.ShapeDtypeStruct((CAP, pairs * 256), BF), jax.ShapeDtypeStruct((1,), jnp.int32)),
        in_specs=[
            pl.BlockSpec(memory_space=pltpu.SMEM),
            pl.BlockSpec(memory_space=pltpu.HBM),
            pl.BlockSpec(memory_space=pltpu.VMEM),
            pl.BlockSpec(memory_space=pltpu.VMEM),
            pl.BlockSpec((2, CAP, 256), lambda i: (start + i, 0, 0)),
            pl.BlockSpec((LAT, 256), lambda i: (0, start + i)),
            pl.BlockSpec((LAT, 256), lambda i: (0, start + i)),
        ] + [pl.BlockSpec(memory_space=pltpu.HBM)] * len(after),
        out_specs=(pl.BlockSpec((CAP, 256), lambda i: (0, i)), pl.BlockSpec(memory_space=pltpu.SMEM)),
        scratch_shapes=[pltpu.VMEM((TOT, 256), BF), pltpu.VMEM((TOT, 256), BF), pltpu.VMEM((TOT, WIDE), BF),
                        pltpu.VMEM((CAP, TOT), F32), pltpu.SemaphoreType.DMA],
        cost_estimate=pl.CostEstimate(flops=pairs * 10 ** 8, bytes_accessed=0, transcendentals=0),
        compiler_params=pltpu.CompilerParams(vmem_limit_bytes=50 * MIB),
        name="attend_heads",
    )(total, packed, keys, queries, q, upk, upv, *after)


def project_kernel(blocks, sel_ref, *refs):
    n = len(PARTS)
    rows, weights = refs[:2 * n], refs[2 * n:2 * n + 5]
    swapped = refs[2 * n + 5:2 * n + 10]
    outs = refs[-4 - 2 * blocks:-4]
    a_ref, w_ref, sem_a, sem_w = refs[-4:]
    core, slot = sel_ref[blocks], sel_ref[blocks + 1]
    waits = []
    for p in range(2):
        first = 0
        for i, width in enumerate(PARTS):
            copy = pltpu.make_async_copy(rows[n * p + i], a_ref.at[slot ^ p, :, pl.ds(first * 128, width * 128)],
                                         sem_a.at[n * p + i])
            copy.start()
            waits.append(copy)
            first += width
    for t in range(blocks):
        for k, pieces in enumerate((((0, 0),), ((1, 0),), ((2, 0), (3, 224)), ((4, 0),))):
            for cc in range(2):
                @pl.when((sel_ref[t] == k) & (core == cc))
                def _():
                    for j, source in enumerate((weights, swapped)):
                        for index, start in pieces:
                            src = source[index]
                            pltpu.make_async_copy(
                                src, w_ref.at[t, pl.ds((j ^ cc) * 448 + start, src.shape[0])], sem_w.at[t]).start()
    for copy in waits:
        copy.wait()
    for t in range(blocks):
        pltpu.make_async_copy(w_ref.at[t], w_ref.at[t], sem_w.at[t]).wait()
        whole = lax.dot_general(a_ref[...].reshape(2 * CAP, 2048), w_ref[t], (((1,), (1,)), ((), ())),
                                preferred_element_type=F32)
        for r in range(2):
            outs[2 * t + r][...] = whole[r * CAP:(r + 1) * CAP].astype(BF)


def project(sel, rows, weights, swapped, blocks, after):
    operands = (*rows, *weights, *swapped, *after)
    return pl.pallas_call(
        functools.partial(project_kernel, blocks),
        out_shape=(jax.ShapeDtypeStruct((CAP, 896), BF),) * (2 * blocks),
        in_specs=[pl.BlockSpec(memory_space=pltpu.SMEM)] + [pl.BlockSpec(memory_space=pltpu.HBM)] * len(operands),
        out_specs=(pl.BlockSpec(memory_space=pltpu.VMEM),) * (2 * blocks),
        scratch_shapes=[pltpu.VMEM((2, CAP, 2048), BF), pltpu.VMEM((blocks, 896, 2048), BF),
                        pltpu.SemaphoreType.DMA((len(rows),)), pltpu.SemaphoreType.DMA((2,))],
        cost_estimate=pl.CostEstimate(flops=10 ** 8, bytes_accessed=0, transcendentals=0),
        compiler_params=pltpu.CompilerParams(vmem_limit_bytes=58 * MIB),
        name="project_chunks",
    )(sel, *operands)


def behind(x, other, more):
    return pl.pallas_call(
        lambda *refs: None,
        out_shape=jax.ShapeDtypeStruct(x.shape, x.dtype),
        in_specs=[pl.BlockSpec(memory_space=pltpu.HBM), pl.BlockSpec(memory_space=pltpu.SMEM)]
        + [pl.BlockSpec(memory_space=pltpu.HBM)] * len(more),
        out_specs=pl.BlockSpec(memory_space=pltpu.HBM),
        input_output_aliases={0: 0},
        cost_estimate=pl.CostEstimate(flops=0, bytes_accessed=0, transcendentals=0),
        compiler_params=pltpu.CompilerParams(vmem_limit_bytes=MIB),
        name="behind",
    )(x, other, *more)


def forward_kernel(ahead_ref, behind_ref, after_ref, ahead_out, behind_out, first_ref, second_ref, sems):
    copies = [pltpu.make_async_copy(behind_ref.at[pl.ds(0, 224)], first_ref, sems.at[0]),
              pltpu.make_async_copy(ahead_ref.at[pl.ds(224, 224)], second_ref, sems.at[1])]
    for copy in copies:
        copy.start()
    for copy in copies:
        copy.wait()


def forward(ahead, back, after):
    return pl.pallas_call(
        forward_kernel,
        out_shape=(jax.ShapeDtypeStruct(ahead.shape, BF),) * 2 + (jax.ShapeDtypeStruct((224, 2048), BF),) * 2,
        in_specs=[pl.BlockSpec(memory_space=pltpu.HBM)] * 2 + [pl.BlockSpec(memory_space=pltpu.SMEM)],
        out_specs=(pl.BlockSpec(memory_space=pltpu.HBM),) * 4,
        input_output_aliases={0: 0, 1: 1},
        scratch_shapes=[pltpu.SemaphoreType.DMA((2,))],
        cost_estimate=pl.CostEstimate(flops=0, bytes_accessed=0, transcendentals=0),
        compiler_params=pltpu.CompilerParams(vmem_limit_bytes=MIB),
        name="forward_halves",
    )(ahead, back, after)


CORE = [(s, s ^ 1) for s in range(16)]
ALONG_Y = [(s, s ^ 8) for s in range(16)]


def along_z(k):
    return [(s, (s // 8) * 8 + ((s // 2 + k) % 4) * 2 + s % 2) for s in range(16)]


def along_x(k):
    return [(h, (h // 4) * 4 + (h + k) % 4) for h in range(8)]


def to_owner(r, dx):
    pairs = []
    for s in range(16):
        for h in range(8):
            y_lo, y_hi, x = s // 8, h // 4, h % 4
            pairs.append((s * 8 + h, ((y_hi ^ r) * 8 + s % 8) * 8 + y_lo * 4 + (x + dx) % 4))
    return pairs


def per_device(queries, latents, positions, up_keys, up_values, out_weight, residual, router_gate):
    heads, qk = queries.shape[1], queries.shape[2]
    s, h = lax.axis_index("seq"), lax.axis_index("head")
    y_lo, z, core = s // 8, (s // 2) % 4, s % 2
    y_hi, x = h // 4, h % 4
    own = payload(latents, positions)
    gathered = lax.all_gather(own, "seq", axis=0, tiled=True)
    weight = out_weight.T
    behind1 = lax.ppermute(weight, "seq", along_z(1))
    ahead1 = lax.ppermute(weight, "seq", along_z(3))
    core_own = lax.ppermute(weight, "seq", CORE)

    q = jnp.pad(jnp.transpose(queries, (1, 0, 2)), ((0, 0), (0, 0), (0, 256 - qk)))
    upk = up_keys.reshape(LAT, heads * 128)
    upv = up_values.reshape(LAT, heads * 128)

    packed, key_inv, query_inv, total = prep(gathered, own, (q, upk, upv))
    scale = (qk ** -0.5) * 1.4426950408889634
    ahead1, behind1, first_half, second_half = forward(ahead1, behind1, total)
    far0 = lax.ppermute(first_half, "seq", along_z(1))
    far1 = lax.ppermute(second_half, "seq", along_z(3))
    core_ahead1, core_behind1 = lax.ppermute(ahead1, "seq", CORE), lax.ppermute(behind1, "seq", CORE)
    mine, theirs, first, after = [], [], 0, (core_own,)
    for i, width in enumerate(PARTS):
        part, total = attend(total, packed, key_inv, query_inv, q, upk, upv, scale, first, width, after)
        first += width
        mine.append(part)
        theirs.append(lax.ppermute(part, "seq", ALONG_Y))
        after = (core_ahead1, core_behind1)
        if i == 1:
            far0, far1 = behind(far0, total, theirs[:1]), behind(far1, total, theirs[:1])
            core_far0, core_far1 = lax.ppermute(far0, "seq", CORE), lax.ppermute(far1, "seq", CORE)
            after = (theirs[0],)
    weights = (weight, ahead1, far0, far1, behind1)
    swapped = (core_own, core_ahead1, core_far0, core_far1, core_behind1)

    direct, crossing = [], []
    for pair in ((2, 1), (3,), (0,)):
        sel = jnp.stack([(x + dx - z) % 4 for dx in pair] + [core, y_hi ^ y_lo]).astype(jnp.int32)
        chunks = project(sel, mine + theirs, weights, swapped, len(pair), direct[:2] + crossing[:1] if pair == (0,) else [])
        for t, dx in enumerate(pair):
            direct.append(lax.ppermute(chunks[2 * t], ("seq", "head"), to_owner(0, dx)))
            crossing.append(lax.ppermute(chunks[2 * t + 1], "head", along_x(dx)) if dx else chunks[2 * t + 1])
    crossed = lax.ppermute(sum(c.astype(F32) for c in crossing).astype(BF), ("seq", "head"), to_owner(1, 0))
    projected = sum(r.astype(F32) for r in direct) + crossed.astype(F32)
    live_rows = (positions < SEQ_LEN).astype(F32)
    gated = (live_rows * router_gate)[:, None] * projected
    return (residual.astype(F32) + gated).astype(BF)


def solution(mesh):
    return jax.shard_map(
        per_device,
        mesh=mesh,
        in_specs=(
            P("seq", "head", None),
            P("seq", None),
            P("seq"),
            P(None, "head", None),
            P(None, "head", None),
            P("head", "seq"),
            P("seq", "head"),
            P("seq"),
        ),
        out_specs=P("seq", "head"),
        check_vma=False,
    )
```
